32 devices in a mesh: slab: 16 (over z, y, x), col: 2 (over core).
Axes of the slice: x: 2, y: 2, z: 4, core: 2. Of those that a mesh axis runs over, the one named last changes fastest.
Arguments:
- coupling: float32 [16, 512, 512], P('slab', None, 'col'), as said below
- tile_pattern: int32 [16, 4, 4], P('slab', None, 'col'), may hold values from 0 to 1, as said below
- orbital_mass: float32 [16, 512], P('slab', 'col'), may hold values from 0.0001 to 0.05
- sources: float32 [16, 512, 256], P('slab', None, 'col'), may hold values from -0.3 to 0.3
Outputs:
- solution: float32 [16, 512, 256], P('slab', None, 'col')
The draws below stay inside these ranges and needn't reach their ends.
Inputs may be any that keep to these rules, and one draw needn't show every extreme that they name: Each coupling block is symmetric and positive semidefinite. `tile_pattern`: in each slab every tile belongs to one group, and two tiles are linked exactly when they share a group, so each pattern is symmetric with ones on its diagonal.
All inputs are finite; a program needn't handle non-finite values.
Results may differ from the reference program's by a relative error of at most 0.0003.
Values sent between devices are 32-bit elements; how exact they have to be, the bound alone decides.
No kernel may reach another device: no remote copies, remote signals or barrier semaphores. Data moves between devices by JAX's collectives and lax.ppermute only.
A program may use at most 128 MiB of HBM per device.

```python
import math
import jax
import jax.numpy as jnp
from jax import lax

ORBITALS = 512
TILE = 128
TILES = 4
MODES = 256
LEVELS = 6
SLABS = 16


def draw_coupling(key, part):
    raw = jnp.clip(jax.random.normal(key, (SLABS, ORBITALS, ORBITALS), jnp.float32), -3.0, 3.0)
    product = jnp.matmul(raw, jnp.swapaxes(raw, 1, 2), precision=lax.Precision.HIGHEST)
    return (product + jnp.swapaxes(product, 1, 2)) * (1.5 / ORBITALS)


def draw_tile_pattern(key, part):
    groups = jax.random.randint(key, (SLABS, TILES), 0, TILES).astype(jnp.int32)
    return (groups[:, :, None] == groups[:, None, :]).astype(jnp.int32)


def shard_levels(key, shape, shards, least, largest):
    level = 1.0
    for dim, blocks in shards:
        draws = jax.random.uniform(jax.random.fold_in(jax.random.fold_in(key, 6), dim), (blocks,), jnp.float32, least / len(shards), largest / len(shards))
        level = level * jnp.repeat(jnp.exp(draws), shape[dim] // blocks).reshape((-1,) + (1,) * (len(shape) - 1 - dim))
    return level


def normal_values(own_key, dims, spread, reach, pieces=(), kind=jnp.bfloat16):
    drawn = spread * jax.random.normal(own_key, dims, jnp.float32)
    if pieces:
        drawn = drawn * shard_levels(own_key, dims, pieces, -0.22, 0.18)
    return jnp.clip(drawn, -reach, reach).astype(kind)


def setup_inputs(seed: int = 0) -> dict:
    key_of = jax.random.split(jax.random.key(seed), 5)
    return {
        "coupling": draw_coupling(jax.random.fold_in(key_of[4], 71), 0),
        "tile_pattern": draw_tile_pattern(jax.random.fold_in(key_of[4], 71), 0),
        "orbital_mass": jnp.clip(jnp.exp(math.log(0.05) - 6.214608 * jax.random.uniform(key_of[2], (SLABS, ORBITALS), jnp.float32) ** shard_levels(key_of[2], (SLABS, ORBITALS), ((0, 16), (1, 2)), -0.2, 0.2)), 0.0001, 0.05),
        "sources": normal_values(key_of[3], (SLABS, ORBITALS, MODES), 0.05, 0.3, ((0, 16), (2, 2)), jnp.float32),
    }


leaf_limit = 128

def factor_inverse(matrix):
    width = matrix.shape[-1]
    if width <= leaf_limit:
        factor = jnp.linalg.cholesky(matrix)
        unit = jnp.broadcast_to(jnp.eye(width, dtype=matrix.dtype), matrix.shape)
        return lax.linalg.triangular_solve(factor, unit, left_side=True, lower=True)
    half_w = width // 2
    top_left = matrix[..., :half_w, :half_w]
    bottom_left = matrix[..., half_w:, :half_w]
    bottom_right = matrix[..., half_w:, half_w:]
    first_inv = factor_inverse(top_left)
    lower_part = jnp.matmul(bottom_left, jnp.swapaxes(first_inv, -1, -2), precision=lax.Precision.HIGHEST)
    schur_part = bottom_right - jnp.matmul(lower_part, jnp.swapaxes(lower_part, -1, -2), precision=lax.Precision.HIGHEST)
    second_inv = factor_inverse(schur_part)
    cross = -jnp.matmul(second_inv, jnp.matmul(lower_part, first_inv, precision=lax.Precision.HIGHEST), precision=lax.Precision.HIGHEST)
    upper_row = jnp.concatenate([first_inv, jnp.zeros_like(lower_part.swapaxes(-1, -2))], axis=-1)
    lower_row = jnp.concatenate([cross, second_inv], axis=-1)
    return jnp.concatenate([upper_row, lower_row], axis=-2)

def solve_spd(matrix, rhs):
    inverse = factor_inverse(matrix)
    inner = jnp.matmul(inverse, rhs, precision=lax.Precision.HIGHEST)
    return jnp.matmul(jnp.swapaxes(inverse, -1, -2), inner, precision=lax.Precision.HIGHEST)

def reference(coupling, tile_pattern, orbital_mass, sources):
    count = coupling.shape[0]
    width = coupling.shape[1]
    tile_mask = jnp.repeat(jnp.repeat(tile_pattern, TILE, axis=1), TILE, axis=2).astype(jnp.float32)
    unit = jnp.eye(width, dtype=jnp.float32)
    bond = unit[None] + tile_mask * coupling
    prior = jnp.concatenate([jnp.zeros_like(bond[:1]), bond[:-1]], axis=0)
    keep_upper = (jnp.arange(count) < count - 1).astype(jnp.float32)[:, None, None]
    lower_blk = -prior
    upper_blk = -bond * keep_upper
    diag_blk = bond + prior + unit[None] * orbital_mass[:, None, :]
    source = sources
    for level_num in range(LEVELS):
        stride = 2 ** level_num
        if stride >= count:
            break
        solved = solve_spd(diag_blk, jnp.concatenate([upper_blk, lower_blk, source], axis=2))
        padding = jnp.zeros_like(solved[:stride])
        from_below = jnp.concatenate([padding, solved[:count - stride]], axis=0)
        from_above = jnp.concatenate([solved[stride:], padding], axis=0)
        below_prod = jnp.einsum('nij,njk->nik', lower_blk, from_below, precision=lax.Precision.HIGHEST)
        above_prod = jnp.einsum('nij,njk->nik', upper_blk, from_above, precision=lax.Precision.HIGHEST)
        diag_blk = diag_blk - below_prod[:, :, :width] - above_prod[:, :, width:2 * width]
        new_lower = -below_prod[:, :, width:2 * width]
        new_upper = -above_prod[:, :, :width]
        source = source - below_prod[:, :, 2 * width:] - above_prod[:, :, 2 * width:]
        lower_blk = new_lower
        upper_blk = new_upper
    return solve_spd(diag_blk, source)
```

```python
import functools

import jax
import jax.numpy as jnp
from jax import lax
from jax.experimental import pallas as pl
from jax.experimental.pallas import tpu as pltpu
from jax.sharding import PartitionSpec as P

LEVELS = 6


LEAF = 128
GROUP = 8


def split(x):
    high = x.astype(jnp.bfloat16)
    low = (x - high.astype(jnp.float32)).astype(jnp.bfloat16)
    return high, low


def dot_split(a, b):
    (ah, al), (bh, bl) = a, b
    mul = functools.partial(jnp.dot, preferred_element_type=jnp.float32)
    return mul(ah, bh) + (mul(ah, bl) + mul(al, bh))


def dot3(a, b):
    return dot_split(split(a), split(b))


def leaf_inverse(blocks):
    shape = (GROUP, LEAF)
    lane = lax.broadcasted_iota(jnp.int32, shape, 1)
    sub = lax.broadcasted_iota(jnp.int32, shape, 0)
    count = LEAF // GROUP
    sets = [[b[GROUP * i : GROUP * (i + 1), :] for i in range(count)] for b in blocks]

    def row_of(v, p):
        return jnp.broadcast_to(v[p : p + 1, :], shape)

    def col_of(v, c):
        return jnp.broadcast_to(v[:, c : c + 1], shape)

    for k in range(count):
        base = GROUP * k
        for rows in sets:
            v = rows[k]
            cols = [col_of(v, base + p) for p in range(GROUP)]
            for p in range(GROUP):
                inv = 1.0 / row_of(cols[p], p)
                here = sub == p
                unit = jnp.where(here, 1.0, 0.0)
                v = jnp.where(lane == base + p, unit, v)
                scaled = row_of(v, p) * inv
                v = jnp.where(here, scaled, v - cols[p] * scaled)
                for q in range(p + 1, GROUP):
                    entry = row_of(cols[q], p) * inv
                    cols[q] = jnp.where(here, entry, cols[q] - cols[p] * entry)
            rows[k] = v
            pivots = [row_of(v, p) for p in range(GROUP)]
            inside = (lane >= base) & (lane < base + GROUP)
            order = list(range(k + 1, count)) + list(range(k))
            for i in order:
                w = rows[i]
                acc = jnp.where(inside, 0.0, w)
                for p in range(GROUP):
                    acc = acc - col_of(w, base + p) * pivots[p]
                rows[i] = acc
    return [jnp.concatenate(rows, axis=0) for rows in sets]


def inverse_in(work_refs):
    n = work_refs[0].shape[-1]
    steps = n // LEAF

    def shifted_update(ref, src, dst, leaf):
        row = ref[src, :LEAF, LEAF:]
        col = ref[src, LEAF:, :LEAF]
        ls = split(leaf)
        cs = split(col)
        q = dot_split(ls, split(row))
        qs = split(q)
        ref[dst, : n - LEAF, : n - LEAF] = ref[src, LEAF:, LEAF:] - dot_split(cs, qs)
        ref[dst, n - LEAF :, : n - LEAF] = q
        ref[dst, : n - LEAF, n - LEAF :] = -dot_split(cs, ls)
        ref[dst, n - LEAF :, n - LEAF :] = leaf

    def body(step, leaves):
        src = lax.rem(step, 2)
        dst = 1 - src
        for ref, leaf in zip(work_refs, leaves):
            shifted_update(ref, src, dst, leaf)
        return tuple(leaf_inverse([ref[dst, :LEAF, :LEAF] for ref in work_refs]))

    leaves = tuple(leaf_inverse([ref[0, :LEAF, :LEAF] for ref in work_refs]))
    leaves = lax.fori_loop(0, steps - 1, body, leaves)
    for ref, leaf in zip(work_refs, leaves):
        shifted_update(ref, (steps - 1) % 2, steps % 2, leaf)


def inverse_kernel(a_ref, o_ref, work):
    work[0] = a_ref[...]
    inverse_in([work])
    o_ref[...] = work[0]


def inverse(a):
    n = a.shape[0]
    return pl.pallas_call(
        inverse_kernel,
        out_shape=jax.ShapeDtypeStruct((n, n), jnp.float32),
        scratch_shapes=[pltpu.VMEM((2, n, n), jnp.float32)],
        compiler_params=pltpu.CompilerParams(vmem_limit_bytes=48 * 1024 * 1024),
    )(a)


def from_behind(shard, axis, by):
    size = lax.axis_size(axis)
    pairs = [(i, i + by) for i in range(size) if 0 <= i + by < size]
    return lax.ppermute(shard, axis, pairs)


def solve_spd(matrix, rhs):
    return jnp.dot(
        inverse(matrix), rhs, precision=lax.Precision.HIGHEST, preferred_element_type=jnp.float32
    )


def on_device(coupling, tile_pattern, orbital_mass, sources):
    width = coupling.shape[1]
    half = coupling.shape[2]
    tiles_row = tile_pattern.shape[1]
    tiles_col = tile_pattern.shape[2]
    tile_width = width // tiles_row
    column = lax.axis_index("col")
    slab_index = lax.axis_index("slab")
    slab_count = lax.axis_size("slab")
    tile_mask = jnp.broadcast_to(
        tile_pattern[0][:, None, :, None].astype(jnp.float32),
        (tiles_row, tile_width, tiles_col, tile_width),
    ).reshape(width, half)
    row_ids = lax.broadcasted_iota(jnp.int32, (width, half), 0)
    col_ids = lax.broadcasted_iota(jnp.int32, (width, half), 1) + column * half
    unit_panel = (row_ids == col_ids).astype(jnp.float32)
    bond_panel = unit_panel + tile_mask * coupling[0]
    prior_panel = from_behind(bond_panel, "slab", 1)
    keep_upper = (slab_index < slab_count - 1).astype(jnp.float32)
    lower_panel = -prior_panel
    upper_panel = -bond_panel * keep_upper
    diag_panel = bond_panel + prior_panel + unit_panel * orbital_mass[0][None, :]
    source_panel = sources[0]
    for level_num in range(LEVELS):
        stride = 2**level_num
        if stride >= slab_count:
            break
        full_diag, full_lower, full_upper = (
            lax.all_gather(diag_panel, "col", axis=1, tiled=True),
            lax.all_gather(lower_panel, "col", axis=1, tiled=True),
            lax.all_gather(upper_panel, "col", axis=1, tiled=True),
        )
        solved = solve_spd(
            full_diag, jnp.concatenate([upper_panel, lower_panel, source_panel], axis=1)
        )
        from_below = from_behind(solved, "slab", stride)
        from_above = from_behind(solved, "slab", -stride)
        below_prod = jnp.dot(
            full_lower,
            from_below,
            precision=lax.Precision.HIGHEST,
            preferred_element_type=jnp.float32,
        )
        above_prod = jnp.dot(
            full_upper,
            from_above,
            precision=lax.Precision.HIGHEST,
            preferred_element_type=jnp.float32,
        )
        diag_panel = diag_panel - below_prod[:, :half] - above_prod[:, half : 2 * half]
        lower_panel = -below_prod[:, half : 2 * half]
        upper_panel = -above_prod[:, :half]
        source_panel = source_panel - below_prod[:, 2 * half :] - above_prod[:, 2 * half :]
    final_diag = lax.all_gather(diag_panel, "col", axis=1, tiled=True)
    solution = solve_spd(final_diag, source_panel)
    return solution[None]


def solution(mesh):
    placed = (
        P("slab", None, "col"),
        P("slab", None, "col"),
        P("slab", "col"),
        P("slab", None, "col"),
    )
    return jax.shard_map(
        on_device, mesh=mesh, in_specs=placed, out_specs=P("slab", None, "col"), check_vma=False
    )
```

```python
import functools
import math

import jax
import jax.numpy as jnp
from jax import lax
from jax.experimental import pallas as pl
from jax.experimental.pallas import tpu as pltpu
from jax.sharding import Mesh
from jax.sharding import PartitionSpec as P

MEMBERS = 4
VMEM_BYTES = 56 * 1024 * 1024
LEAF = 128
GROUP = 8


def split(x):
    high = x.astype(jnp.bfloat16)
    low = (x - high.astype(jnp.float32)).astype(jnp.bfloat16)
    return high, low


def dot_split(a, b):
    (ah, al), (bh, bl) = a, b
    mul = functools.partial(jnp.dot, preferred_element_type=jnp.float32)
    return mul(ah, bh) + (mul(ah, bl) + mul(al, bh))


def dot3(a, b):
    return dot_split(split(a), split(b))


def leaf_inverse(blocks):
    shape = (GROUP, LEAF)
    lane = lax.broadcasted_iota(jnp.int32, shape, 1)
    sub = lax.broadcasted_iota(jnp.int32, shape, 0)
    count = LEAF // GROUP
    sets = [[b[GROUP * i : GROUP * (i + 1), :] for i in range(count)] for b in blocks]

    def row_of(v, p):
        return jnp.broadcast_to(v[p : p + 1, :], shape)

    def col_of(v, c):
        return jnp.broadcast_to(v[:, c : c + 1], shape)

    for k in range(count):
        base = GROUP * k
        for rows in sets:
            v = rows[k]
            cols = [col_of(v, base + p) for p in range(GROUP)]
            for p in range(GROUP):
                inv = 1.0 / row_of(cols[p], p)
                here = sub == p
                unit = jnp.where(here, 1.0, 0.0)
                v = jnp.where(lane == base + p, unit, v)
                scaled = row_of(v, p) * inv
                v = jnp.where(here, scaled, v - cols[p] * scaled)
                for q in range(p + 1, GROUP):
                    entry = row_of(cols[q], p) * inv
                    cols[q] = jnp.where(here, entry, cols[q] - cols[p] * entry)
            rows[k] = v
            pivots = [row_of(v, p) for p in range(GROUP)]
            inside = (lane >= base) & (lane < base + GROUP)
            order = list(range(k + 1, count)) + list(range(k))
            for i in order:
                w = rows[i]
                acc = jnp.where(inside, 0.0, w)
                for p in range(GROUP):
                    acc = acc - col_of(w, base + p) * pivots[p]
                rows[i] = acc
    return [jnp.concatenate(rows, axis=0) for rows in sets]


def inverse_in(work_refs):
    n = work_refs[0].shape[-1]
    steps = n // LEAF

    def shifted_update(ref, src, dst, leaf):
        row = ref[src, :LEAF, LEAF:]
        col = ref[src, LEAF:, :LEAF]
        ls = split(leaf)
        cs = split(col)
        q = dot_split(ls, split(row))
        qs = split(q)
        ref[dst, : n - LEAF, : n - LEAF] = ref[src, LEAF:, LEAF:] - dot_split(cs, qs)
        ref[dst, n - LEAF :, : n - LEAF] = q
        ref[dst, : n - LEAF, n - LEAF :] = -dot_split(cs, ls)
        ref[dst, n - LEAF :, n - LEAF :] = leaf

    def body(step, leaves):
        src = lax.rem(step, 2)
        dst = 1 - src
        for ref, leaf in zip(work_refs, leaves):
            shifted_update(ref, src, dst, leaf)
        return tuple(leaf_inverse([ref[dst, :LEAF, :LEAF] for ref in work_refs]))

    leaves = tuple(leaf_inverse([ref[0, :LEAF, :LEAF] for ref in work_refs]))
    leaves = lax.fori_loop(0, steps - 1, body, leaves)
    for ref, leaf in zip(work_refs, leaves):
        shifted_update(ref, (steps - 1) % 2, steps % 2, leaf)


def plus_diagonal(matrix, row):
    shape = matrix.shape
    here = lax.broadcasted_iota(jnp.int32, shape, 0) == lax.broadcasted_iota(jnp.int32, shape, 1)
    return matrix + jnp.where(here, jnp.broadcast_to(row, shape), 0.0)


def dot_down(a, b):
    (ah, al), (bh, bl) = split(a), split(b)
    mul = functools.partial(
        lax.dot_general,
        dimension_numbers=(((0,), (0,)), ((), ())),
        preferred_element_type=jnp.float32,
    )
    return mul(ah, bh) + (mul(ah, bl) + mul(al, bh))


def reduce_kernel(
    flags, gathered, p1, p3, i2, y10, y12, y32, y3i, yo, yi, goi, gio, mo, mi, work_a, work_b
):
    width = p1.shape[0]
    right = flags[0]
    last = flags[1]

    def bond(k):
        member = jnp.where(right == 1, MEMBERS - 1 - k, k)
        return jnp.concatenate(
            [gathered[2 * member, :width, :], gathered[2 * member + 1, :width, :]], axis=1
        )

    def mass(k):
        member = jnp.where((right == 1) & (k > 0), MEMBERS - k, k)
        return jnp.concatenate(
            [
                gathered[2 * member, width : width + 1, :],
                gathered[2 * member + 1, width : width + 1, :],
            ],
            axis=1,
        )

    m1, m2, m3 = mass(1), mass(2), mass(3)
    work_a[0] = plus_diagonal(bond(0) + bond(1), m1)
    work_b[0] = plus_diagonal(bond(2) + bond(3), m3)
    inverse_in([work_a, work_b])
    p1[...] = work_a[0]
    p3[...] = work_b[0]
    c0, c1, c2, c3 = (split(bond(k)) for k in range(MEMBERS))
    q1 = split(p1[...])
    y10[...] = dot_split(c0, q1)
    y12[...] = dot_split(c1, q1)
    q3 = split(p3[...])
    y32[...] = dot_split(c2, q3)
    y3i[...] = dot_split(c3, q3)
    to_o = dot_split(split(y12[...]), c0)
    to_i = dot_split(split(y32[...]), c3)
    from_o = dot_split(split(y10[...]), c1)
    from_i = dot_split(split(y3i[...]), c2)
    mass2 = plus_diagonal(y12[...] * m1 + y32[...] * m3, m2)
    work_a[0] = to_o + to_i + mass2
    inverse_in([work_a])
    i2[...] = work_a[0]
    q2 = split(i2[...])
    yo[...] = dot_split(split(from_o), q2)
    yi[...] = dot_split(split(from_i), q2)
    so, si = split(yo[...]), split(yi[...])
    goi[...] = dot_split(so, split(to_i))
    back = dot_split(si, split(to_o))
    gio[...] = back
    sm = split(mass2)
    m0 = mass(0)
    left_on = jnp.where(right == 1, 0.0, 1.0)
    mo[...] = plus_diagonal(y10[...] * m1 + dot_split(so, sm), m0 * left_on)
    mi[...] = plus_diagonal(
        y3i[...] * m3 + dot_split(si, sm) + back * jnp.where(last == 1, 1.0, 0.0),
        m0 * (1.0 - left_on),
    )


def whole(flags, mine, other):
    first = flags[2] == 0
    a, b = mine[...], other[...]
    return jnp.concatenate([jnp.where(first, a, b), jnp.where(first, b, a)], axis=1)


def chain_kernel(flags, goi, gio, mo, mi, mine, other, new_mi, si, y, work):
    mass_o = mo[...] + whole(flags, mine, other)
    work[0] = goi[...] + mass_o
    inverse_in([work])
    si[...] = work[0]
    y[...] = dot3(gio[...], si[...])
    new_mi[...] = mi[...] + dot3(y[...], mass_o)


def root_kernel(flags, goi, gio, mo, mi, o_mine, o_other, i_mine, i_other, inv_i, y, inv_o, work):
    mass_i = mi[...] + whole(flags, i_mine, i_other)
    work[0] = gio[...] + mass_i
    inverse_in([work])
    inv_i[...] = work[0]
    y[...] = dot3(goi[...], inv_i[...])
    mass_o = mo[...] + whole(flags, o_mine, o_other)
    work[0] = mass_o + dot3(y[...], mass_i)
    inverse_in([work])
    inv_o[...] = work[0]


def columns_kernel(flags, rhs, p1, p3, i2, y10, y12, y32, y3i, yo, yi, v1, v2, v3, ro, ri):
    right = flags[0]
    r0 = rhs[0]
    r2 = rhs[2]
    r1 = rhs[jnp.where(right == 1, 3, 1)]
    r3 = rhs[jnp.where(right == 1, 1, 3)]
    s1, s3 = split(r1), split(r3)
    v1[...] = dot_split(split(p1[...]), s1)
    v3[...] = dot_split(split(p3[...]), s3)
    r2 = r2 + dot_split(split(y12[...]), s1) + dot_split(split(y32[...]), s3)
    s2 = split(r2)
    v2[...] = dot_split(split(i2[...]), s2)
    left_on = jnp.where(right == 1, 0.0, 1.0)
    ro[...] = r0 * left_on + dot_split(split(y10[...]), s1) + dot_split(split(yo[...]), s2)
    ri[...] = r0 * (1.0 - left_on) + dot_split(split(y3i[...]), s3) + dot_split(split(yi[...]), s2)


def chain_columns_kernel(y, si, ro, ri, new_ri, vo):
    s = split(ro[...])
    new_ri[...] = ri[...] + dot_split(split(y[...]), s)
    vo[...] = dot_split(split(si[...]), s)


def root_columns_kernel(inv_i, y, inv_o, ro, ri, xo, xi):
    s = split(ri[...])
    xo[...] = dot3(inv_o[...], ro[...] + dot_split(split(y[...]), s))
    xi[...] = dot_split(split(inv_i[...]), s) + dot_down(y[...], xo[...])


def chain_back_kernel(vo, y, xi, xo):
    xo[...] = vo[...] + dot_down(y[...], xi[...])


def back_kernel(flags, y10, y12, y32, y3i, yo, yi, v1, v2, v3, xo, xi, out):
    right = flags[0]
    member = flags[3]
    so, si = xo[...], xi[...]
    x2 = v2[...] + dot_down(yo[...], so) + dot_down(yi[...], si)
    x1 = v1[...] + dot_down(y10[...], so) + dot_down(y12[...], x2)
    x3 = v3[...] + dot_down(y32[...], x2) + dot_down(y3i[...], si)
    is_right = right == 1
    end = jnp.where(is_right, si, so)
    low = jnp.where(is_right, x3, x1)
    high = jnp.where(is_right, x1, x3)
    out[...] = jnp.where(
        member == 0, end, jnp.where(member == 1, low, jnp.where(member == 2, x2, high))
    )


def call(kernel, args, outs, scratch=(), flops=0):
    def spec(a):
        space = pltpu.SMEM if a.dtype == jnp.int32 else pltpu.VMEM
        return pl.BlockSpec(memory_space=space)

    moved = sum(a.size * 4 for a in args) + sum(4 * math.prod(s) for s in outs)
    return pl.pallas_call(
        kernel,
        out_shape=[jax.ShapeDtypeStruct(s, jnp.float32) for s in outs],
        in_specs=[spec(a) for a in args],
        out_specs=[pl.BlockSpec(memory_space=pltpu.VMEM) for _ in outs],
        scratch_shapes=[pltpu.VMEM(s, jnp.float32) for s in scratch],
        cost_estimate=pl.CostEstimate(flops=flops, bytes_accessed=moved, transcendentals=0),
        compiler_params=pltpu.CompilerParams(vmem_limit_bytes=VMEM_BYTES),
    )(*args)


def on_device(coupling, tile_pattern, orbital_mass, sources):
    width = coupling.shape[1]
    half = coupling.shape[2]
    modes = sources.shape[2]
    tiles_row = tile_pattern.shape[1]
    tiles_col = tile_pattern.shape[2]
    tile_width = width // tiles_row
    column = lax.axis_index("col")
    member = lax.axis_index("member")
    group = lax.axis_index("group")
    groups = lax.axis_size("group")
    middle = groups // 2
    tile_mask = jnp.broadcast_to(
        tile_pattern[0][:, None, :, None].astype(jnp.float32),
        (tiles_row, tile_width, tiles_col, tile_width),
    ).reshape(width, half)
    row_ids = lax.broadcasted_iota(jnp.int32, (width, half), 0)
    col_ids = lax.broadcasted_iota(jnp.int32, (width, half), 1) + column * half
    unit_panel = (row_ids == col_ids).astype(jnp.float32)
    bond_panel = unit_panel + tile_mask * coupling[0]
    panel = jnp.concatenate(
        [bond_panel, jnp.broadcast_to(orbital_mass, (GROUP, half))], axis=0
    )
    gathered = lax.all_gather(panel, ("member", "col"), axis=0, tiled=False)
    rhs = lax.all_gather(sources[0], "member", axis=0, tiled=False)
    flags = jnp.stack(
        [
            (group >= middle).astype(jnp.int32),
            (group == groups - 1).astype(jnp.int32),
            column.astype(jnp.int32),
            member.astype(jnp.int32),
        ]
    )
    square = (width, width)
    block = (width, modes)
    room = (2, width, width)
    unit_flops = 6 * width**3
    p1, p3, i2, y10, y12, y32, y3i, yo, yi, goi, gio, mo, mi = call(
        reduce_kernel, [flags, gathered], [square] * 13, [room, room], 40 * unit_flops
    )
    v1, v2, v3, ro, ri = call(
        columns_kernel,
        [flags, rhs, p1, p3, i2, y10, y12, y32, y3i, yo, yi],
        [block] * 5,
        flops=3 * unit_flops,
    )

    def send(x, pairs):
        return lax.ppermute(x, "group", pairs)

    def my_half(x):
        return lax.dynamic_slice_in_dim(x, column * half, half, axis=1)

    def other_half(x):
        return lax.ppermute(x, "col", [(0, 1), (1, 0)])

    first = [(groups - 1, groups - 2)]
    into_o = send(my_half(mi), first)
    ro = ro + send(ri, first)
    into_i = jnp.zeros_like(into_o)
    steps = []
    for t in range(middle - 1):
        new_mi, si, y = call(
            chain_kernel,
            [flags, goi, gio, mo, mi, into_o, other_half(into_o)],
            [square] * 3,
            [room],
            20 * unit_flops,
        )
        new_ri, vo = call(
            chain_columns_kernel, [y, si, ro, ri], [block] * 2, flops=unit_flops
        )
        steps.append((y, vo))
        upward = [(t, t + 1)]
        downward = [(groups - 2 - t, groups - 3 - t)]
        part = my_half(new_mi)
        from_left, from_right = send(part, upward), send(part, downward)
        rhs_left, rhs_right = send(new_ri, upward), send(new_ri, downward)
        into_o = into_o + from_left
        ro = ro + rhs_left
        if groups - 3 - t >= middle:
            into_o = into_o + from_right
            ro = ro + rhs_right
        else:
            into_i = into_i + from_right
            ri = ri + rhs_right
    inv_i, y, inv_o = call(
        root_kernel,
        [flags, goi, gio, mo, mi, into_o, other_half(into_o), into_i, other_half(into_i)],
        [square] * 3,
        [room],
        40 * unit_flops,
    )
    xo, xi = call(
        root_columns_kernel, [inv_i, y, inv_o, ro, ri], [block] * 2, flops=unit_flops
    )
    for t in reversed(range(middle - 1)):
        y, vo = steps[t]
        from_right = send(xo, [(t + 1, t)])
        from_left = send(jnp.where(group == middle - 1, xi, xo), [(groups - 3 - t, groups - 2 - t)])
        on_left = group == t
        on_right = group == groups - 2 - t
        xi = jnp.where(on_left, from_right, jnp.where(on_right, from_left, xi))
        (outer,) = call(chain_back_kernel, [vo, y, xi], [block], flops=unit_flops)
        xo = jnp.where(on_left | on_right, outer, xo)
    from_left = send(xo, [(groups - 2, groups - 1)])
    ground = group == groups - 1
    xi = jnp.where(ground, from_left, xi)
    xo = jnp.where(ground, 0.0, xo)
    (out,) = call(
        back_kernel,
        [flags, y10, y12, y32, y3i, yo, yi, v1, v2, v3, xo, xi],
        [block],
        flops=unit_flops,
    )
    return out[None]


def solution(mesh):
    groups = mesh.shape["slab"] // MEMBERS
    fine = Mesh(
        mesh.devices.reshape(groups, MEMBERS, mesh.shape["col"]), ("group", "member", "col")
    )
    slab = ("group", "member")
    placed = (
        P(slab, None, "col"),
        P(slab, None, "col"),
        P(slab, "col"),
        P(slab, None, "col"),
    )
    return jax.shard_map(
        on_device, mesh=fine, in_specs=placed, out_specs=P(slab, None, "col"), check_vma=False
    )
```

```python
import functools
import math

import jax
import jax.numpy as jnp
from jax import lax
from jax.experimental import pallas as pl
from jax.experimental.pallas import tpu as pltpu
from jax.sharding import Mesh
from jax.sharding import PartitionSpec as P

MEMBERS = 4
SPARE_BYTES = 16 * 1024 * 1024
LEAF_TILE = 128
LEAF = 128
PANEL = 32
GROUP = 8


def split(x):
    high = x.astype(jnp.bfloat16)
    low = (x - high.astype(jnp.float32)).astype(jnp.bfloat16)
    return high, low


def dot_split(a, b):
    (ah, al), (bh, bl) = a, b
    mul = functools.partial(jnp.dot, preferred_element_type=jnp.float32)
    return mul(ah, bh) + (mul(ah, bl) + mul(al, bh))


def dot3(a, b):
    return dot_split(split(a), split(b))


def reciprocal(x):
    guess = pl.reciprocal(x, approx=True)
    return guess * (2.0 - x * guess)


def leaf_inverse(blocks):
    shape = (GROUP, LEAF)
    lane = lax.broadcasted_iota(jnp.int32, shape, 1)
    sub = lax.broadcasted_iota(jnp.int32, shape, 0)
    count = LEAF // GROUP
    sets = [[b[GROUP * i : GROUP * (i + 1), :] for i in range(count)] for b in blocks]

    def row_of(v, p):
        return jnp.broadcast_to(v[p : p + 1, :], shape)

    def col_of(v, c):
        return jnp.broadcast_to(v[:, c : c + 1], shape)

    def eliminate(rows, k, panel):
        base = GROUP * k
        v = rows[k]
        cols = [col_of(v, base + p) for p in range(GROUP)]
        for p in range(GROUP):
            inv = reciprocal(row_of(cols[p], p))
            here = sub == p
            unit = jnp.where(here, 1.0, 0.0)
            v = jnp.where(lane == base + p, unit, v)
            scaled = row_of(v, p) * inv
            v = jnp.where(here, scaled, v - cols[p] * scaled)
            for q in range(p + 1, GROUP):
                entry = row_of(cols[q], p) * inv
                cols[q] = jnp.where(here, entry, cols[q] - cols[p] * entry)
        rows[k] = v
        pivots = [row_of(v, p) for p in range(GROUP)]
        inside = (lane >= base) & (lane < base + GROUP)
        for i in panel:
            if i != k:
                w = rows[i]
                acc = jnp.where(inside, 0.0, w)
                for p in range(GROUP):
                    acc = acc - col_of(w, base + p) * pivots[p]
                rows[i] = acc

    per = PANEL // GROUP
    for j in range(count // per):
        panel = list(range(per * j, per * (j + 1)))
        others = list(range(per * (j + 1), count)) + list(range(per * j))
        for k in panel:
            for rows in sets:
                eliminate(rows, k, panel[k - per * j + 1 :] + panel[: k - per * j])
        inside = (lane >= PANEL * j) & (lane < PANEL * (j + 1))
        zeros = jnp.zeros(shape, jnp.float32)
        for rows in sets:
            left = jnp.concatenate([jnp.where(inside, rows[i], 0.0) for i in others], axis=0)
            pivot = jnp.concatenate(
                [rows[i] if i in panel else zeros for i in range(count)], axis=0
            )
            product = dot3(left, pivot)
            for at, i in enumerate(others):
                kept = jnp.where(inside, 0.0, rows[i])
                rows[i] = kept - product[GROUP * at : GROUP * (at + 1), :]
    return [jnp.concatenate(rows, axis=0) for rows in sets]


def inverse_in(work_refs):
    n = work_refs[0].shape[-1]
    steps = n // LEAF

    def shifted_update(ref, src, dst, leaf):
        row = ref[src, :LEAF, LEAF:]
        col = ref[src, LEAF:, :LEAF]
        ls = split(leaf)
        cs = split(col)
        q = dot_split(ls, split(row))
        qs = split(q)
        ref[dst, : n - LEAF, : n - LEAF] = ref[src, LEAF:, LEAF:] - dot_split(cs, qs)
        ref[dst, n - LEAF :, : n - LEAF] = q
        ref[dst, : n - LEAF, n - LEAF :] = -dot_split(cs, ls)
        ref[dst, n - LEAF :, n - LEAF :] = leaf

    def body(step, leaves):
        src = lax.rem(step, 2)
        dst = 1 - src
        for ref, leaf in zip(work_refs, leaves):
            shifted_update(ref, src, dst, leaf)
        return tuple(leaf_inverse([ref[dst, :LEAF, :LEAF] for ref in work_refs]))

    leaves = tuple(leaf_inverse([ref[0, :LEAF, :LEAF] for ref in work_refs]))
    leaves = lax.fori_loop(0, steps - 1, body, leaves)
    for ref, leaf in zip(work_refs, leaves):
        shifted_update(ref, (steps - 1) % 2, steps % 2, leaf)


def plus_diagonal(matrix, row):
    shape = matrix.shape
    here = lax.broadcasted_iota(jnp.int32, shape, 0) == lax.broadcasted_iota(jnp.int32, shape, 1)
    return matrix + jnp.where(here, jnp.broadcast_to(row, shape), 0.0)


def dot_down(a, b):
    (ah, al), (bh, bl) = split(a), split(b)
    mul = functools.partial(
        lax.dot_general,
        dimension_numbers=(((0,), (0,)), ((), ())),
        preferred_element_type=jnp.float32,
    )
    return mul(ah, bh) + (mul(ah, bl) + mul(al, bh))


RIGHT, LAST, COL, MEMBER, SETTLED = range(5)


def place_bonds(flags, pattern, pieces, bonds):
    width = bonds.shape[-1]
    tiles = width // LEAF_TILE
    half = width // 2
    me = flags[MEMBER]
    for source in range(2):
        core = flags[COL] if source == 0 else 1 - flags[COL]
        own, by_x, by_y, top, bottom = pieces[5 * source : 5 * source + 5]
        for rel in range(MEMBERS):
            member = me ^ rel
            for r in range(tiles):
                rows = slice(LEAF_TILE * r, LEAF_TILE * (r + 1))
                if rel < 3:
                    tile_row = (own, by_x, by_y)[rel][rows, :]
                elif r < tiles // 2:
                    tile_row = top[rows, :]
                else:
                    tile_row = bottom[LEAF_TILE * r - half : LEAF_TILE * (r + 1) - half, :]
                for c in range(tiles // 2):
                    on = pattern[((member * 2 + core) * tiles + r) * (tiles // 2) + c]
                    tile = tile_row[:, LEAF_TILE * c : LEAF_TILE * (c + 1)]
                    scaled = tile * on.astype(jnp.float32)
                    column = pl.multiple_of(core * half + LEAF_TILE * c, LEAF_TILE)
                    bonds[member, rows, pl.ds(column, LEAF_TILE)] = scaled


def reduce_kernel(flags, pattern, masses, *refs):
    pieces = refs[:10]
    (p1, p3, i2, y10, y12, y32, y3i, yo, yi, goi, gio, mo, mi, mi_half) = refs[10:24]
    bonds, work_a, work_b = refs[24:]
    width = p1.shape[0]
    right = flags[RIGHT]
    place_bonds(flags, pattern, pieces, bonds)
    ones = jnp.ones((1, width), jnp.float32)

    def bond(k):
        return plus_diagonal(bonds[jnp.where(right == 1, MEMBERS - 1 - k, k)], ones)

    def mass(k):
        member = jnp.where((right == 1) & (k > 0), MEMBERS - k, k)
        return jnp.concatenate([masses[2 * member], masses[2 * member + 1]], axis=1)

    m1, m2, m3 = mass(1), mass(2), mass(3)
    work_a[0] = plus_diagonal(bond(0) + bond(1), m1)
    work_b[0] = plus_diagonal(bond(2) + bond(3), m3)
    inverse_in([work_a, work_b])
    p1[...] = work_a[0]
    p3[...] = work_b[0]
    c0, c1, c2, c3 = (split(bond(k)) for k in range(MEMBERS))
    q1 = split(p1[...])
    y10[...] = dot_split(c0, q1)
    y12[...] = dot_split(c1, q1)
    q3 = split(p3[...])
    y32[...] = dot_split(c2, q3)
    y3i[...] = dot_split(c3, q3)
    to_o = dot_split(split(y12[...]), c0)
    to_i = dot_split(split(y32[...]), c3)
    from_o = dot_split(split(y10[...]), c1)
    from_i = dot_split(split(y3i[...]), c2)
    mass2 = plus_diagonal(y12[...] * m1 + y32[...] * m3, m2)
    work_a[0] = to_o + to_i + mass2
    inverse_in([work_a])
    i2[...] = work_a[0]
    q2 = split(i2[...])
    yo[...] = dot_split(split(from_o), q2)
    yi[...] = dot_split(split(from_i), q2)
    so, si = split(yo[...]), split(yi[...])
    goi[...] = dot_split(so, split(to_i))
    back = dot_split(si, split(to_o))
    gio[...] = back
    sm = split(mass2)
    m0 = mass(0)
    left_on = jnp.where(right == 1, 0.0, 1.0)
    mo[...] = plus_diagonal(y10[...] * m1 + dot_split(so, sm), m0 * left_on)
    mi[...] = plus_diagonal(
        y3i[...] * m3 + dot_split(si, sm) + back * jnp.where(flags[LAST] == 1, 1.0, 0.0),
        m0 * (1.0 - left_on),
    )
    keep_half(flags, mi, mi_half)


def keep_half(flags, full, half_ref):
    half = half_ref.shape[1]
    half_ref[...] = jnp.where(flags[COL] == 0, full[:, :half], full[:, half:])


def whole(flags, mine, other):
    first = flags[COL] == 0
    a, b = mine[...], other[...]
    return jnp.concatenate([jnp.where(first, a, b), jnp.where(first, b, a)], axis=1)


def chain_kernel(flags, goi, gio, mo, mi, mine, other, new_half, si, y, work):
    mass_o = mo[...] + whole(flags, mine, other)
    work[0] = goi[...] + mass_o
    inverse_in([work])
    si[...] = work[0]
    y[...] = dot3(gio[...], si[...])
    work[0] = mi[...] + dot3(y[...], mass_o)
    keep_half(flags, work.at[0], new_half)


def root_first_kernel(flags, goi, gio, mo, mi, o_mine, o_other, i_mine, i_other, inv_i, y, left, work):
    mass_i = mi[...] + whole(flags, i_mine, i_other)
    work[0] = gio[...] + mass_i
    inverse_in([work])
    inv_i[...] = work[0]
    y[...] = dot3(goi[...], inv_i[...])
    mass_o = mo[...] + whole(flags, o_mine, o_other)
    left[...] = mass_o + dot3(y[...], mass_i)


def root_last_kernel(inv_i, y, left, ro, ro_in, ri, ri_in, xo, xi, work, inner, outer):
    work[0] = left[...]
    s = split(ri[...] + ri_in[...])
    inner[...] = dot_split(split(inv_i[...]), s)
    outer[...] = ro[...] + ro_in[...] + dot_split(split(y[...]), s)
    inverse_in([work])
    xo[...] = dot3(work[0], outer[...])
    xi[...] = inner[...] + dot_down(y[...], xo[...])


def columns_kernel(
    flags, own, by_x, by_y, by_xy, p1, p3, i2, y10, y12, y32, y3i, yo, yi, w, ao, ai, ro, ri, rhs
):
    right = flags[RIGHT]
    member = flags[MEMBER]
    for rel, piece in enumerate((own, by_x, by_y, by_xy)):
        rhs[member ^ rel] = piece[...]
    r0 = rhs[0]
    r2 = rhs[2]
    r1 = rhs[jnp.where(right == 1, 3, 1)]
    r3 = rhs[jnp.where(right == 1, 1, 3)]
    s1, s3 = split(r1), split(r3)
    v1 = dot_split(split(p1[...]), s1)
    v3 = dot_split(split(p3[...]), s3)
    r2 = r2 + dot_split(split(y12[...]), s1) + dot_split(split(y32[...]), s3)
    s2 = split(r2)
    v2 = dot_split(split(i2[...]), s2)
    left_on = jnp.where(right == 1, 0.0, 1.0)
    yos, yis = split(yo[...]), split(yi[...])
    ro[...] = r0 * left_on + dot_split(split(y10[...]), s1) + dot_split(yos, s2)
    ri[...] = r0 * (1.0 - left_on) + dot_split(split(y3i[...]), s3) + dot_split(yis, s2)
    is_2 = member == 2
    is_1 = member == jnp.where(right == 1, 3, 1)
    z = jnp.where(is_1, y12[...], y32[...])
    zs = split(z)
    w[...] = jnp.where(is_2, v2, jnp.where(is_1, v1, v3) + dot_down(z, v2))
    ao[...] = jnp.where(is_2, yo[...], dot_split(yos, zs) + jnp.where(is_1, y10[...], 0.0))
    ai[...] = jnp.where(is_2, yi[...], dot_split(yis, zs) + jnp.where(is_1, 0.0, y3i[...]))


def chain_columns_kernel(y, si, ro, ro_in, ri, new_ri, vo):
    s = split(ro[...] + ro_in[...])
    new_ri[...] = ri[...] + dot_split(split(y[...]), s)
    vo[...] = dot_split(split(si[...]), s)


def chain_back_kernel(vo, y, xi, xo):
    xo[...] = vo[...] + dot_down(y[...], xi[...])


def final_kernel(flags, w, ao, ai, y, vo, last_y, last_vo, xo, xi, in_a, in_b, in_c, out):
    last = flags[LAST] == 1
    settled = flags[SETTLED] == 1
    came = in_a[...] + in_b[...] + in_c[...]
    end = jnp.where(last, last_vo[...], vo[...]) + dot_down(
        jnp.where(last, last_y[...], y[...]), came
    )
    end_o = jnp.where(settled, xo[...], jnp.where(last, 0.0, end))
    end_i = jnp.where(settled, xi[...], jnp.where(last, end, came))
    mine = w[...] + dot_down(ao[...], end_o) + dot_down(ai[...], end_i)
    here = jnp.where(flags[RIGHT] == 1, end_i, end_o)
    out[...] = jnp.where(flags[MEMBER] == 0, here, mine)


def call(kernel, args, outs, scratch=(), flops=0):
    def spec(a):
        space = pltpu.SMEM if a.dtype == jnp.int32 else pltpu.VMEM
        return pl.BlockSpec(memory_space=space)

    moved = sum(a.size * 4 for a in args) + sum(4 * math.prod(s) for s in outs)
    held = moved + sum(4 * math.prod(s) for s in scratch)
    return pl.pallas_call(
        kernel,
        out_shape=[jax.ShapeDtypeStruct(s, jnp.float32) for s in outs],
        in_specs=[spec(a) for a in args],
        out_specs=[pl.BlockSpec(memory_space=pltpu.VMEM) for _ in outs],
        scratch_shapes=[pltpu.VMEM(s, jnp.float32) for s in scratch],
        cost_estimate=pl.CostEstimate(flops=flops, bytes_accessed=moved, transcendentals=0),
        compiler_params=pltpu.CompilerParams(vmem_limit_bytes=held + SPARE_BYTES),
    )(*args)


def on_device(coupling, tile_pattern, orbital_mass, sources):
    width = coupling.shape[1]
    half = coupling.shape[2]
    modes = sources.shape[2]
    column = lax.axis_index("col")
    member = lax.axis_index("member")
    group = lax.axis_index("group")
    groups = lax.axis_size("group")
    middle = groups // 2

    def send(x, pairs):
        return lax.ppermute(x, "group", pairs)

    def swap(x, bits):
        return lax.ppermute(x, "member", [(m, m ^ bits) for m in range(MEMBERS)])

    def other_core(x):
        return lax.ppermute(x, "col", [(0, 1), (1, 0)])

    def after(x, *others):
        return lax.optimization_barrier((x, *others))[0]

    own = coupling[0]
    by_x, by_y = swap(own, 1), swap(own, 2)
    top, bottom = swap(by_x[: width // 2], 2), swap(by_y[width // 2 :], 1)
    mine = [own, by_x, by_y, top, bottom]
    pieces = mine + [other_core(piece) for piece in mine]
    pattern = lax.all_gather(tile_pattern[0], ("member", "col"), axis=0, tiled=False)
    masses = lax.all_gather(orbital_mass, ("member", "col"), axis=0, tiled=False)
    source = after(sources[0], top, bottom)
    rhs = [source, swap(source, 1), swap(source, 2), swap(source, 3)]
    settled = (group != 0) & (group < groups - 2)
    flags = jnp.stack(
        [
            (group >= middle).astype(jnp.int32),
            (group == groups - 1).astype(jnp.int32),
            column.astype(jnp.int32),
            member.astype(jnp.int32),
            settled.astype(jnp.int32),
        ]
    )
    square = (width, width)
    block = (width, modes)
    panel = (width, half)
    room = (2, width, width)
    unit_flops = 6 * width**3
    p1, p3, i2, y10, y12, y32, y3i, yo, yi, goi, gio, mo, mi, mi_half = call(
        reduce_kernel,
        [flags, pattern.reshape(-1), masses, *pieces],
        [square] * 13 + [panel],
        [(MEMBERS, width, width), room, room],
        40 * unit_flops,
    )
    first = [(groups - 1, groups - 2)]
    into_o = send(mi_half, first)
    w, ao, ai, ro, ri = call(
        columns_kernel,
        [flags, *rhs, p1, p3, i2, y10, y12, y32, y3i, yo, yi],
        [block, square, square, block, block],
        [(MEMBERS, width, modes)],
        flops=6 * unit_flops,
    )
    ro_in = send(ri, first)
    into_o = after(into_o, ro)
    steps = []
    for t in range(middle - 1):
        new_half, si, y = call(
            chain_kernel,
            [flags, goi, gio, mo, mi, into_o, other_core(into_o)],
            [panel, square, square],
            [room],
            20 * unit_flops,
        )
        upward = [(t, t + 1)]
        downward = [(groups - 2 - t, groups - 3 - t)]
        from_left, from_right = send(new_half, upward), send(new_half, downward)
        new_ri, vo = call(
            chain_columns_kernel, [y, si, ro, ro_in, ri], [block] * 2, flops=unit_flops
        )
        steps.append((y, vo))
        rhs_left, rhs_right = send(new_ri, upward), send(new_ri, downward)
        from_left, from_right = after(from_left, vo), after(from_right, vo)
        if groups - 3 - t >= middle:
            into_o = from_left + from_right
            ro_in = rhs_left + rhs_right
        else:
            into_o, into_i = from_left, from_right
            ro_in, ri_in = rhs_left, rhs_right
    inv_i, y, left = call(
        root_first_kernel,
        [flags, goi, gio, mo, mi, into_o, other_core(into_o), into_i, other_core(into_i)],
        [square] * 3,
        [room],
        20 * unit_flops,
    )
    last_y, last_vo = (send(part, [(groups - 2, groups - 1)]) for part in steps[0])
    xo, xi = call(
        root_last_kernel,
        [inv_i, y, left, ro, ro_in, ri, ri_in],
        [block] * 2,
        [room, block, block],
        20 * unit_flops,
    )
    for t in reversed(range(1, middle - 1)):
        y, vo = steps[t]
        from_right = send(xo, [(t + 1, t)])
        from_left = send(jnp.where(group == middle - 1, xi, xo), [(groups - 3 - t, groups - 2 - t)])
        on_left = group == t
        on_right = group == groups - 2 - t
        xi = jnp.where(on_left, from_right, jnp.where(on_right, from_left, xi))
        (outer,) = call(chain_back_kernel, [vo, y, xi], [block], flops=unit_flops)
        xo = jnp.where(on_left | on_right, outer, xo)
    outward = xi if middle - 1 == groups - 3 else xo
    in_a = send(xo, [(1, 0)])
    in_b = send(outward, [(groups - 3, groups - 2)])
    in_c = send(outward, [(groups - 3, groups - 1)])
    y, vo = steps[0]
    (out,) = call(
        final_kernel,
        [flags, w, ao, ai, y, vo, last_y, last_vo, xo, xi, in_a, in_b, in_c],
        [block],
        flops=2 * unit_flops,
    )
    return out[None]


def solution(mesh):
    groups = mesh.shape["slab"] // MEMBERS
    fine = Mesh(
        mesh.devices.reshape(groups, MEMBERS, mesh.shape["col"]), ("group", "member", "col")
    )
    slab = ("group", "member")
    placed = (
        P(slab, None, "col"),
        P(slab, None, "col"),
        P(slab, "col"),
        P(slab, None, "col"),
    )
    return jax.shard_map(
        on_device, mesh=fine, in_specs=placed, out_specs=P(slab, None, "col"), check_vma=False
    )
```

```python
import functools
import math

import jax
import jax.numpy as jnp
from jax import lax
from jax.experimental import pallas as pl
from jax.experimental.pallas import tpu as pltpu
from jax.sharding import Mesh
from jax.sharding import PartitionSpec as P

MEMBERS = 4
SPARE_BYTES = 16 * 1024 * 1024

LEAF = 128
PANEL = 32
GROUP = 8


def split(x):
    high = x.astype(jnp.bfloat16)
    low = (x - high.astype(jnp.float32)).astype(jnp.bfloat16)
    return high, low


def dot_split(a, b):
    (ah, al), (bh, bl) = a, b
    mul = functools.partial(jnp.dot, preferred_element_type=jnp.float32)
    return mul(ah, bh) + (mul(ah, bl) + mul(al, bh))


def dot3(a, b):
    return dot_split(split(a), split(b))


def reciprocal(x):
    guess = pl.reciprocal(x, approx=True)
    return guess * (2.0 - x * guess)


def leaf_inverse(blocks, background=()):
    shape = (GROUP, LEAF)
    lane = lax.broadcasted_iota(jnp.int32, shape, 1)
    sub = lax.broadcasted_iota(jnp.int32, shape, 0)
    count = LEAF // GROUP
    sets = [[b[GROUP * i : GROUP * (i + 1), :] for i in range(count)] for b in blocks]
    background = list(background)

    def row_of(v, p):
        return jnp.broadcast_to(v[p : p + 1, :], shape)

    def col_of(v, c):
        return jnp.broadcast_to(v[:, c : c + 1], shape)

    def eliminate(k, order):
        base = GROUP * k
        vs = [rows[k] for rows in sets]
        cols = [[col_of(v, base + p) for p in range(GROUP)] for v in vs]
        for p in range(GROUP):
            here = sub == p
            unit = jnp.where(here, 1.0, 0.0)
            invs = [reciprocal(row_of(c[p], p)) for c in cols]
            for q in range(p + 1, GROUP):
                for c, inv in zip(cols, invs):
                    entry = row_of(c[q], p) * inv
                    c[q] = jnp.where(here, entry, c[q] - c[p] * entry)
            for at, (c, inv) in enumerate(zip(cols, invs)):
                v = jnp.where(lane == base + p, unit, vs[at])
                scaled = row_of(v, p) * inv
                vs[at] = jnp.where(here, scaled, v - c[p] * scaled)
        inside = (lane >= base) & (lane < base + GROUP)
        pivots = [[row_of(v, p) for p in range(GROUP)] for v in vs]
        for rows, v in zip(sets, vs):
            rows[k] = v
        for i in order:
            for rows, pivot in zip(sets, pivots):
                w = rows[i]
                terms = [col_of(w, base + p) * pivot[p] for p in range(GROUP)]
                while len(terms) > 1:
                    terms = [x + y for x, y in zip(terms[::2], terms[1::2])]
                rows[i] = jnp.where(inside, 0.0, w) - terms[0]

    per = PANEL // GROUP
    panels = count // per
    for j in range(panels):
        panel = list(range(per * j, per * (j + 1)))
        if j + 1 < panels:
            eager = list(range(per * (j + 1), per * (j + 2)))
        else:
            eager = list(range(per * j))
        others = [i for i in range(count) if i not in panel and i not in eager]
        for k in panel:
            eliminate(k, [i for i in panel if i > k] + [i for i in panel if i < k] + eager)
        inside = (lane >= PANEL * j) & (lane < PANEL * (j + 1))
        zeros = jnp.zeros(shape, jnp.float32)
        if others:
            for rows in sets:
                left = jnp.concatenate([jnp.where(inside, rows[i], 0.0) for i in others], axis=0)
                pivot = jnp.concatenate(
                    [rows[i] if i in panel else zeros for i in range(count)], axis=0
                )
                product = dot3(left, pivot)
                for at, i in enumerate(others):
                    kept = jnp.where(inside, 0.0, rows[i])
                    rows[i] = kept - product[GROUP * at : GROUP * (at + 1), :]
        share = -(-len(background) // (panels - j))
        for part in background[:share]:
            part()
        background = background[share:]
    return [jnp.concatenate(rows, axis=0) for rows in sets]


def inverse_in(work_refs, background=()):
    n = work_refs[0].shape[-1]
    steps = n // LEAF
    rest = n - LEAF

    def update(ref, src, dst, leaf):
        ls = split(leaf)
        cs = [split(ref[src, LEAF * r : LEAF * (r + 1), :LEAF]) for r in range(1, steps)]
        q = dot_split(ls, split(ref[src, :LEAF, LEAF : 2 * LEAF]))
        qs = [split(q)]
        pivot = ref[src, LEAF : 2 * LEAF, LEAF : 2 * LEAF] - dot_split(cs[0], qs[0])

        def prepare():
            wide = dot_split(ls, split(ref[src, :LEAF, 2 * LEAF :]))
            ref[dst, rest:, :LEAF] = q
            ref[dst, rest:, LEAF:rest] = wide
            ref[dst, rest:, rest:] = leaf
            ref[dst, :LEAF, :LEAF] = pivot
            whole_q = jnp.concatenate([q, wide], axis=1)
            qs[0] = split(whole_q)

        def strip(r):
            def run():
                rows = slice(LEAF * r, LEAF * (r + 1))
                out = slice(LEAF * (r - 1), LEAF * r)
                new = ref[src, rows, LEAF:] - dot_split(cs[r - 1], qs[0])
                if r == 1:
                    ref[dst, out, LEAF:rest] = new[:, LEAF:]
                else:
                    ref[dst, out, :rest] = new
                ref[dst, out, rest:] = -dot_split(cs[r - 1], ls)

            return run

        return pivot, [prepare] + [strip(r) for r in range(1, steps)]

    def body(step, leaves):
        src = lax.rem(step, 2)
        pivots, parts = [], []
        for ref, leaf in zip(work_refs, leaves):
            pivot, own = update(ref, src, 1 - src, leaf)
            pivots.append(pivot)
            parts.append(own)
        return tuple(leaf_inverse(pivots, [part for group in zip(*parts) for part in group]))

    leaves = tuple(leaf_inverse([ref[0, :LEAF, :LEAF] for ref in work_refs], background))
    leaves = lax.fori_loop(0, steps - 1, body, leaves)
    for ref, leaf in zip(work_refs, leaves):
        for part in update(ref, (steps - 1) % 2, steps % 2, leaf)[1]:
            part()


def plus_diagonal(matrix, row):
    shape = matrix.shape
    here = lax.broadcasted_iota(jnp.int32, shape, 0) == lax.broadcasted_iota(jnp.int32, shape, 1)
    return matrix + jnp.where(here, jnp.broadcast_to(row, shape), 0.0)


def dot_down(a, b):
    (ah, al), (bh, bl) = split(a), split(b)
    mul = functools.partial(
        lax.dot_general,
        dimension_numbers=(((0,), (0,)), ((), ())),
        preferred_element_type=jnp.float32,
    )
    return mul(ah, bh) + (mul(ah, bl) + mul(al, bh))


RIGHT, LAST, COL, MEMBER, SETTLED, PLANE = range(6)


def panel_kernel(pattern, coupling, mass, panel):
    width, half = coupling.shape
    tile_w = width // (width // LEAF)
    first = lax.axis_index("col") * half
    rows = lax.broadcasted_iota(jnp.int32, (LEAF, LEAF), 0)
    columns = lax.broadcasted_iota(jnp.int32, (LEAF, LEAF), 1)
    across = half // tile_w
    for r in range(width // tile_w):
        for c in range(across):
            at = (slice(tile_w * r, tile_w * (r + 1)), slice(tile_w * c, tile_w * (c + 1)))
            unit = (rows + tile_w * r == columns + (first + tile_w * c)).astype(jnp.float32)
            panel[at] = unit + pattern[across * r + c].astype(jnp.float32) * coupling[at]
    panel[width:, :] = jnp.broadcast_to(mass[...], (GROUP, half))


def place_bonds(flags, pieces, bonds):
    half = bonds.shape[-1] // 2
    me = flags[MEMBER]
    for source in range(2):
        core = flags[COL] if source == 0 else 1 - flags[COL]
        columns = pl.ds(pl.multiple_of(core * half, half), half)
        own, by_x, by_y, top, bottom = pieces[5 * source : 5 * source + 5]
        for rel, piece in enumerate((own, by_x, by_y)):
            bonds[me ^ rel, :, columns] = piece[...]
        bonds[me ^ 3, :half, columns] = top[...]
        bonds[me ^ 3, half:, columns] = bottom[...]


def reduce_kernel(flags, *refs):
    pieces = refs[:10]
    (p1, p3, i2, y10, y12, y32, y3i, yo, yi, goi, gio, mo, mi, mi_half) = refs[10:24]
    bonds, work_a, work_b = refs[24:]
    width = p1.shape[0]
    right = flags[RIGHT]
    place_bonds(flags, pieces, bonds)

    def bond(k):
        return bonds[jnp.where(right == 1, MEMBERS - 1 - k, k), :width, :]

    def mass(k):
        member = jnp.where((right == 1) & (k > 0), MEMBERS - k, k)
        return bonds[member, width : width + 1, :]

    m1, m2, m3 = mass(1), mass(2), mass(3)
    work_a[0] = plus_diagonal(bond(0) + bond(1), m1)
    work_b[0] = plus_diagonal(bond(2) + bond(3), m3)
    inverse_in([work_a, work_b])
    p1[...] = work_a[0]
    p3[...] = work_b[0]
    c0, c1, c2, c3 = (split(bond(k)) for k in range(MEMBERS))
    q1 = split(p1[...])
    q3 = split(p3[...])
    y12[...] = dot_split(c1, q1)
    y32[...] = dot_split(c2, q3)
    to_o = dot_split(split(y12[...]), c0)
    to_i = dot_split(split(y32[...]), c3)
    mass2 = plus_diagonal(y12[...] * m1 + y32[...] * m3, m2)
    work_a[0] = to_o + to_i + mass2

    def ends_i():
        y3i[...] = dot_split(c3, q3)

    def ends_o():
        y10[...] = dot_split(c0, q1)

    def from_i():
        work_b[0] = dot_split(split(y3i[...]), c2)

    def from_o():
        work_b[1] = dot_split(split(y10[...]), c1)

    inverse_in([work_a], [ends_i, ends_o, from_i, from_o])
    i2[...] = work_a[0]
    q2 = split(i2[...])
    sm = split(mass2)
    m0 = mass(0)
    left_on = jnp.where(right == 1, 0.0, 1.0)
    yi[...] = dot_split(split(work_b[0]), q2)
    si = split(yi[...])
    back = dot_split(si, split(to_o))
    gio[...] = back
    mi[...] = plus_diagonal(
        y3i[...] * m3 + dot_split(si, sm) + back * jnp.where(flags[LAST] == 1, 1.0, 0.0),
        m0 * (1.0 - left_on),
    )
    keep_half(flags, mi, mi_half)

    @pl.when(flags[LAST] == 0)
    def _():
        yo[...] = dot_split(split(work_b[1]), q2)
        so = split(yo[...])
        goi[...] = dot_split(so, split(to_i))
        mo[...] = plus_diagonal(y10[...] * m1 + dot_split(so, sm), m0 * left_on)

    @pl.when(flags[LAST] == 1)
    def _():
        yo[...] = jnp.zeros_like(yo)


def keep_half(flags, full, half_ref):
    half = half_ref.shape[1]
    half_ref[...] = jnp.where(flags[COL] == 0, full[:, :half], full[:, half:])


def whole(flags, mine, other):
    first = flags[COL] == 0
    a, b = mine[...], other[...]
    return jnp.concatenate([jnp.where(first, a, b), jnp.where(first, b, a)], axis=1)


def chain_kernel(planes, flags, goi, gio, mo, mi, mine, other, new_half, si, y, work):
    @pl.when((flags[PLANE] == planes[0]) | (flags[PLANE] == planes[1]))
    def _():
        mass_o = mo[...] + whole(flags, mine, other)
        work[0] = goi[...] + mass_o
        inverse_in([work])
        si[...] = work[0]
        y[...] = dot3(gio[...], si[...])
        work[0] = mi[...] + dot3(y[...], mass_o)
        keep_half(flags, work.at[0], new_half)


def root_first_kernel(
    root, flags, goi, gio, mo, mi, o_mine, o_other, i_mine, i_other, inv_i, y, left, work
):
    @pl.when(flags[PLANE] == root)
    def _():
        mass_i = mi[...] + whole(flags, i_mine, i_other)
        work[0] = gio[...] + mass_i
        inverse_in([work])
        inv_i[...] = work[0]
        y[...] = dot3(goi[...], inv_i[...])
        mass_o = mo[...] + whole(flags, o_mine, o_other)
        left[...] = mass_o + dot3(y[...], mass_i)


def root_last_kernel(
    root, flags, inv_i, y, left, ro, ro_in, ri, ri_in, xo, xi, work, inner, outer
):
    @pl.when(flags[PLANE] == root)
    def _():
        work[0] = left[...]

        def columns():
            s = split(ri[...] + ri_in[...])
            inner[...] = dot_split(split(inv_i[...]), s)
            outer[...] = ro[...] + ro_in[...] + dot_split(split(y[...]), s)

        inverse_in([work], [columns])
        xo[...] = dot3(work[0], outer[...])
        xi[...] = inner[...] + dot_down(y[...], xo[...])


def columns_kernel(
    flags, own, by_x, by_y, by_xy, p1, p3, i2, y10, y12, y32, y3i, yo, yi, w, ao, ai, ro, ri, rhs
):
    right = flags[RIGHT]
    member = flags[MEMBER]
    for rel, piece in enumerate((own, by_x, by_y, by_xy)):
        rhs[member ^ rel] = piece[...]
    r0 = rhs[0]
    r2 = rhs[2]
    r1 = rhs[jnp.where(right == 1, 3, 1)]
    r3 = rhs[jnp.where(right == 1, 1, 3)]
    s1, s3 = split(r1), split(r3)
    v1 = dot_split(split(p1[...]), s1)
    v3 = dot_split(split(p3[...]), s3)
    r2 = r2 + dot_split(split(y12[...]), s1) + dot_split(split(y32[...]), s3)
    s2 = split(r2)
    v2 = dot_split(split(i2[...]), s2)
    left_on = jnp.where(right == 1, 0.0, 1.0)
    yos, yis = split(yo[...]), split(yi[...])
    ro[...] = r0 * left_on + dot_split(split(y10[...]), s1) + dot_split(yos, s2)
    ri[...] = r0 * (1.0 - left_on) + dot_split(split(y3i[...]), s3) + dot_split(yis, s2)
    is_2 = member == 2
    is_1 = member == jnp.where(right == 1, 3, 1)
    z = jnp.where(is_1, y12[...], y32[...])
    zs = split(z)
    w[...] = jnp.where(is_2, v2, jnp.where(is_1, v1, v3) + dot_down(z, v2))
    ao[...] = jnp.where(is_2, yo[...], dot_split(yos, zs) + jnp.where(is_1, y10[...], 0.0))
    ai[...] = jnp.where(is_2, yi[...], dot_split(yis, zs) + jnp.where(is_1, 0.0, y3i[...]))


def chain_columns_kernel(y, si, ro, ro_in, ri, new_ri, vo):
    s = split(ro[...] + ro_in[...])
    new_ri[...] = ri[...] + dot_split(split(y[...]), s)
    vo[...] = dot_split(split(si[...]), s)


def chain_back_kernel(vo, y, xi, xo):
    xo[...] = vo[...] + dot_down(y[...], xi[...])


def final_kernel(flags, w, ao, ai, y, vo, last_y, last_vo, xo, xi, in_a, in_b, in_c, out):
    last = flags[LAST] == 1
    settled = flags[SETTLED] == 1
    came = in_a[...] + in_b[...] + in_c[...]
    end = jnp.where(last, last_vo[...], vo[...]) + dot_down(
        jnp.where(last, last_y[...], y[...]), came
    )
    end_o = jnp.where(settled, xo[...], jnp.where(last, 0.0, end))
    end_i = jnp.where(settled, xi[...], jnp.where(last, end, came))
    mine = w[...] + dot_down(ao[...], end_o) + dot_down(ai[...], end_i)
    here = jnp.where(flags[RIGHT] == 1, end_i, end_o)
    out[...] = jnp.where(flags[MEMBER] == 0, here, mine)


def call(kernel, args, outs, scratch=(), flops=0):
    def spec(a):
        space = pltpu.SMEM if a.dtype == jnp.int32 else pltpu.VMEM
        return pl.BlockSpec(memory_space=space)

    moved = sum(a.size * 4 for a in args) + sum(4 * math.prod(s) for s in outs)
    held = moved + sum(4 * math.prod(s) for s in scratch)
    return pl.pallas_call(
        kernel,
        out_shape=[jax.ShapeDtypeStruct(s, jnp.float32) for s in outs],
        in_specs=[spec(a) for a in args],
        out_specs=[pl.BlockSpec(memory_space=pltpu.VMEM) for _ in outs],
        scratch_shapes=[pltpu.VMEM(s, jnp.float32) for s in scratch],
        cost_estimate=pl.CostEstimate(flops=flops, bytes_accessed=moved, transcendentals=0),
        compiler_params=pltpu.CompilerParams(vmem_limit_bytes=held + SPARE_BYTES),
    )(*args)


def on_device(coupling, tile_pattern, orbital_mass, sources):
    width = coupling.shape[1]
    half = coupling.shape[2]
    modes = sources.shape[2]
    column = lax.axis_index("col")
    member = lax.axis_index("member")
    group = lax.axis_index("group")
    groups = lax.axis_size("group")
    middle = groups // 2

    def send(x, pairs):
        return lax.ppermute(x, "group", pairs)

    def swap(x, bits):
        return lax.ppermute(x, "member", [(m, m ^ bits) for m in range(MEMBERS)])

    def other_core(x):
        return lax.ppermute(x, "col", [(0, 1), (1, 0)])

    def after(x, *others):
        return lax.optimization_barrier((x, *others))[0]

    (own,) = call(
        panel_kernel,
        [tile_pattern[0].reshape(-1), coupling[0], orbital_mass],
        [(width + GROUP, half)],
    )
    by_x, by_y = swap(own, 1), swap(own, 2)
    top, bottom = swap(by_x[:half], 2), swap(by_y[half:], 1)
    mine = [own, by_x, by_y, top, bottom]
    pieces = mine + [other_core(piece) for piece in mine]
    source = after(sources[0], top, bottom)
    rhs = [source, swap(source, 1), swap(source, 2), swap(source, 3)]
    settled = (group != 0) & (group < groups - 2)
    flags = jnp.stack(
        [
            (group >= middle).astype(jnp.int32),
            (group == groups - 1).astype(jnp.int32),
            column.astype(jnp.int32),
            member.astype(jnp.int32),
            settled.astype(jnp.int32),
            group.astype(jnp.int32),
        ]
    )
    square = (width, width)
    block = (width, modes)
    panel = (width, half)
    room = (2, width, width)
    unit_flops = 6 * width**3
    p1, p3, i2, y10, y12, y32, y3i, yo, yi, goi, gio, mo, mi, mi_half = call(
        reduce_kernel,
        [flags, *pieces],
        [square] * 13 + [panel],
        [(MEMBERS, width + GROUP, width), room, room],
        40 * unit_flops,
    )
    first = [(groups - 1, groups - 2)]
    into_o = send(mi_half, first)
    w, ao, ai, ro, ri = call(
        columns_kernel,
        [flags, *rhs, p1, p3, i2, y10, y12, y32, y3i, yo, yi],
        [block, square, square, block, block],
        [(MEMBERS, width, modes)],
        flops=6 * unit_flops,
    )
    ro_in = send(ri, first)
    into_o = after(into_o, ro)
    steps = []
    for t in range(middle - 1):
        new_half, si, y = call(
            functools.partial(chain_kernel, (t, groups - 2 - t)),
            [flags, goi, gio, mo, mi, into_o, other_core(into_o)],
            [panel, square, square],
            [room],
            20 * unit_flops,
        )
        upward = [(t, t + 1)]
        downward = [(groups - 2 - t, groups - 3 - t)]
        from_left, from_right = send(new_half, upward), send(new_half, downward)
        new_ri, vo = call(
            chain_columns_kernel, [y, si, ro, ro_in, ri], [block] * 2, flops=unit_flops
        )
        steps.append((y, vo))
        rhs_left, rhs_right = send(new_ri, upward), send(new_ri, downward)
        from_left, from_right = after(from_left, vo), after(from_right, vo)
        if groups - 3 - t >= middle:
            into_o = from_left + from_right
            ro_in = rhs_left + rhs_right
        else:
            into_o, into_i = from_left, from_right
            ro_in, ri_in = rhs_left, rhs_right
    inv_i, y, left = call(
        functools.partial(root_first_kernel, middle - 1),
        [flags, goi, gio, mo, mi, into_o, other_core(into_o), into_i, other_core(into_i)],
        [square] * 3,
        [room],
        20 * unit_flops,
    )
    last_y, last_vo = (send(after(part, inv_i), [(groups - 2, groups - 1)]) for part in steps[0])
    xo, xi = call(
        functools.partial(root_last_kernel, middle - 1),
        [flags, inv_i, y, left, ro, ro_in, ri, ri_in],
        [block] * 2,
        [room, block, block],
        20 * unit_flops,
    )
    for t in reversed(range(1, middle - 1)):
        y, vo = steps[t]
        from_right = send(xo, [(t + 1, t)])
        from_left = send(jnp.where(group == middle - 1, xi, xo), [(groups - 3 - t, groups - 2 - t)])
        on_left = group == t
        on_right = group == groups - 2 - t
        xi = jnp.where(on_left, from_right, jnp.where(on_right, from_left, xi))
        (outer,) = call(chain_back_kernel, [vo, y, xi], [block], flops=unit_flops)
        xo = jnp.where(on_left | on_right, outer, xo)
    outward = xi if middle - 1 == groups - 3 else xo
    in_a = send(xo, [(1, 0)])
    in_b = send(outward, [(groups - 3, groups - 2)])
    in_c = send(outward, [(groups - 3, groups - 1)])
    y, vo = steps[0]
    (out,) = call(
        final_kernel,
        [flags, w, ao, ai, y, vo, last_y, last_vo, xo, xi, in_a, in_b, in_c],
        [block],
        flops=2 * unit_flops,
    )
    return out[None]


def solution(mesh):
    groups = mesh.shape["slab"] // MEMBERS
    fine = Mesh(
        mesh.devices.reshape(groups, MEMBERS, mesh.shape["col"]), ("group", "member", "col")
    )
    slab = ("group", "member")
    placed = (
        P(slab, None, "col"),
        P(slab, None, "col"),
        P(slab, "col"),
        P(slab, None, "col"),
    )
    return jax.shard_map(
        on_device, mesh=fine, in_specs=placed, out_specs=P(slab, None, "col"), check_vma=False
    )
```

```python
import functools
import math

import jax
import jax.numpy as jnp
from jax import lax
from jax.experimental import pallas as pl
from jax.experimental.pallas import tpu as pltpu
from jax.sharding import Mesh
from jax.sharding import PartitionSpec as P

MEMBERS = 4
SPARE_BYTES = 16 * 1024 * 1024

LEAF = 128
PANEL = 32
GROUP = 8


def split(x):
    high = x.astype(jnp.bfloat16)
    low = (x - high.astype(jnp.float32)).astype(jnp.bfloat16)
    return high, low


def dot_split(a, b):
    (ah, al), (bh, bl) = a, b
    mul = functools.partial(jnp.dot, preferred_element_type=jnp.float32)
    return mul(ah, bh) + (mul(ah, bl) + mul(al, bh))


def dot3(a, b):
    return dot_split(split(a), split(b))


def leaf_inverse(blocks, background=()):
    shape = (GROUP, LEAF)
    lane = lax.broadcasted_iota(jnp.int32, shape, 1)
    sub = lax.broadcasted_iota(jnp.int32, shape, 0)
    count = LEAF // GROUP
    sets = [[b[GROUP * i : GROUP * (i + 1), :] for i in range(count)] for b in blocks]
    background = list(background)

    def row_of(v, p):
        return jnp.broadcast_to(v[p : p + 1, :], shape)

    def col_of(v, c):
        return jnp.broadcast_to(v[:, c : c + 1], shape)

    def eliminate(k, order):
        base = GROUP * k
        vs = [rows[k] for rows in sets]
        cols = [[col_of(v, base + p) for p in range(GROUP)] for v in vs]
        for p in range(0, GROUP, 2):
            first, second = sub == p, sub == p + 1
            both = first | second
            for at, c in enumerate(cols):
                a, b = row_of(c[p], p), row_of(c[p + 1], p)
                b_low, d = row_of(c[p], p + 1), row_of(c[p + 1], p + 1)
                det = a * d - b * b_low
                guess = pl.reciprocal(det, approx=True)
                refine = 2.0 - det * guess
                m0 = jnp.where(first, -1.0, jnp.where(second, 0.0, c[p]))
                m1 = jnp.where(first, 0.0, jnp.where(second, -1.0, c[p + 1]))

                def solved(x):
                    e0, e1 = row_of(x, p), row_of(x, p + 1)
                    t0 = d * e0 - b * e1
                    t1 = a * e1 - b_low * e0
                    return jnp.where(both, 0.0, x) - ((m0 * t0 + m1 * t1) * guess) * refine

                for q in range(p + 2, GROUP):
                    c[q] = solved(c[q])
                unit0 = jnp.where(first, 1.0, 0.0)
                unit1 = jnp.where(second, 1.0, 0.0)
                v = jnp.where(lane == base + p, unit0, jnp.where(lane == base + p + 1, unit1, vs[at]))
                vs[at] = solved(v)
        inside = (lane >= base) & (lane < base + GROUP)
        pivots = [[row_of(v, p) for p in range(GROUP)] for v in vs]
        for rows, v in zip(sets, vs):
            rows[k] = v
        for i in order:
            for rows, pivot in zip(sets, pivots):
                w = rows[i]
                terms = [col_of(w, base + p) * pivot[p] for p in range(GROUP)]
                while len(terms) > 1:
                    terms = [x + y for x, y in zip(terms[::2], terms[1::2])]
                rows[i] = jnp.where(inside, 0.0, w) - terms[0]

    per = PANEL // GROUP
    panels = count // per
    for j in range(panels):
        panel = list(range(per * j, per * (j + 1)))
        if j + 1 < panels:
            eager = list(range(per * (j + 1), per * (j + 2)))
        else:
            eager = list(range(per * j))
        others = [i for i in range(count) if i not in panel and i not in eager]
        for k in panel:
            eliminate(k, [i for i in panel if i > k] + [i for i in panel if i < k] + eager)
        inside = (lane >= PANEL * j) & (lane < PANEL * (j + 1))
        zeros = jnp.zeros(shape, jnp.float32)
        if others:
            for rows in sets:
                left = jnp.concatenate([jnp.where(inside, rows[i], 0.0) for i in others], axis=0)
                pivot = jnp.concatenate(
                    [rows[i] if i in panel else zeros for i in range(count)], axis=0
                )
                product = dot3(left, pivot)
                for at, i in enumerate(others):
                    kept = jnp.where(inside, 0.0, rows[i])
                    rows[i] = kept - product[GROUP * at : GROUP * (at + 1), :]
        share = -(-len(background) // (panels - j))
        for part in background[:share]:
            part()
        background = background[share:]
    return [jnp.concatenate(rows, axis=0) for rows in sets]


def inverse_in(work_refs, background=()):
    n = work_refs[0].shape[-1]
    steps = n // LEAF
    rest = n - LEAF
    scales = []
    for ref in work_refs:
        largest = jnp.max(jnp.max(jnp.abs(ref[0]), axis=0, keepdims=True), axis=1, keepdims=True)
        scales.append(1.0 / largest)
        ref[0] = ref[0] * scales[-1]

    def update(ref, src, dst, leaf):
        ls = split(leaf)
        cs = [split(ref[src, LEAF * r : LEAF * (r + 1), :LEAF]) for r in range(1, steps)]
        q = dot_split(ls, split(ref[src, :LEAF, LEAF : 2 * LEAF]))
        qs = [split(q)]
        pivot = ref[src, LEAF : 2 * LEAF, LEAF : 2 * LEAF] - dot_split(cs[0], qs[0])

        def prepare():
            wide = dot_split(ls, split(ref[src, :LEAF, 2 * LEAF :]))
            ref[dst, rest:, :LEAF] = q
            ref[dst, rest:, LEAF:rest] = wide
            ref[dst, rest:, rest:] = leaf
            ref[dst, :LEAF, :LEAF] = pivot
            whole_q = jnp.concatenate([q, wide], axis=1)
            qs[0] = split(whole_q)

        def strip(r):
            def run():
                rows = slice(LEAF * r, LEAF * (r + 1))
                out = slice(LEAF * (r - 1), LEAF * r)
                new = ref[src, rows, LEAF:] - dot_split(cs[r - 1], qs[0])
                if r == 1:
                    ref[dst, out, LEAF:rest] = new[:, LEAF:]
                else:
                    ref[dst, out, :rest] = new
                ref[dst, out, rest:] = -dot_split(cs[r - 1], ls)

            return run

        return pivot, [prepare] + [strip(r) for r in range(1, steps)]

    def body(step, leaves):
        src = lax.rem(step, 2)
        pivots, parts = [], []
        for ref, leaf in zip(work_refs, leaves):
            pivot, own = update(ref, src, 1 - src, leaf)
            pivots.append(pivot)
            parts.append(own)
        return tuple(leaf_inverse(pivots, [part for group in zip(*parts) for part in group]))

    leaves = tuple(leaf_inverse([ref[0, :LEAF, :LEAF] for ref in work_refs], background))
    leaves = lax.fori_loop(0, steps - 1, body, leaves)
    for ref, leaf in zip(work_refs, leaves):
        for part in update(ref, (steps - 1) % 2, steps % 2, leaf)[1]:
            part()
    for ref, scale in zip(work_refs, scales):
        ref[0] = ref[0] * scale


def plus_diagonal(matrix, row):
    shape = matrix.shape
    here = lax.broadcasted_iota(jnp.int32, shape, 0) == lax.broadcasted_iota(jnp.int32, shape, 1)
    return matrix + jnp.where(here, jnp.broadcast_to(row, shape), 0.0)


def dot_down(a, b):
    (ah, al), (bh, bl) = split(a), split(b)
    mul = functools.partial(
        lax.dot_general,
        dimension_numbers=(((0,), (0,)), ((), ())),
        preferred_element_type=jnp.float32,
    )
    return mul(ah, bh) + (mul(ah, bl) + mul(al, bh))


RIGHT, LAST, COL, MEMBER, SETTLED, PLANE = range(6)


def panel_kernel(pattern, coupling, mass, panel):
    width, half = coupling.shape
    tile_w = width // (width // LEAF)
    first = lax.axis_index("col") * half
    rows = lax.broadcasted_iota(jnp.int32, (LEAF, LEAF), 0)
    columns = lax.broadcasted_iota(jnp.int32, (LEAF, LEAF), 1)
    across = half // tile_w
    for r in range(width // tile_w):
        for c in range(across):
            at = (slice(tile_w * r, tile_w * (r + 1)), slice(tile_w * c, tile_w * (c + 1)))
            unit = (rows + tile_w * r == columns + (first + tile_w * c)).astype(jnp.float32)
            panel[at] = unit + pattern[across * r + c].astype(jnp.float32) * coupling[at]
    panel[width:, :] = jnp.broadcast_to(mass[...], (GROUP, half))


def place_bonds(flags, pieces, bonds):
    half = bonds.shape[-1] // 2
    me = flags[MEMBER]
    for source in range(2):
        core = flags[COL] if source == 0 else 1 - flags[COL]
        columns = pl.ds(pl.multiple_of(core * half, half), half)
        own, by_x, by_y, top, bottom = pieces[5 * source : 5 * source + 5]
        for rel, piece in enumerate((own, by_x, by_y)):
            bonds[me ^ rel, :, columns] = piece[...]
        bonds[me ^ 3, :half, columns] = top[...]
        bonds[me ^ 3, half:, columns] = bottom[...]


def first_kernel(flags, *refs):
    pieces = refs[:10]
    bonds, inverse, placed, work = refs[10:]
    width = inverse.shape[0]
    right = flags[RIGHT]
    place_bonds(flags, pieces, placed)
    for k in range(MEMBERS):
        at = jnp.where(right == 1, MEMBERS - 1 - k, k)
        bonds[k, :width, :] = placed[at, :width, :]
        at = jnp.where((right == 1) & (k > 0), MEMBERS - k, k)
        bonds[k, width:, :] = placed[at, width:, :]
    side = 2 * flags[COL]
    work[0] = plus_diagonal(
        bonds[side, :width, :] + bonds[side + 1, :width, :], bonds[side + 1, width : width + 1, :]
    )
    inverse_in([work])
    inverse[...] = work[0]


def sides(flags, mine, other):
    first = flags[COL] == 0
    a, b = mine[...], other[...]
    return jnp.where(first, a, b), jnp.where(first, b, a)


def reduce_kernel(
    flags, bonds, mine, other, i2, y10, y12, y32, y3i, yo, yi, goi, gio, mo, mi, mi_half, work_a, work_b
):
    width = i2.shape[0]

    def bond(k):
        return bonds[k, :width, :]

    def mass(k):
        return bonds[k, width : width + 1, :]

    right = flags[RIGHT]
    m1, m2, m3 = mass(1), mass(2), mass(3)
    c0, c1, c2, c3 = (split(bond(k)) for k in range(MEMBERS))
    p1, p3 = sides(flags, mine, other)
    q1, q3 = split(p1), split(p3)
    y12[...] = dot_split(c1, q1)
    y32[...] = dot_split(c2, q3)
    to_o = dot_split(split(y12[...]), c0)
    to_i = dot_split(split(y32[...]), c3)
    mass2 = plus_diagonal(y12[...] * m1 + y32[...] * m3, m2)
    work_a[0] = to_o + to_i + mass2

    def ends_i():
        y3i[...] = dot_split(c3, q3)

    def ends_o():
        y10[...] = dot_split(c0, q1)

    def from_i():
        work_b[0] = dot_split(split(y3i[...]), c2)

    def from_o():
        work_b[1] = dot_split(split(y10[...]), c1)

    inverse_in([work_a], [ends_i, ends_o, from_i, from_o])
    i2[...] = work_a[0]
    q2 = split(i2[...])
    sm = split(mass2)
    m0 = mass(0)
    left_on = jnp.where(right == 1, 0.0, 1.0)
    yi[...] = dot_split(split(work_b[0]), q2)
    si = split(yi[...])
    back = dot_split(si, split(to_o))
    gio[...] = back
    mi[...] = plus_diagonal(
        y3i[...] * m3 + dot_split(si, sm) + back * jnp.where(flags[LAST] == 1, 1.0, 0.0),
        m0 * (1.0 - left_on),
    )
    keep_half(flags, mi, mi_half)

    @pl.when(flags[LAST] == 0)
    def _():
        yo[...] = dot_split(split(work_b[1]), q2)
        so = split(yo[...])
        goi[...] = dot_split(so, split(to_i))
        mo[...] = plus_diagonal(y10[...] * m1 + dot_split(so, sm), m0 * left_on)

    @pl.when(flags[LAST] == 1)
    def _():
        yo[...] = jnp.zeros_like(yo)


def keep_half(flags, full, half_ref):
    half = half_ref.shape[1]
    half_ref[...] = jnp.where(flags[COL] == 0, full[:, :half], full[:, half:])


def whole(flags, mine, other):
    first = flags[COL] == 0
    a, b = mine[...], other[...]
    return jnp.concatenate([jnp.where(first, a, b), jnp.where(first, b, a)], axis=1)


def chain_kernel(planes, flags, goi, gio, mo, mi, mine, other, new_half, si, y, work):
    @pl.when((flags[PLANE] == planes[0]) | (flags[PLANE] == planes[1]))
    def _():
        mass_o = mo[...] + whole(flags, mine, other)
        work[0] = goi[...] + mass_o
        inverse_in([work])
        si[...] = work[0]
        y[...] = dot3(gio[...], si[...])
        work[0] = mi[...] + dot3(y[...], mass_o)
        keep_half(flags, work.at[0], new_half)


def root_first_kernel(
    root, flags, goi, gio, mo, mi, o_mine, o_other, i_mine, i_other, inv_i, y, left, work
):
    @pl.when(flags[PLANE] == root)
    def _():
        mass_i = mi[...] + whole(flags, i_mine, i_other)
        work[0] = gio[...] + mass_i
        inverse_in([work])
        inv_i[...] = work[0]
        y[...] = dot3(goi[...], inv_i[...])
        mass_o = mo[...] + whole(flags, o_mine, o_other)
        left[...] = mass_o + dot3(y[...], mass_i)


def root_last_kernel(
    root, flags, inv_i, y, left, ro, ro_in, ri, ri_in, xo, xi, work, inner, outer
):
    @pl.when(flags[PLANE] == root)
    def _():
        work[0] = left[...]

        def columns():
            s = split(ri[...] + ri_in[...])
            inner[...] = dot_split(split(inv_i[...]), s)
            outer[...] = ro[...] + ro_in[...] + dot_split(split(y[...]), s)

        inverse_in([work], [columns])
        xo[...] = dot3(work[0], outer[...])
        xi[...] = inner[...] + dot_down(y[...], xo[...])


def columns_kernel(
    flags, own, by_x, by_y, by_xy, p_mine, p_other, i2, y10, y12, y32, y3i, yo, yi, w, ao, ai, ro, ri, rhs
):
    right = flags[RIGHT]
    member = flags[MEMBER]
    for rel, piece in enumerate((own, by_x, by_y, by_xy)):
        rhs[member ^ rel] = piece[...]
    r0 = rhs[0]
    r2 = rhs[2]
    r1 = rhs[jnp.where(right == 1, 3, 1)]
    r3 = rhs[jnp.where(right == 1, 1, 3)]
    s1, s3 = split(r1), split(r3)
    p1, p3 = sides(flags, p_mine, p_other)
    v1 = dot_split(split(p1), s1)
    v3 = dot_split(split(p3), s3)
    r2 = r2 + dot_split(split(y12[...]), s1) + dot_split(split(y32[...]), s3)
    s2 = split(r2)
    v2 = dot_split(split(i2[...]), s2)
    left_on = jnp.where(right == 1, 0.0, 1.0)
    yos, yis = split(yo[...]), split(yi[...])
    ro[...] = r0 * left_on + dot_split(split(y10[...]), s1) + dot_split(yos, s2)
    ri[...] = r0 * (1.0 - left_on) + dot_split(split(y3i[...]), s3) + dot_split(yis, s2)
    is_2 = member == 2
    is_1 = member == jnp.where(right == 1, 3, 1)
    z = jnp.where(is_1, y12[...], y32[...])
    zs = split(z)
    w[...] = jnp.where(is_2, v2, jnp.where(is_1, v1, v3) + dot_down(z, v2))
    ao[...] = jnp.where(is_2, yo[...], dot_split(yos, zs) + jnp.where(is_1, y10[...], 0.0))
    ai[...] = jnp.where(is_2, yi[...], dot_split(yis, zs) + jnp.where(is_1, 0.0, y3i[...]))


def chain_columns_kernel(y, si, ro, ro_in, ri, new_ri, vo):
    s = split(ro[...] + ro_in[...])
    new_ri[...] = ri[...] + dot_split(split(y[...]), s)
    vo[...] = dot_split(split(si[...]), s)


def chain_back_kernel(vo, y, xi, xo):
    xo[...] = vo[...] + dot_down(y[...], xi[...])


def final_kernel(flags, w, ao, ai, y, vo, last_y, last_vo, xo, xi, in_a, in_b, in_c, out):
    last = flags[LAST] == 1
    settled = flags[SETTLED] == 1
    came = in_a[...] + in_b[...] + in_c[...]
    end = jnp.where(last, last_vo[...], vo[...]) + dot_down(
        jnp.where(last, last_y[...], y[...]), came
    )
    end_o = jnp.where(settled, xo[...], jnp.where(last, 0.0, end))
    end_i = jnp.where(settled, xi[...], jnp.where(last, end, came))
    mine = w[...] + dot_down(ao[...], end_o) + dot_down(ai[...], end_i)
    here = jnp.where(flags[RIGHT] == 1, end_i, end_o)
    out[...] = jnp.where(flags[MEMBER] == 0, here, mine)


def call(kernel, args, outs, scratch=(), flops=0):
    def spec(a):
        space = pltpu.SMEM if a.dtype == jnp.int32 else pltpu.VMEM
        return pl.BlockSpec(memory_space=space)

    moved = sum(a.size * 4 for a in args) + sum(4 * math.prod(s) for s in outs)
    held = moved + sum(4 * math.prod(s) for s in scratch)
    return pl.pallas_call(
        kernel,
        out_shape=[jax.ShapeDtypeStruct(s, jnp.float32) for s in outs],
        in_specs=[spec(a) for a in args],
        out_specs=[pl.BlockSpec(memory_space=pltpu.VMEM) for _ in outs],
        scratch_shapes=[pltpu.VMEM(s, jnp.float32) for s in scratch],
        cost_estimate=pl.CostEstimate(flops=flops, bytes_accessed=moved, transcendentals=0),
        compiler_params=pltpu.CompilerParams(vmem_limit_bytes=held + SPARE_BYTES),
    )(*args)


def on_device(coupling, tile_pattern, orbital_mass, sources):
    width = coupling.shape[1]
    half = coupling.shape[2]
    modes = sources.shape[2]
    column = lax.axis_index("col")
    member = lax.axis_index("member")
    group = lax.axis_index("group")
    groups = lax.axis_size("group")
    middle = groups // 2

    def send(x, pairs):
        return lax.ppermute(x, "group", pairs)

    def swap(x, bits):
        return lax.ppermute(x, "member", [(m, m ^ bits) for m in range(MEMBERS)])

    def other_core(x):
        return lax.ppermute(x, "col", [(0, 1), (1, 0)])

    def after(x, *others):
        return lax.optimization_barrier((x, *others))[0]

    (own,) = call(
        panel_kernel,
        [tile_pattern[0].reshape(-1), coupling[0], orbital_mass],
        [(width + GROUP, half)],
    )
    by_x, by_y = swap(own, 1), swap(own, 2)
    top, bottom = swap(by_x[:half], 2), swap(by_y[half:], 1)
    mine = [own, by_x, by_y, top, bottom]
    pieces = mine + [other_core(piece) for piece in mine]
    settled = flags[SETTLED] == 1
    came = in_a[...] + in_b[...] + in_c[...]
    end = jnp.where(last, last_vo[...], vo[...]) + dot_down(
        jnp.where(last, last_y[...], y[...]), came
    )
    end_o = jnp.where(settled, xo[...], jnp.where(last, 0.0, end))
    end_i = jnp.where(settled, xi[...], jnp.where(last, end, came))
    mine = w[...] + dot_down(ao[...], end_o) + dot_down(ai[...], end_i)
    here = jnp.where(flags[RIGHT] == 1, end_i, end_o)
    out[...] = jnp.where(flags[MEMBER] == 0, here, mine)


def call(kernel, args, outs, scratch=(), flops=0):
    def spec(a):
        space = pltpu.SMEM if a.dtype == jnp.int32 else pltpu.VMEM
        return pl.BlockSpec(memory_space=space)

    moved = sum(a.size * 4 for a in args) + sum(4 * math.prod(s) for s in outs)
    held = moved + sum(4 * math.prod(s) for s in scratch)
    return pl.pallas_call(
        kernel,
        out_shape=[jax.ShapeDtypeStruct(s, jnp.float32) for s in outs],
        in_specs=[spec(a) for a in args],
        out_specs=[pl.BlockSpec(memory_space=pltpu.VMEM) for _ in outs],
        scratch_shapes=[pltpu.VMEM(s, jnp.float32) for s in scratch],
        cost_estimate=pl.CostEstimate(flops=flops, bytes_accessed=moved, transcendentals=0),
        compiler_params=pltpu.CompilerParams(vmem_limit_bytes=held + SPARE_BYTES),
    )(*args)


def on_device(coupling, tile_pattern, orbital_mass, sources):
    width = coupling.shape[1]
    half = coupling.shape[2]
    modes = sources.shape[2]
    column = lax.axis_index("col")
    member = lax.axis_index("member")
    group = lax.axis_index("group")
    groups = lax.axis_size("group")
    middle = groups // 2

    def send(x, pairs):
        return lax.ppermute(x, "group", pairs)

    def swap(x, bits):
        return lax.ppermute(x, "member", [(m, m ^ bits) for m in range(MEMBERS)])

    def other_core(x):
        return lax.ppermute(x, "col", [(0, 1), (1, 0)])

    def after(x, *others):
        return lax.optimization_barrier((x, *others))[0]

    (own,) = call(
        panel_kernel,
        [tile_pattern[0].reshape(-1), coupling[0], orbital_mass],
        [(width + GROUP, half)],
    )
    by_x, by_y = swap(own, 1), swap(own, 2)
    top, bottom = swap(by_x[:half], 2), swap(by_y[half:], 1)
    mine = [own, by_x, by_y, top, bottom]
    pieces = mine + [other_core(piece) for piece in mine]
    source = after(sources[0], top, bottom)
    rhs = [source, swap(source, 1), swap(source, 2), swap(source, 3)]
    settled = (group != 0) & (group < groups - 2)
    flags = jnp.stack(
        [
            (group >= middle).astype(jnp.int32),
            (group == groups - 1).astype(jnp.int32),
            column.astype(jnp.int32),
            member.astype(jnp.int32),
            settled.astype(jnp.int32),
            group.astype(jnp.int32),
        ]
    )
    square = (width, width)
    block = (width, modes)
    panel = (width, half)
    room = (2, width, width)
    unit_flops = 6 * width**3
    bonds, p_mine = call(
        first_kernel,
        [flags, *pieces],
        [(MEMBERS, width + GROUP, width), square],
        [(MEMBERS, width + GROUP, width), room],
        20 * unit_flops,
    )
    p_other = other_core(p_mine)
    source = after(sources[0], p_mine)
    rhs = [source, swap(source, 1), swap(source, 2), swap(source, 3)]
    i2, y10, y12, y32, y3i, yo, yi, goi, gio, mo, mi, mi_half = call(
        reduce_kernel,
        [flags, bonds, p_mine, p_other],
        [square] * 11 + [panel],
        [room, room],
        30 * unit_flops,
    )
    first = [(groups - 1, groups - 2)]
    into_o = send(mi_half, first)
    w, ao, ai, ro, ri = call(
        columns_kernel,
        [flags, *rhs, p_mine, p_other, i2, y10, y12, y32, y3i, yo, yi],
        [block, square, square, block, block],
        [(MEMBERS, width, modes)],
        flops=6 * unit_flops,
    )
    ro_in = send(ri, first)
    into_o = after(into_o, ro)
    steps = []
    for t in range(middle - 1):
        new_half, si, y = call(
            functools.partial(chain_kernel, (t, groups - 2 - t)),
            [flags, goi, gio, mo, mi, into_o, other_core(into_o)],
            [panel, square, square],
            [room],
            20 * unit_flops,
        )
        upward = [(t, t + 1)]
        downward = [(groups - 2 - t, groups - 3 - t)]
        from_left, from_right = send(new_half, upward), send(new_half, downward)
        new_ri, vo = call(
            chain_columns_kernel, [y, si, ro, ro_in, ri], [block] * 2, flops=unit_flops
        )
        steps.append((y, vo))
        rhs_left, rhs_right = send(new_ri, upward), send(new_ri, downward)
        from_left, from_right = after(from_left, vo), after(from_right, vo)
        if groups - 3 - t >= middle:
            into_o = from_left + from_right
            ro_in = rhs_left + rhs_right
        else:
            into_o, into_i = from_left, from_right
            ro_in, ri_in = rhs_left, rhs_right
    inv_i, y, left = call(
        functools.partial(root_first_kernel, middle - 1),
        [flags, goi, gio, mo, mi, into_o, other_core(into_o), into_i, other_core(into_i)],
        [square] * 3,
        [room],
        20 * unit_flops,
    )
    last_y, last_vo = (send(after(part, inv_i), [(groups - 2, groups - 1)]) for part in steps[0])
    xo, xi = call(
        functools.partial(root_last_kernel, middle - 1),
        [flags, inv_i, y, left, ro, ro_in, ri, ri_in],
        [block] * 2,
        [room, block, block],
        20 * unit_flops,
    )
    for t in reversed(range(1, middle - 1)):
        y, vo = steps[t]
        from_right = send(xo, [(t + 1, t)])
        from_left = send(jnp.where(group == middle - 1, xi, xo), [(groups - 3 - t, groups - 2 - t)])
        on_left = group == t
        on_right = group == groups - 2 - t
        xi = jnp.where(on_left, from_right, jnp.where(on_right, from_left, xi))
        (outer,) = call(chain_back_kernel, [vo, y, xi], [block], flops=unit_flops)
        xo = jnp.where(on_left | on_right, outer, xo)
    outward = xi if middle - 1 == groups - 3 else xo
    in_a = send(xo, [(1, 0)])
    in_b = send(outward, [(groups - 3, groups - 2)])
    in_c = send(outward, [(groups - 3, groups - 1)])
    y, vo = steps[0]
    (out,) = call(
        final_kernel,
        [flags, w, ao, ai, y, vo, last_y, last_vo, xo, xi, in_a, in_b, in_c],
        [block],
        flops=2 * unit_flops,
    )
    return out[None]


def solution(mesh):
    groups = mesh.shape["slab"] // MEMBERS
    fine = Mesh(
        mesh.devices.reshape(groups, MEMBERS, mesh.shape["col"]), ("group", "member", "col")
    )
    slab = ("group", "member")
    placed = (
        P(slab, None, "col"),
        P(slab, None, "col"),
        P(slab, "col"),
        P(slab, None, "col"),
    )
    return jax.shard_map(
        on_device, mesh=fine, in_specs=placed, out_specs=P(slab, None, "col"), check_vma=False
    )
```

```python
import functools
import math

import jax
import jax.numpy as jnp
from jax import lax
from jax.experimental import pallas as pl
from jax.experimental.pallas import tpu as pltpu
from jax.sharding import Mesh
from jax.sharding import PartitionSpec as P

MEMBERS = 4
SPARE_BYTES = 16 * 1024 * 1024

LEAF = 128
PANEL = 32
GROUP = 8


def split(x):
    high = x.astype(jnp.bfloat16)
    low = (x - high.astype(jnp.float32)).astype(jnp.bfloat16)
    return high, low


def dot_split(a, b):
    (ah, al), (bh, bl) = a, b
    mul = functools.partial(jnp.dot, preferred_element_type=jnp.float32)
    return mul(ah, bh) + (mul(ah, bl) + mul(al, bh))


def dot3(a, b):
    return dot_split(split(a), split(b))


def dot_down(a, b):
    (ah, al), (bh, bl) = split(a), split(b)
    mul = functools.partial(
        lax.dot_general,
        dimension_numbers=(((0,), (0,)), ((), ())),
        preferred_element_type=jnp.float32,
    )
    return mul(ah, bh) + (mul(ah, bl) + mul(al, bh))


def reciprocal(x):
    guess = pl.reciprocal(x, approx=True)
    return guess * (2.0 - x * guess)


def leaf_reduce(block, room, background=()):
    shape = (GROUP, LEAF)
    lane = lax.broadcasted_iota(jnp.int32, shape, 1)
    sub = lax.broadcasted_iota(jnp.int32, shape, 0)
    background = list(background)
    room[0] = block

    def row_of(v, p):
        return jnp.broadcast_to(v[p : p + 1, :], shape)

    def col_of(v, c):
        return jnp.broadcast_to(v[:, c : c + 1], shape)

    def rows_at(i):
        return slice(GROUP * i, GROUP * (i + 1))

    def eliminate(k, order):
        base = GROUP * k
        v = room[0, rows_at(k), :]
        cols = [col_of(v, base + p) for p in range(GROUP)]
        for p in range(GROUP):
            here = sub == p
            inv = reciprocal(row_of(cols[p], p))
            for q in range(p + 1, GROUP):
                entry = row_of(cols[q], p) * inv
                cols[q] = jnp.where(here, entry, cols[q] - cols[p] * entry)
            v = jnp.where(lane == base + p, jnp.where(here, 1.0, 0.0), v)
            scaled = row_of(v, p) * inv
            v = jnp.where(here, scaled, v - cols[p] * scaled)
        room[0, rows_at(k), :] = v
        inside = (lane >= base) & (lane < base + GROUP)
        pivots = [row_of(v, p) for p in range(GROUP)]
        for i in order:
            w = room[0, rows_at(i), :]
            terms = [col_of(w, base + p) * pivots[p] for p in range(GROUP)]
            while len(terms) > 1:
                terms = [x + y for x, y in zip(terms[::2], terms[1::2])]
            room[0, rows_at(i), :] = jnp.where(inside, 0.0, w) - terms[0]

    per = PANEL // GROUP
    panels = LEAF // PANEL
    wide_lane = lax.broadcasted_iota(jnp.int32, (PANEL, LEAF), 1)
    wide_sub = lax.broadcasted_iota(jnp.int32, (PANEL, LEAF), 0)
    for j in range(panels):
        top = PANEL * j
        here = slice(top, top + PANEL)
        start = jnp.where(wide_lane < top, room[0, here, :], 0.0)
        room[1, here, :] = start + jnp.where(wide_lane == wide_sub + top, 1.0, 0.0)
        panel = list(range(per * j, per * (j + 1)))
        lazy = 2 * (j + 2) <= panels
        eager = list(range(per * (j + 1), per * (j + 2 if lazy else panels)))
        for k in panel:
            eliminate(k, [i for i in panel if i > k] + [i for i in panel if i < k] + eager)
        room[2, here, :] = jnp.where(wide_lane < top + PANEL, room[0, here, :], 0.0)
        if lazy:
            below = slice(top + 2 * PANEL, LEAF)
            depth = LEAF - top - 2 * PANEL
            lanes = lax.broadcasted_iota(jnp.int32, (depth, LEAF), 1)
            inside = (lanes >= top) & (lanes < top + PANEL)
            w = room[0, below, :]
            parts = [room[0, here, :]]
            if top:
                parts = [jnp.zeros((top, LEAF), jnp.float32)] + parts
            parts.append(jnp.zeros((LEAF - top - PANEL, LEAF), jnp.float32))
            product = dot3(jnp.where(inside, w, 0.0), jnp.concatenate(parts, axis=0))
            room[0, below, :] = jnp.where(inside, 0.0, w) - product
        share = -(-len(background) // (panels - j))
        for part in background[:share]:
            part()
        background = background[share:]


def inverse_in(ref, room, background=()):
    n = ref.shape[-1]
    steps = n // LEAF
    rest = n - LEAF

    def update(src, dst, leaf):
        ls = split(leaf)
        cs = [split(ref[src, LEAF * r : LEAF * (r + 1), :LEAF]) for r in range(1, steps)]
        q = dot_split(ls, split(ref[src, :LEAF, LEAF : 2 * LEAF]))
        qs = [split(q)]
        pivot = ref[src, LEAF : 2 * LEAF, LEAF : 2 * LEAF] - dot_split(cs[0], qs[0])

        def prepare():
            wide = dot_split(ls, split(ref[src, :LEAF, 2 * LEAF :]))
            ref[dst, rest:, :LEAF] = q
            ref[dst, rest:, LEAF:rest] = wide
            ref[dst, rest:, rest:] = leaf
            ref[dst, :LEAF, :LEAF] = pivot
            whole_q = jnp.concatenate([q, wide], axis=1)
            qs[0] = split(whole_q)

        def strip(r):
            def run():
                rows = slice(LEAF * r, LEAF * (r + 1))
                out = slice(LEAF * (r - 1), LEAF * r)
                new = ref[src, rows, LEAF:] - dot_split(cs[r - 1], qs[0])
                if r == 1:
                    ref[dst, out, LEAF:rest] = new[:, LEAF:]
                else:
                    ref[dst, out, :rest] = new
                ref[dst, out, rest:] = -dot_split(cs[r - 1], ls)

            return run

        return pivot, [prepare] + [strip(r) for r in range(1, steps)]

    def leaf():
        return dot3(room[1].T, room[2])

    def body(step, carry):
        src = lax.rem(step, 2)
        pivot, parts = update(src, 1 - src, leaf())
        leaf_reduce(pivot, room, parts)
        return carry

    leaf_reduce(ref[0, :LEAF, :LEAF], room, background)
    lax.fori_loop(0, steps - 1, body, 0)
    for part in update((steps - 1) % 2, steps % 2, leaf())[1]:
        part()


def plus_diagonal(matrix, row):
    shape = matrix.shape
    here = lax.broadcasted_iota(jnp.int32, shape, 0) == lax.broadcasted_iota(jnp.int32, shape, 1)
    return matrix + jnp.where(here, jnp.broadcast_to(row, shape), 0.0)


RIGHT, LAST, COL, MEMBER, SETTLED, PLANE = range(6)


def panel_kernel(pattern, coupling, mass, panel):
    width, half = coupling.shape
    tile_w = width // (width // LEAF)
    first = lax.axis_index("col") * half
    rows = lax.broadcasted_iota(jnp.int32, (LEAF, LEAF), 0)
    columns = lax.broadcasted_iota(jnp.int32, (LEAF, LEAF), 1)
    across = half // tile_w
    for r in range(width // tile_w):
        for c in range(across):
            at = (slice(tile_w * r, tile_w * (r + 1)), slice(tile_w * c, tile_w * (c + 1)))
            unit = (rows + tile_w * r == columns + (first + tile_w * c)).astype(jnp.float32)
            panel[at] = unit + pattern[across * r + c].astype(jnp.float32) * coupling[at]
    panel[width:, :] = jnp.broadcast_to(mass[...], (GROUP, half))


def place_bonds(flags, pieces, bonds):
    half = bonds.shape[-1] // 2
    me = flags[MEMBER]
    for source in range(2):
        core = flags[COL] if source == 0 else 1 - flags[COL]
        columns = pl.ds(pl.multiple_of(core * half, half), half)
        own, by_x, by_y, top, bottom = pieces[5 * source : 5 * source + 5]
        for rel, piece in enumerate((own, by_x, by_y)):
            bonds[me ^ rel, :, columns] = piece[...]
        bonds[me ^ 3, :half, columns] = top[...]
        bonds[me ^ 3, half:, columns] = bottom[...]


def first_kernel(flags, *refs):
    pieces = refs[:10]
    bonds, inverse, placed, work, room = refs[10:]
    width = inverse.shape[0]
    right = flags[RIGHT]
    place_bonds(flags, pieces, placed)
    for k in range(MEMBERS):
        at = jnp.where(right == 1, MEMBERS - 1 - k, k)
        bonds[k, :width, :] = placed[at, :width, :]
        at = jnp.where((right == 1) & (k > 0), MEMBERS - k, k)
        bonds[k, width:, :] = placed[at, width:, :]
    side = 2 * flags[COL]
    work[0] = plus_diagonal(
        bonds[side, :width, :] + bonds[side + 1, :width, :], bonds[side + 1, width : width + 1, :]
    )
    inverse_in(work, room)
    inverse[...] = work[0]


def sides(flags, mine, other):
    first = flags[COL] == 0
    a, b = mine[...], other[...]
    return jnp.where(first, a, b), jnp.where(first, b, a)


def reduce_kernel(
    flags, bonds, mine, other, i2, y10, y12, y32, y3i, yo, yi, goi, gio, mo, mi, mi_half, work_a, work_b, room
):
    width = i2.shape[0]

    def bond(k):
        return bonds[k, :width, :]

    def mass(k):
        return bonds[k, width : width + 1, :]

    right = flags[RIGHT]
    m1, m2, m3 = mass(1), mass(2), mass(3)
    c0, c1, c2, c3 = (split(bond(k)) for k in range(MEMBERS))
    p1, p3 = sides(flags, mine, other)
    q1, q3 = split(p1), split(p3)
    y12[...] = dot_split(c1, q1)
    y32[...] = dot_split(c2, q3)
    to_o = dot_split(split(y12[...]), c0)
    to_i = dot_split(split(y32[...]), c3)
    mass2 = plus_diagonal(y12[...] * m1 + y32[...] * m3, m2)
    work_a[0] = to_o + to_i + mass2

    def ends_i():
        y3i[...] = dot_split(c3, q3)

    def ends_o():
        y10[...] = dot_split(c0, q1)

    def from_i():
        work_b[0] = dot_split(split(y3i[...]), c2)

    def from_o():
        work_b[1] = dot_split(split(y10[...]), c1)

    inverse_in(work_a, room, [ends_i, ends_o, from_i, from_o])
    i2[...] = work_a[0]
    q2 = split(i2[...])
    sm = split(mass2)
    m0 = mass(0)
    left_on = jnp.where(right == 1, 0.0, 1.0)
    yi[...] = dot_split(split(work_b[0]), q2)
    si = split(yi[...])
    back = dot_split(si, split(to_o))
    gio[...] = back
    mi[...] = plus_diagonal(
        y3i[...] * m3 + dot_split(si, sm) + back * jnp.where(flags[LAST] == 1, 1.0, 0.0),
        m0 * (1.0 - left_on),
    )
    keep_half(flags, mi, mi_half)

    @pl.when(flags[LAST] == 0)
    def _():
        yo[...] = dot_split(split(work_b[1]), q2)
        so = split(yo[...])
        goi[...] = dot_split(so, split(to_i))
        mo[...] = plus_diagonal(y10[...] * m1 + dot_split(so, sm), m0 * left_on)

    @pl.when(flags[LAST] == 1)
    def _():
        yo[...] = jnp.zeros_like(yo)


def keep_half(flags, full, half_ref):
    half = half_ref.shape[1]
    half_ref[...] = jnp.where(flags[COL] == 0, full[:, :half], full[:, half:])


def whole(flags, mine, other):
    first = flags[COL] == 0
    a, b = mine[...], other[...]
    return jnp.concatenate([jnp.where(first, a, b), jnp.where(first, b, a)], axis=1)


def chain_kernel(planes, flags, goi, gio, mo, mi, mine, other, new_half, si, y, work, room):
    @pl.when((flags[PLANE] == planes[0]) | (flags[PLANE] == planes[1]))
    def _():
        mass_o = mo[...] + whole(flags, mine, other)
        work[0] = goi[...] + mass_o
        inverse_in(work, room)
        si[...] = work[0]
        y[...] = dot3(gio[...], si[...])
        work[0] = mi[...] + dot3(y[...], mass_o)
        keep_half(flags, work.at[0], new_half)


def root_first_kernel(
    root, flags, goi, gio, mo, mi, o_mine, o_other, i_mine, i_other, inv_i, y, left, work, room
):
    @pl.when(flags[PLANE] == root)
    def _():
        mass_i = mi[...] + whole(flags, i_mine, i_other)
        work[0] = gio[...] + mass_i
        inverse_in(work, room)
        inv_i[...] = work[0]
        y[...] = dot3(goi[...], inv_i[...])
        mass_o = mo[...] + whole(flags, o_mine, o_other)
        left[...] = mass_o + dot3(y[...], mass_i)


def root_last_kernel(
    root, flags, inv_i, y, left, ro, ro_in, ri, ri_in, xo, xi, work, room, inner, outer
):
    @pl.when(flags[PLANE] == root)
    def _():
        work[0] = left[...]

        def columns():
            s = split(ri[...] + ri_in[...])
            inner[...] = dot_split(split(inv_i[...]), s)
            outer[...] = ro[...] + ro_in[...] + dot_split(split(y[...]), s)

        inverse_in(work, room, [columns])
        xo[...] = dot3(work[0], outer[...])
        xi[...] = inner[...] + dot_down(y[...], xo[...])


def columns_kernel(
    flags, own, by_x, by_y, by_xy, p_mine, p_other, i2, y10, y12, y32, y3i, yo, yi, w, ao, ai, ro, ri, rhs
):
    right = flags[RIGHT]
    member = flags[MEMBER]
    for rel, piece in enumerate((own, by_x, by_y, by_xy)):
        rhs[member ^ rel] = piece[...]
    r0 = rhs[0]
    r2 = rhs[2]
    r1 = rhs[jnp.where(right == 1, 3, 1)]
    r3 = rhs[jnp.where(right == 1, 1, 3)]
    s1, s3 = split(r1), split(r3)
    p1, p3 = sides(flags, p_mine, p_other)
    v1 = dot_split(split(p1), s1)
    v3 = dot_split(split(p3), s3)
    r2 = r2 + dot_split(split(y12[...]), s1) + dot_split(split(y32[...]), s3)
    s2 = split(r2)
    v2 = dot_split(split(i2[...]), s2)
    left_on = jnp.where(right == 1, 0.0, 1.0)
    yos, yis = split(yo[...]), split(yi[...])
    ro[...] = r0 * left_on + dot_split(split(y10[...]), s1) + dot_split(yos, s2)
    ri[...] = r0 * (1.0 - left_on) + dot_split(split(y3i[...]), s3) + dot_split(yis, s2)
    is_2 = member == 2
    is_1 = member == jnp.where(right == 1, 3, 1)
    z = jnp.where(is_1, y12[...], y32[...])
    zs = split(z)
    w[...] = jnp.where(is_2, v2, jnp.where(is_1, v1, v3) + dot_down(z, v2))
    ao[...] = jnp.where(is_2, yo[...], dot_split(yos, zs) + jnp.where(is_1, y10[...], 0.0))
    ai[...] = jnp.where(is_2, yi[...], dot_split(yis, zs) + jnp.where(is_1, 0.0, y3i[...]))


def chain_columns_kernel(y, si, ro, ro_in, ri, new_ri, vo):
    s = split(ro[...] + ro_in[...])
    new_ri[...] = ri[...] + dot_split(split(y[...]), s)
    vo[...] = dot_split(split(si[...]), s)


def chain_back_kernel(vo, y, xi, xo):
    xo[...] = vo[...] + dot_down(y[...], xi[...])


def final_kernel(flags, w, ao, ai, y, vo, last_y, last_vo, xo, xi, in_a, in_b, in_c, out):
    last = flags[LAST] == 1
    settled = flags[SETTLED] == 1
    came = in_a[...] + in_b[...] + in_c[...]
    end = jnp.where(last, last_vo[...], vo[...]) + dot_down(
        jnp.where(last, last_y[...], y[...]), came
    )
    end_o = jnp.where(settled, xo[...], jnp.where(last, 0.0, end))
    end_i = jnp.where(settled, xi[...], jnp.where(last, end, came))
    mine = w[...] + dot_down(ao[...], end_o) + dot_down(ai[...], end_i)
    here = jnp.where(flags[RIGHT] == 1, end_i, end_o)
    out[...] = jnp.where(flags[MEMBER] == 0, here, mine)


def call(kernel, args, outs, scratch=(), flops=0):
    def spec(a):
        space = pltpu.SMEM if a.dtype == jnp.int32 else pltpu.VMEM
        return pl.BlockSpec(memory_space=space)

    moved = sum(a.size * 4 for a in args) + sum(4 * math.prod(s) for s in outs)
    held = moved + sum(4 * math.prod(s) for s in scratch)
    return pl.pallas_call(
        kernel,
        out_shape=[jax.ShapeDtypeStruct(s, jnp.float32) for s in outs],
        in_specs=[spec(a) for a in args],
        out_specs=[pl.BlockSpec(memory_space=pltpu.VMEM) for _ in outs],
        scratch_shapes=[pltpu.VMEM(s, jnp.float32) for s in scratch],
        cost_estimate=pl.CostEstimate(flops=flops, bytes_accessed=moved, transcendentals=0),
        compiler_params=pltpu.CompilerParams(vmem_limit_bytes=held + SPARE_BYTES),
    )(*args)


def on_device(coupling, tile_pattern, orbital_mass, sources):
    width = coupling.shape[1]
    half = coupling.shape[2]
    modes = sources.shape[2]
    column = lax.axis_index("col")
    member = lax.axis_index("member")
    group = lax.axis_index("group")
    groups = lax.axis_size("group")
    middle = groups // 2

    def send(x, pairs):
        return lax.ppermute(x, "group", pairs)

    def swap(x, bits):
        return lax.ppermute(x, "member", [(m, m ^ bits) for m in range(MEMBERS)])

    def other_core(x):
        return lax.ppermute(x, "col", [(0, 1), (1, 0)])

    def after(x, *others):
        return lax.optimization_barrier((x, *others))[0]

    (own,) = call(
        panel_kernel,
        [tile_pattern[0].reshape(-1), coupling[0], orbital_mass],
        [(width + GROUP, half)],
    )
    by_x, by_y = swap(own, 1), swap(own, 2)
    top, bottom = swap(by_x[:half], 2), swap(by_y[half:], 1)
    mine = [own, by_x, by_y, top, bottom]
    pieces = mine + [other_core(piece) for piece in mine]
    settled = flags[SETTLED] == 1
    came = in_a[...] + in_b[...] + in_c[...]
    end = jnp.where(last, last_vo[...], vo[...]) + dot_down(
        jnp.where(last, last_y[...], y[...]), came
    )
    end_o = jnp.where(settled, xo[...], jnp.where(last, 0.0, end))
    end_i = jnp.where(settled, xi[...], jnp.where(last, end, came))
    mine = w[...] + dot_down(ao[...], end_o) + dot_down(ai[...], end_i)
    here = jnp.where(flags[RIGHT] == 1, end_i, end_o)
    out[...] = jnp.where(flags[MEMBER] == 0, here, mine)


def call(kernel, args, outs, scratch=(), flops=0):
    def spec(a):
        space = pltpu.SMEM if a.dtype == jnp.int32 else pltpu.VMEM
        return pl.BlockSpec(memory_space=space)

    moved = sum(a.size * 4 for a in args) + sum(4 * math.prod(s) for s in outs)
    held = moved + sum(4 * math.prod(s) for s in scratch)
    return pl.pallas_call(
        kernel,
        out_shape=[jax.ShapeDtypeStruct(s, jnp.float32) for s in outs],
        in_specs=[spec(a) for a in args],
        out_specs=[pl.BlockSpec(memory_space=pltpu.VMEM) for _ in outs],
        scratch_shapes=[pltpu.VMEM(s, jnp.float32) for s in scratch],
        cost_estimate=pl.CostEstimate(flops=flops, bytes_accessed=moved, transcendentals=0),
        compiler_params=pltpu.CompilerParams(vmem_limit_bytes=held + SPARE_BYTES),
    )(*args)


def on_device(coupling, tile_pattern, orbital_mass, sources):
    width = coupling.shape[1]
    half = coupling.shape[2]
    modes = sources.shape[2]
    column = lax.axis_index("col")
    member = lax.axis_index("member")
    group = lax.axis_index("group")
    groups = lax.axis_size("group")
    middle = groups // 2

    def send(x, pairs):
        return lax.ppermute(x, "group", pairs)

    def swap(x, bits):
        return lax.ppermute(x, "member", [(m, m ^ bits) for m in range(MEMBERS)])

    def other_core(x):
        return lax.ppermute(x, "col", [(0, 1), (1, 0)])

    def after(x, *others):
        return lax.optimization_barrier((x, *others))[0]

    (own,) = call(
        panel_kernel,
        [tile_pattern[0].reshape(-1), coupling[0], orbital_mass],
        [(width + GROUP, half)],
    )
    by_x, by_y = swap(own, 1), swap(own, 2)
    top, bottom = swap(by_x[:half], 2), swap(by_y[half:], 1)
    mine = [own, by_x, by_y, top, bottom]
    pieces = mine + [other_core(piece) for piece in mine]
    source = after(sources[0], top, bottom)
    rhs = [source, swap(source, 1), swap(source, 2), swap(source, 3)]
    settled = (group != 0) & (group < groups - 2)
    flags = jnp.stack(
        [
            (group >= middle).astype(jnp.int32),
            (group == groups - 1).astype(jnp.int32),
            column.astype(jnp.int32),
            member.astype(jnp.int32),
            settled.astype(jnp.int32),
            group.astype(jnp.int32),
        ]
    )
    square = (width, width)
    block = (width, modes)
    panel = (width, half)
    work = (2, width, width)
    room = (3, LEAF, LEAF)
    unit_flops = 6 * width**3
    bonds, p_mine = call(
        first_kernel,
        [flags, *pieces],
        [(MEMBERS, width + GROUP, width), square],
        [(MEMBERS, width + GROUP, width), work, room],
        20 * unit_flops,
    )
    p_other = other_core(p_mine)
    source = after(sources[0], p_mine)
    rhs = [source, swap(source, 1), swap(source, 2), swap(source, 3)]
    i2, y10, y12, y32, y3i, yo, yi, goi, gio, mo, mi, mi_half = call(
        reduce_kernel,
        [flags, bonds, p_mine, p_other],
        [square] * 11 + [panel],
        [work, work, room],
        30 * unit_flops,
    )
    first = [(groups - 1, groups - 2)]
    into_o = send(mi_half, first)
    w, ao, ai, ro, ri = call(
        columns_kernel,
        [flags, *rhs, p_mine, p_other, i2, y10, y12, y32, y3i, yo, yi],
        [block, square, square, block, block],
        [(MEMBERS, width, modes)],
        flops=6 * unit_flops,
    )
    ro_in = send(ri, first)
    into_o = after(into_o, ro)
    steps = []
    for t in range(middle - 1):
        new_half, si, y = call(
            functools.partial(chain_kernel, (t, groups - 2 - t)),
            [flags, goi, gio, mo, mi, into_o, other_core(into_o)],
            [panel, square, square],
            [work, room],
            20 * unit_flops,
        )
        upward = [(t, t + 1)]
        downward = [(groups - 2 - t, groups - 3 - t)]
        from_left, from_right = send(new_half, upward), send(new_half, downward)
        new_ri, vo = call(
            chain_columns_kernel, [y, si, ro, ro_in, ri], [block] * 2, flops=unit_flops
        )
        steps.append((y, vo))
        rhs_left, rhs_right = send(new_ri, upward), send(new_ri, downward)
        from_left, from_right = after(from_left, vo), after(from_right, vo)
        if groups - 3 - t >= middle:
            into_o = from_left + from_right
            ro_in = rhs_left + rhs_right
        else:
            into_o, into_i = from_left, from_right
            ro_in, ri_in = rhs_left, rhs_right
    inv_i, y, left = call(
        functools.partial(root_first_kernel, middle - 1),
        [flags, goi, gio, mo, mi, into_o, other_core(into_o), into_i, other_core(into_i)],
        [square] * 3,
        [work, room],
        20 * unit_flops,
    )
    last_y, last_vo = (send(after(part, inv_i), [(groups - 2, groups - 1)]) for part in steps[0])
    xo, xi = call(
        functools.partial(root_last_kernel, middle - 1),
        [flags, inv_i, y, left, ro, ro_in, ri, ri_in],
        [block] * 2,
        [work, room, block, block],
        20 * unit_flops,
    )
    for t in reversed(range(1, middle - 1)):
        y, vo = steps[t]
        from_right = send(xo, [(t + 1, t)])
        from_left = send(jnp.where(group == middle - 1, xi, xo), [(groups - 3 - t, groups - 2 - t)])
        on_left = group == t
        on_right = group == groups - 2 - t
        xi = jnp.where(on_left, from_right, jnp.where(on_right, from_left, xi))
        (outer,) = call(chain_back_kernel, [vo, y, xi], [block], flops=unit_flops)
        xo = jnp.where(on_left | on_right, outer, xo)
    outward = xi if middle - 1 == groups - 3 else xo
    in_a = send(xo, [(1, 0)])
    in_b = send(outward, [(groups - 3, groups - 2)])
    in_c = send(outward, [(groups - 3, groups - 1)])
    y, vo = steps[0]
    (out,) = call(
        final_kernel,
        [flags, w, ao, ai, y, vo, last_y, last_vo, xo, xi, in_a, in_b, in_c],
        [block],
        flops=2 * unit_flops,
    )
    return out[None]


def solution(mesh):
    groups = mesh.shape["slab"] // MEMBERS
    fine = Mesh(
        mesh.devices.reshape(groups, MEMBERS, mesh.shape["col"]), ("group", "member", "col")
    )
    slab = ("group", "member")
    placed = (
        P(slab, None, "col"),
        P(slab, None, "col"),
        P(slab, "col"),
        P(slab, None, "col"),
    )
    return jax.shard_map(
        on_device, mesh=fine, in_specs=placed, out_specs=P(slab, None, "col"), check_vma=False
    )
```

```python
import functools
import math

import jax
import jax.numpy as jnp
from jax import lax
from jax.experimental import pallas as pl
from jax.experimental.pallas import tpu as pltpu
from jax.sharding import Mesh
from jax.sharding import PartitionSpec as P

MEMBERS = 4
SPARE_BYTES = 16 * 1024 * 1024
LEAF = 128
PANEL = 32
GROUP = 8


def split(x):
    high = x.astype(jnp.bfloat16)
    low = (x - high.astype(jnp.float32)).astype(jnp.bfloat16)
    return high, low


def dot_split(a, b):
    (ah, al), (bh, bl) = a, b
    mul = functools.partial(jnp.dot, preferred_element_type=jnp.float32)
    return mul(ah, bh) + (mul(ah, bl) + mul(al, bh))


def dot3(a, b):
    return dot_split(split(a), split(b))


def reciprocal(x):
    guess = pl.reciprocal(x, approx=True)
    return guess * (2.0 - x * guess)


def leaf_inverse(blocks, background=()):
    shape = (GROUP, LEAF)
    lane = lax.broadcasted_iota(jnp.int32, shape, 1)
    sub = lax.broadcasted_iota(jnp.int32, shape, 0)
    count = LEAF // GROUP
    sets = [[b[GROUP * i : GROUP * (i + 1), :] for i in range(count)] for b in blocks]
    background = list(background)

    def row_of(v, p):
        return jnp.broadcast_to(v[p : p + 1, :], shape)

    def col_of(v, c):
        return jnp.broadcast_to(v[:, c : c + 1], shape)

    def eliminate(k, order):
        base = GROUP * k
        vs = [rows[k] for rows in sets]
        cols = [[col_of(v, base + p) for p in range(GROUP)] for v in vs]
        for p in range(GROUP):
            here = sub == p
            unit = jnp.where(here, 1.0, 0.0)
            invs = [reciprocal(row_of(c[p], p)) for c in cols]
            for q in range(p + 1, GROUP):
                for c, inv in zip(cols, invs):
                    entry = row_of(c[q], p) * inv
                    c[q] = jnp.where(here, entry, c[q] - c[p] * entry)
            for at, (c, inv) in enumerate(zip(cols, invs)):
                v = jnp.where(lane == base + p, unit, vs[at])
                scaled = row_of(v, p) * inv
                vs[at] = jnp.where(here, scaled, v - c[p] * scaled)
        inside = (lane >= base) & (lane < base + GROUP)
        pivots = [[row_of(v, p) for p in range(GROUP)] for v in vs]
        for rows, v in zip(sets, vs):
            rows[k] = v
        for i in order:
            for rows, pivot in zip(sets, pivots):
                w = rows[i]
                terms = [col_of(w, base + p) * pivot[p] for p in range(GROUP)]
                while len(terms) > 1:
                    terms = [x + y for x, y in zip(terms[::2], terms[1::2])]
                rows[i] = jnp.where(inside, 0.0, w) - terms[0]

    per = PANEL // GROUP
    panels = count // per
    for j in range(panels):
        panel = list(range(per * j, per * (j + 1)))
        if j + 1 < panels:
            eager = list(range(per * (j + 1), per * (j + 2)))
        else:
            eager = list(range(per * j))
        others = [i for i in range(count) if i not in panel and i not in eager]
        for k in panel:
            eliminate(k, [i for i in panel if i > k] + [i for i in panel if i < k] + eager)
        inside = (lane >= PANEL * j) & (lane < PANEL * (j + 1))
        zeros = jnp.zeros(shape, jnp.float32)
        if others:
            for rows in sets:
                left = jnp.concatenate([jnp.where(inside, rows[i], 0.0) for i in others], axis=0)
                pivot = jnp.concatenate(
                    [rows[i] if i in panel else zeros for i in range(count)], axis=0
                )
                product = dot3(left, pivot)
                for at, i in enumerate(others):
                    kept = jnp.where(inside, 0.0, rows[i])
                    rows[i] = kept - product[GROUP * at : GROUP * (at + 1), :]
        share = -(-len(background) // (panels - j))
        for part in background[:share]:
            part()
        background = background[share:]
    return [jnp.concatenate(rows, axis=0) for rows in sets]


def inverse_in(work_refs, background=()):
    n = work_refs[0].shape[-1]
    steps = n // LEAF
    rest = n - LEAF

    def update(ref, src, dst, leaf):
        ls = split(leaf)
        cs = [split(ref[src, LEAF * r : LEAF * (r + 1), :LEAF]) for r in range(1, steps)]
        q = dot_split(ls, split(ref[src, :LEAF, LEAF : 2 * LEAF]))
        qs = [split(q)]
        pivot = ref[src, LEAF : 2 * LEAF, LEAF : 2 * LEAF] - dot_split(cs[0], qs[0])

        def prepare():
            wide = dot_split(ls, split(ref[src, :LEAF, 2 * LEAF :]))
            ref[dst, rest:, :LEAF] = q
            ref[dst, rest:, LEAF:rest] = wide
            ref[dst, rest:, rest:] = leaf
            ref[dst, :LEAF, :LEAF] = pivot
            whole_q = jnp.concatenate([q, wide], axis=1)
            qs[0] = split(whole_q)

        def strip(r):
            def run():
                rows = slice(LEAF * r, LEAF * (r + 1))
                out = slice(LEAF * (r - 1), LEAF * r)
                new = ref[src, rows, LEAF:] - dot_split(cs[r - 1], qs[0])
                if r == 1:
                    ref[dst, out, LEAF:rest] = new[:, LEAF:]
                else:
                    ref[dst, out, :rest] = new
                ref[dst, out, rest:] = -dot_split(cs[r - 1], ls)

            return run

        return pivot, [prepare] + [strip(r) for r in range(1, steps)]

    def body(step, leaves):
        src = lax.rem(step, 2)
        pivots, parts = [], []
        for ref, leaf in zip(work_refs, leaves):
            pivot, own = update(ref, src, 1 - src, leaf)
            pivots.append(pivot)
            parts.append(own)
        return tuple(leaf_inverse(pivots, [part for group in zip(*parts) for part in group]))

    leaves = tuple(leaf_inverse([ref[0, :LEAF, :LEAF] for ref in work_refs], background))
    leaves = lax.fori_loop(0, steps - 1, body, leaves)
    for ref, leaf in zip(work_refs, leaves):
        for part in update(ref, (steps - 1) % 2, steps % 2, leaf)[1]:
            part()


def plus_diagonal(matrix, row):
    shape = matrix.shape
    here = lax.broadcasted_iota(jnp.int32, shape, 0) == lax.broadcasted_iota(jnp.int32, shape, 1)
    return matrix + jnp.where(here, jnp.broadcast_to(row, shape), 0.0)


def dot_down(a, b):
    (ah, al), (bh, bl) = split(a), split(b)
    mul = functools.partial(
        lax.dot_general,
        dimension_numbers=(((0,), (0,)), ((), ())),
        preferred_element_type=jnp.float32,
    )
    return mul(ah, bh) + (mul(ah, bl) + mul(al, bh))


RIGHT, LAST, COL, MEMBER, SETTLED, PLANE = range(6)


def panel_kernel(pattern, coupling, mass, panel):
    width, half = coupling.shape
    tile_w = width // (width // LEAF)
    first = lax.axis_index("col") * half
    rows = lax.broadcasted_iota(jnp.int32, (LEAF, LEAF), 0)
    columns = lax.broadcasted_iota(jnp.int32, (LEAF, LEAF), 1)
    across = half // tile_w
    for r in range(width // tile_w):
        for c in range(across):
            at = (slice(tile_w * r, tile_w * (r + 1)), slice(tile_w * c, tile_w * (c + 1)))
            unit = (rows + tile_w * r == columns + (first + tile_w * c)).astype(jnp.float32)
            panel[at] = unit + pattern[across * r + c].astype(jnp.float32) * coupling[at]
    panel[width:, :] = jnp.broadcast_to(mass[...], (GROUP, half))


def place_bonds(flags, pieces, bonds):
    half = bonds.shape[-1] // 2
    me = flags[MEMBER]
    for source in range(2):
        core = flags[COL] if source == 0 else 1 - flags[COL]
        columns = pl.ds(pl.multiple_of(core * half, half), half)
        own, by_x, by_y, top, bottom = pieces[5 * source : 5 * source + 5]
        for rel, piece in enumerate((own, by_x, by_y)):
            bonds[me ^ rel, :, columns] = piece[...]
        bonds[me ^ 3, :half, columns] = top[...]
        bonds[me ^ 3, half:, columns] = bottom[...]


def first_kernel(flags, *refs):
    pieces = refs[:10]
    bonds, inverse, placed, work = refs[10:]
    width = inverse.shape[0]
    right = flags[RIGHT]
    place_bonds(flags, pieces, placed)
    for k in range(MEMBERS):
        at = jnp.where(right == 1, MEMBERS - 1 - k, k)
        bonds[k, :width, :] = placed[at, :width, :]
        at = jnp.where((right == 1) & (k > 0), MEMBERS - k, k)
        bonds[k, width:, :] = placed[at, width:, :]
    side = 2 * flags[COL]
    work[0] = plus_diagonal(
        bonds[side, :width, :] + bonds[side + 1, :width, :], bonds[side + 1, width : width + 1, :]
    )
    inverse_in([work])
    inverse[...] = work[0]


def sides(flags, mine, other):
    first = flags[COL] == 0
    a, b = mine[...], other[...]
    return jnp.where(first, a, b), jnp.where(first, b, a)


def reduce_kernel(
    flags, bonds, mine, other, i2, y10, y12, y32, y3i, yo, yi, goi, gio, mo, mi, mi_half, work_a, work_b
):
    width = i2.shape[0]

    def bond(k):
        return bonds[k, :width, :]

    def mass(k):
        return bonds[k, width : width + 1, :]

    right = flags[RIGHT]
    m1, m2, m3 = mass(1), mass(2), mass(3)
    c0, c1, c2, c3 = (split(bond(k)) for k in range(MEMBERS))
    p1, p3 = sides(flags, mine, other)
    q1, q3 = split(p1), split(p3)
    y12[...] = dot_split(c1, q1)
    y32[...] = dot_split(c2, q3)
    to_o = dot_split(split(y12[...]), c0)
    to_i = dot_split(split(y32[...]), c3)
    mass2 = plus_diagonal(y12[...] * m1 + y32[...] * m3, m2)
    work_a[0] = to_o + to_i + mass2

    def ends_i():
        y3i[...] = dot_split(c3, q3)

    def ends_o():
        y10[...] = dot_split(c0, q1)

    def from_i():
        work_b[0] = dot_split(split(y3i[...]), c2)

    def from_o():
        work_b[1] = dot_split(split(y10[...]), c1)

    inverse_in([work_a], [ends_i, ends_o, from_i, from_o])
    i2[...] = work_a[0]
    q2 = split(i2[...])
    sm = split(mass2)
    m0 = mass(0)
    left_on = jnp.where(right == 1, 0.0, 1.0)
    yi[...] = dot_split(split(work_b[0]), q2)
    si = split(yi[...])
    back = dot_split(si, split(to_o))
    gio[...] = back
    mi[...] = plus_diagonal(
        y3i[...] * m3 + dot_split(si, sm) + back * jnp.where(flags[LAST] == 1, 1.0, 0.0),
        m0 * (1.0 - left_on),
    )
    pack_half(flags, mi, mi_half)

    @pl.when(flags[LAST] == 0)
    def _():
        yo[...] = dot_split(split(work_b[1]), q2)
        so = split(yo[...])
        goi[...] = dot_split(so, split(to_i))
        mo[...] = plus_diagonal(y10[...] * m1 + dot_split(so, sm), m0 * left_on)

    @pl.when(flags[LAST] == 1)
    def _():
        yo[...] = jnp.zeros_like(yo)


def pack_half(flags, full, packed):
    half = packed.shape[1]
    middle = half + half // 2
    first = flags[COL] == 0
    packed[:half, :] = jnp.where(first, full[:half, :half], full[half:, half:])
    packed[half:, :] = jnp.where(first, full[half:middle, :half], full[middle:, :half])


def whole(flags, mine, other):
    half = mine.shape[1]
    first = flags[COL] == 0
    a, b = mine[...], other[...]
    low, high = jnp.where(first, a, b), jnp.where(first, b, a)
    corner = jnp.concatenate([low[half:], high[half:]], axis=0)
    return jnp.concatenate(
        [
            jnp.concatenate([low[:half], corner.T], axis=1),
            jnp.concatenate([corner, high[:half]], axis=1),
        ],
        axis=0,
    )


def chain_kernel(planes, flags, goi, gio, mo, mi, mine, other, new_half, si, y, work):
    @pl.when((flags[PLANE] == planes[0]) | (flags[PLANE] == planes[1]))
    def _():
        mass_o = mo[...] + whole(flags, mine, other)
        work[0] = goi[...] + mass_o
        inverse_in([work])
        si[...] = work[0]
        y[...] = dot3(gio[...], si[...])
        work[0] = mi[...] + dot3(y[...], mass_o)
        pack_half(flags, work.at[0], new_half)


def root_first_kernel(
    root, flags, goi, gio, mo, mi, o_mine, o_other, i_mine, i_other, inv_i, y, left, work
):
    @pl.when(flags[PLANE] == root)
    def _():
        mass_i = mi[...] + whole(flags, i_mine, i_other)
        work[0] = gio[...] + mass_i
        inverse_in([work])
        inv_i[...] = work[0]
        y[...] = dot3(goi[...], inv_i[...])
        mass_o = mo[...] + whole(flags, o_mine, o_other)
        left[...] = mass_o + dot3(y[...], mass_i)


def root_last_kernel(
    root, flags, inv_i, y, left, ro, ro_in, ri, ri_in, xo, xi, work, inner, outer
):
    @pl.when(flags[PLANE] == root)
    def _():
        work[0] = left[...]

        def columns():
            s = split(ri[...] + ri_in[...])
            inner[...] = dot_split(split(inv_i[...]), s)
            outer[...] = ro[...] + ro_in[...] + dot_split(split(y[...]), s)

        inverse_in([work], [columns])
        xo[...] = dot3(work[0], outer[...])
        xi[...] = inner[...] + dot_down(y[...], xo[...])


def columns_kernel(
    flags, own, by_x, by_y, by_xy, p_mine, p_other, i2, y10, y12, y32, y3i, yo, yi, w, ao, ai, ro, ri, rhs
):
    right = flags[RIGHT]
    member = flags[MEMBER]
    for rel, piece in enumerate((own, by_x, by_y, by_xy)):
        rhs[member ^ rel] = piece[...]
    r0 = rhs[0]
    r2 = rhs[2]
    r1 = rhs[jnp.where(right == 1, 3, 1)]
    r3 = rhs[jnp.where(right == 1, 1, 3)]
    s1, s3 = split(r1), split(r3)
    p1, p3 = sides(flags, p_mine, p_other)
    v1 = dot_split(split(p1), s1)
    v3 = dot_split(split(p3), s3)
    r2 = r2 + dot_split(split(y12[...]), s1) + dot_split(split(y32[...]), s3)
    s2 = split(r2)
    v2 = dot_split(split(i2[...]), s2)
    left_on = jnp.where(right == 1, 0.0, 1.0)
    yos, yis = split(yo[...]), split(yi[...])
    ro[...] = r0 * left_on + dot_split(split(y10[...]), s1) + dot_split(yos, s2)
    ri[...] = r0 * (1.0 - left_on) + dot_split(split(y3i[...]), s3) + dot_split(yis, s2)
    is_2 = member == 2
    is_1 = member == jnp.where(right == 1, 3, 1)
    z = jnp.where(is_1, y12[...], y32[...])
    zs = split(z)
    w[...] = jnp.where(is_2, v2, jnp.where(is_1, v1, v3) + dot_down(z, v2))
    ao[...] = jnp.where(is_2, yo[...], dot_split(yos, zs) + jnp.where(is_1, y10[...], 0.0))
    ai[...] = jnp.where(is_2, yi[...], dot_split(yis, zs) + jnp.where(is_1, 0.0, y3i[...]))


def chain_columns_kernel(y, si, ro, ro_in, ri, new_ri, vo):
    s = split(ro[...] + ro_in[...])
    new_ri[...] = ri[...] + dot_split(split(y[...]), s)
    vo[...] = dot_split(split(si[...]), s)


def chain_back_kernel(vo, y, xi, xo):
    xo[...] = vo[...] + dot_down(y[...], xi[...])


def final_kernel(flags, w, ao, ai, y, vo, last_y, last_vo, xo, xi, in_a, in_b, in_c, out):
    last = flags[LAST] == 1
    settled = flags[SETTLED] == 1
    came = in_a[...] + in_b[...] + in_c[...]
    end = jnp.where(last, last_vo[...], vo[...]) + dot_down(
        jnp.where(last, last_y[...], y[...]), came
    )
    end_o = jnp.where(settled, xo[...], jnp.where(last, 0.0, end))
    end_i = jnp.where(settled, xi[...], jnp.where(last, end, came))
    mine = w[...] + dot_down(ao[...], end_o) + dot_down(ai[...], end_i)
    here = jnp.where(flags[RIGHT] == 1, end_i, end_o)
    out[...] = jnp.where(flags[MEMBER] == 0, here, mine)


def call(kernel, args, outs, scratch=(), flops=0):
    def spec(a):
        space = pltpu.SMEM if a.dtype == jnp.int32 else pltpu.VMEM
        return pl.BlockSpec(memory_space=space)

    moved = sum(a.size * 4 for a in args) + sum(4 * math.prod(s) for s in outs)
    held = moved + sum(4 * math.prod(s) for s in scratch)
    return pl.pallas_call(
        kernel,
        out_shape=[jax.ShapeDtypeStruct(s, jnp.float32) for s in outs],
        in_specs=[spec(a) for a in args],
        out_specs=[pl.BlockSpec(memory_space=pltpu.VMEM) for _ in outs],
        scratch_shapes=[pltpu.VMEM(s, jnp.float32) for s in scratch],
        cost_estimate=pl.CostEstimate(flops=flops, bytes_accessed=moved, transcendentals=0),
        compiler_params=pltpu.CompilerParams(vmem_limit_bytes=held + SPARE_BYTES),
    )(*args)


def on_device(coupling, tile_pattern, orbital_mass, sources):
    width = coupling.shape[1]
    half = coupling.shape[2]
    modes = sources.shape[2]
    column = lax.axis_index("col")
    member = lax.axis_index("member")
    group = lax.axis_index("group")
    groups = lax.axis_size("group")
    middle = groups // 2

    def send(x, pairs):
        return lax.ppermute(x, "group", pairs)

    def swap(x, bits):
        return lax.ppermute(x, "member", [(m, m ^ bits) for m in range(MEMBERS)])

    def other_core(x):
        return lax.ppermute(x, "col", [(0, 1), (1, 0)])

    def after(x, *others):
        return lax.optimization_barrier((x, *others))[0]

    (own,) = call(
        panel_kernel,
        [tile_pattern[0].reshape(-1), coupling[0], orbital_mass],
        [(width + GROUP, half)],
    )
    by_x, by_y = swap(own, 1), swap(own, 2)
    top, bottom = swap(by_x[:half], 2), swap(by_y[half:], 1)
    mine = [own, by_x, by_y, top, bottom]
    pieces = mine + [other_core(piece) for piece in mine]
    settled = flags[SETTLED] == 1
    came = in_a[...] + in_b[...] + in_c[...]
    end = jnp.where(last, last_vo[...], vo[...]) + dot_down(
        jnp.where(last, last_y[...], y[...]), came
    )
    end_o = jnp.where(settled, xo[...], jnp.where(last, 0.0, end))
    end_i = jnp.where(settled, xi[...], jnp.where(last, end, came))
    mine = w[...] + dot_down(ao[...], end_o) + dot_down(ai[...], end_i)
    here = jnp.where(flags[RIGHT] == 1, end_i, end_o)
    out[...] = jnp.where(flags[MEMBER] == 0, here, mine)


def call(kernel, args, outs, scratch=(), flops=0):
    def spec(a):
        space = pltpu.SMEM if a.dtype == jnp.int32 else pltpu.VMEM
        return pl.BlockSpec(memory_space=space)

    moved = sum(a.size * 4 for a in args) + sum(4 * math.prod(s) for s in outs)
    held = moved + sum(4 * math.prod(s) for s in scratch)
    return pl.pallas_call(
        kernel,
        out_shape=[jax.ShapeDtypeStruct(s, jnp.float32) for s in outs],
        in_specs=[spec(a) for a in args],
        out_specs=[pl.BlockSpec(memory_space=pltpu.VMEM) for _ in outs],
        scratch_shapes=[pltpu.VMEM(s, jnp.float32) for s in scratch],
        cost_estimate=pl.CostEstimate(flops=flops, bytes_accessed=moved, transcendentals=0),
        compiler_params=pltpu.CompilerParams(vmem_limit_bytes=held + SPARE_BYTES),
    )(*args)


def on_device(coupling, tile_pattern, orbital_mass, sources):
    width = coupling.shape[1]
    half = coupling.shape[2]
    modes = sources.shape[2]
    column = lax.axis_index("col")
    member = lax.axis_index("member")
    group = lax.axis_index("group")
    groups = lax.axis_size("group")
    middle = groups // 2

    def send(x, pairs):
        return lax.ppermute(x, "group", pairs)

    def swap(x, bits):
        return lax.ppermute(x, "member", [(m, m ^ bits) for m in range(MEMBERS)])

    def other_core(x):
        return lax.ppermute(x, "col", [(0, 1), (1, 0)])

    def after(x, *others):
        return lax.optimization_barrier((x, *others))[0]

    (own,) = call(
        panel_kernel,
        [tile_pattern[0].reshape(-1), coupling[0], orbital_mass],
        [(width + GROUP, half)],
    )
    by_x, by_y = swap(own, 1), swap(own, 2)
    top, bottom = swap(by_x[:half], 2), swap(by_y[half:], 1)
    mine = [own, by_x, by_y, top, bottom]
    pieces = mine + [other_core(piece) for piece in mine]
    source = after(sources[0], top, bottom)
    rhs = [source, swap(source, 1), swap(source, 2), swap(source, 3)]
    settled = (group != 0) & (group < groups - 2)
    flags = jnp.stack(
        [
            (group >= middle).astype(jnp.int32),
            (group == groups - 1).astype(jnp.int32),
            column.astype(jnp.int32),
            member.astype(jnp.int32),
            settled.astype(jnp.int32),
            group.astype(jnp.int32),
        ]
    )
    square = (width, width)
    block = (width, modes)
    packed = (half + half // 2, half)
    room = (2, width, width)
    unit_flops = 6 * width**3
    bonds, p_mine = call(
        first_kernel,
        [flags, *pieces],
        [(MEMBERS, width + GROUP, width), square],
        [(MEMBERS, width + GROUP, width), room],
        20 * unit_flops,
    )
    p_other = other_core(p_mine)
    i2, y10, y12, y32, y3i, yo, yi, goi, gio, mo, mi, mi_half = call(
        reduce_kernel,
        [flags, bonds, p_mine, p_other],
        [square] * 11 + [packed],
        [room, room],
        30 * unit_flops,
    )
    first = [(groups - 1, groups - 2)]
    into_o = send(mi_half, first)
    source = after(sources[0], mi_half)
    rhs = [source, swap(source, 1), swap(source, 2), swap(source, 3)]
    steps = []
    for t in range(middle - 1):
        new_half, si, y = call(
            functools.partial(chain_kernel, (t, groups - 2 - t)),
            [flags, goi, gio, mo, mi, into_o, other_core(into_o)],
            [packed, square, square],
            [room],
            20 * unit_flops,
        )
        upward = [(t, t + 1)]
        downward = [(groups - 2 - t, groups - 3 - t)]
        from_left, from_right = send(new_half, upward), send(new_half, downward)
        if t == 0:
            w, ao, ai, ro, ri = call(
                columns_kernel,
                [
                    *[flags, after(rhs[0], new_half), *rhs[1:], p_mine, p_other],
                    *[i2, y10, y12, y32, y3i, yo, yi],
                ],
                [block, square, square, block, block],
                [(MEMBERS, width, modes)],
                flops=6 * unit_flops,
            )
            ro_in = send(ri, first)
        new_ri, vo = call(
            chain_columns_kernel, [y, si, ro, ro_in, ri], [block] * 2, flops=unit_flops
        )
        steps.append((y, vo))
        rhs_left, rhs_right = send(new_ri, upward), send(new_ri, downward)
        from_left, from_right = after(from_left, vo), after(from_right, vo)
        if groups - 3 - t >= middle:
            into_o = from_left + from_right
            ro_in = rhs_left + rhs_right
        else:
            into_o, into_i = from_left, from_right
            ro_in, ri_in = rhs_left, rhs_right
    inv_i, y, left = call(
        functools.partial(root_first_kernel, middle - 1),
        [flags, goi, gio, mo, mi, into_o, other_core(into_o), into_i, other_core(into_i)],
        [square] * 3,
        [room],
        20 * unit_flops,
    )
    last_y, last_vo = (send(after(part, inv_i), [(groups - 2, groups - 1)]) for part in steps[0])
    xo, xi = call(
        functools.partial(root_last_kernel, middle - 1),
        [flags, inv_i, y, left, ro, ro_in, ri, ri_in],
        [block] * 2,
        [room, block, block],
        20 * unit_flops,
    )
    for t in reversed(range(1, middle - 1)):
        y, vo = steps[t]
        from_right = send(xo, [(t + 1, t)])
        from_left = send(jnp.where(group == middle - 1, xi, xo), [(groups - 3 - t, groups - 2 - t)])
        on_left = group == t
        on_right = group == groups - 2 - t
        xi = jnp.where(on_left, from_right, jnp.where(on_right, from_left, xi))
        (outer,) = call(chain_back_kernel, [vo, y, xi], [block], flops=unit_flops)
        xo = jnp.where(on_left | on_right, outer, xo)
    outward = xi if middle - 1 == groups - 3 else xo
    in_a = send(xo, [(1, 0)])
    in_b = send(outward, [(groups - 3, groups - 2)])
    in_c = send(outward, [(groups - 3, groups - 1)])
    y, vo = steps[0]
    (out,) = call(
        final_kernel,
        [flags, w, ao, ai, y, vo, last_y, last_vo, xo, xi, in_a, in_b, in_c],
        [block],
        flops=2 * unit_flops,
    )
    return out[None]


def solution(mesh):
    groups = mesh.shape["slab"] // MEMBERS
    fine = Mesh(
        mesh.devices.reshape(groups, MEMBERS, mesh.shape["col"]), ("group", "member", "col")
    )
    slab = ("group", "member")
    placed = (
        P(slab, None, "col"),
        P(slab, None, "col"),
        P(slab, "col"),
        P(slab, None, "col"),
    )
    return jax.shard_map(
        on_device, mesh=fine, in_specs=placed, out_specs=P(slab, None, "col"), check_vma=False
    )
```

```python
import functools
import math

import jax
import jax.numpy as jnp
from jax import lax
from jax.experimental import pallas as pl
from jax.experimental.pallas import tpu as pltpu
from jax.sharding import Mesh
from jax.sharding import PartitionSpec as P

MEMBERS = 4
SPARE_BYTES = 16 * 1024 * 1024
LEAF = 128
PANEL = 16
GROUP = 8


def split(x):
    high = x.astype(jnp.bfloat16)
    low = (x - high.astype(jnp.float32)).astype(jnp.bfloat16)
    return high, low


def dot_split(a, b):
    (ah, al), (bh, bl) = a, b
    left = jnp.concatenate([ah, ah, al], axis=1)
    right = jnp.concatenate([bh, bl, bh], axis=0)
    return jnp.dot(left, right, preferred_element_type=jnp.float32)


def dot3(a, b):
    return dot_split(split(a), split(b))


def reciprocal(x):
    guess = pl.reciprocal(x, approx=True)
    return guess * (2.0 - x * guess)


def leaf_inverse(blocks, background=()):
    shape = (GROUP, LEAF)
    lane = lax.broadcasted_iota(jnp.int32, shape, 1)
    sub = lax.broadcasted_iota(jnp.int32, shape, 0)
    count = LEAF // GROUP
    sets = [[b[GROUP * i : GROUP * (i + 1), :] for i in range(count)] for b in blocks]
    background = list(background)

    def row_of(v, p):
        return jnp.broadcast_to(v[p : p + 1, :], shape)

    def col_of(v, c):
        return jnp.broadcast_to(v[:, c : c + 1], shape)

    def eliminate(k, order):
        base = GROUP * k
        vs = [rows[k] for rows in sets]
        cols = [[col_of(v, base + p) for p in range(GROUP)] for v in vs]
        inside = (lane >= base) & (lane < base + GROUP)
        unit = jnp.where(lane == sub + base, 1.0, 0.0)
        vs = [jnp.where(inside, unit, v) for v in vs]
        for p in range(GROUP):
            here = sub == p
            invs = [reciprocal(row_of(c[p], p)) for c in cols]
            for q in range(p + 1, GROUP):
                for c, inv in zip(cols, invs):
                    entry = row_of(c[q], p) * inv
                    c[q] = jnp.where(here, entry, c[q] - c[p] * entry)
            for at, (c, inv) in enumerate(zip(cols, invs)):
                scaled = row_of(vs[at], p) * inv
                vs[at] = jnp.where(here, scaled, vs[at] - c[p] * scaled)
        pivots = [[row_of(v, p) for p in range(GROUP)] for v in vs]
        for rows, v in zip(sets, vs):
            rows[k] = v
        for i in order:
            for rows, pivot in zip(sets, pivots):
                w = rows[i]
                terms = [col_of(w, base + p) * pivot[p] for p in range(GROUP)]
                while len(terms) > 1:
                    terms = [x + y for x, y in zip(terms[::2], terms[1::2])]
                rows[i] = jnp.where(inside, 0.0, w) - terms[0]

    per = PANEL // GROUP
    panels = count // per
    for j in range(panels):
        panel = list(range(per * j, per * (j + 1)))
        eager = list(range(per * (j + 1), per * (j + 2))) if j + 1 < panels else []
        others = [i for i in range(count) if i not in panel and i not in eager]
        for k in panel:
            eliminate(k, [i for i in panel if i > k] + [i for i in panel if i < k] + eager)
        inside = (lane >= PANEL * j) & (lane < PANEL * (j + 1))
        zeros = jnp.zeros(shape, jnp.float32)
        if others:
            for rows in sets:
                left = jnp.concatenate([jnp.where(inside, rows[i], 0.0) for i in others], axis=0)
                pivot = jnp.concatenate(
                    [rows[i] if i in panel else zeros for i in range(count)], axis=0
                )
                product = dot3(left, pivot)
                for at, i in enumerate(others):
                    kept = jnp.where(inside, 0.0, rows[i])
                    rows[i] = kept - product[GROUP * at : GROUP * (at + 1), :]
        share = -(-len(background) // (panels - j))
        for part in background[:share]:
            part()
        background = background[share:]
    return [jnp.concatenate(rows, axis=0) for rows in sets]


def inverse_in(work_refs, background=()):
    n = work_refs[0].shape[-1]
    steps = n // LEAF
    rest = n - LEAF

    def update(ref, src, dst, leaf):
        ls = split(leaf)
        cs = [split(ref[src, LEAF * r : LEAF * (r + 1), :LEAF]) for r in range(1, steps)]
        q = dot_split(ls, split(ref[src, :LEAF, LEAF : 2 * LEAF]))
        qs = [split(q)]
        pivot = ref[src, LEAF : 2 * LEAF, LEAF : 2 * LEAF] - dot_split(cs[0], qs[0])

        def prepare():
            wide = dot_split(ls, split(ref[src, :LEAF, 2 * LEAF :]))
            ref[dst, rest:, :LEAF] = q
            ref[dst, rest:, LEAF:rest] = wide
            ref[dst, rest:, rest:] = leaf
            ref[dst, :LEAF, :LEAF] = pivot
            whole_q = jnp.concatenate([q, wide], axis=1)
            qs[0] = split(whole_q)

        def strip(r):
            def run():
                rows = slice(LEAF * r, LEAF * (r + 1))
                out = slice(LEAF * (r - 1), LEAF * r)
                new = ref[src, rows, LEAF:] - dot_split(cs[r - 1], qs[0])
                if r == 1:
                    ref[dst, out, LEAF:rest] = new[:, LEAF:]
                else:
                    ref[dst, out, :rest] = new
                ref[dst, out, rest:] = -dot_split(cs[r - 1], ls)

            return run

        return pivot, [prepare] + [strip(r) for r in range(1, steps)]

    def body(step, leaves):
        src = lax.rem(step, 2)
        pivots, parts = [], []
        for ref, leaf in zip(work_refs, leaves):
            pivot, own = update(ref, src, 1 - src, leaf)
            pivots.append(pivot)
            parts.append(own)
        return tuple(leaf_inverse(pivots, [part for group in zip(*parts) for part in group]))

    leaves = tuple(leaf_inverse([ref[0, :LEAF, :LEAF] for ref in work_refs], background))
    leaves = lax.fori_loop(0, steps - 1, body, leaves)
    for ref, leaf in zip(work_refs, leaves):
        for part in update(ref, (steps - 1) % 2, steps % 2, leaf)[1]:
            part()


def plus_diagonal(matrix, row):
    shape = matrix.shape
    here = lax.broadcasted_iota(jnp.int32, shape, 0) == lax.broadcasted_iota(jnp.int32, shape, 1)
    return matrix + jnp.where(here, jnp.broadcast_to(row, shape), 0.0)


def dot_down(a, b):
    (ah, al), (bh, bl) = split(a), split(b)
    mul = functools.partial(
        lax.dot_general,
        dimension_numbers=(((0,), (0,)), ((), ())),
        preferred_element_type=jnp.float32,
    )
    return mul(ah, bh) + (mul(ah, bl) + mul(al, bh))


RIGHT, LAST, COL, MEMBER, SETTLED, PLANE = range(6)


def panel_kernel(pattern, coupling, mass, panel):
    width, half = coupling.shape
    tile_w = width // (width // LEAF)
    first = lax.axis_index("col") * half
    rows = lax.broadcasted_iota(jnp.int32, (LEAF, LEAF), 0)
    columns = lax.broadcasted_iota(jnp.int32, (LEAF, LEAF), 1)
    across = half // tile_w
    for r in range(width // tile_w):
        for c in range(across):
            at = (slice(tile_w * r, tile_w * (r + 1)), slice(tile_w * c, tile_w * (c + 1)))
            unit = (rows + tile_w * r == columns + (first + tile_w * c)).astype(jnp.float32)
            panel[at] = unit + pattern[across * r + c].astype(jnp.float32) * coupling[at]
    panel[width:, :] = jnp.broadcast_to(mass[...], (GROUP, half))


def place_bonds(flags, pieces, bonds):
    half = bonds.shape[-1] // 2
    me = flags[MEMBER]
    for source in range(2):
        core = flags[COL] if source == 0 else 1 - flags[COL]
        columns = pl.ds(pl.multiple_of(core * half, half), half)
        own, by_x, by_y, top, bottom = pieces[5 * source : 5 * source + 5]
        for rel, piece in enumerate((own, by_x, by_y)):
            bonds[me ^ rel, :, columns] = piece[...]
        bonds[me ^ 3, :half, columns] = top[...]
        bonds[me ^ 3, half:, columns] = bottom[...]


def first_kernel(flags, *refs):
    pieces = refs[:10]
    bonds, inverse, placed, work = refs[10:]
    width = inverse.shape[0]
    right = flags[RIGHT]
    place_bonds(flags, pieces, placed)
    for k in range(MEMBERS):
        at = jnp.where(right == 1, MEMBERS - 1 - k, k)
        bonds[k, :width, :] = placed[at, :width, :]
        at = jnp.where((right == 1) & (k > 0), MEMBERS - k, k)
        bonds[k, width:, :] = placed[at, width:, :]
    side = 2 * flags[COL]
    work[0] = plus_diagonal(
        bonds[side, :width, :] + bonds[side + 1, :width, :], bonds[side + 1, width : width + 1, :]
    )
    inverse_in([work])
    inverse[...] = work[0]


def sides(flags, mine, other):
    first = flags[COL] == 0
    a, b = mine[...], other[...]
    return jnp.where(first, a, b), jnp.where(first, b, a)


def reduce_kernel(
    flags, bonds, mine, other, i2, y10, y12, y32, y3i, yo, yi, goi, gio, mo, mi, mi_half, work_a, work_b
):
    width = i2.shape[0]

    def bond(k):
        return bonds[k, :width, :]

    def mass(k):
        return bonds[k, width : width + 1, :]

    right = flags[RIGHT]
    m1, m2, m3 = mass(1), mass(2), mass(3)
    c0, c1, c2, c3 = (split(bond(k)) for k in range(MEMBERS))
    p1, p3 = sides(flags, mine, other)
    q1, q3 = split(p1), split(p3)
    y12[...] = dot_split(c1, q1)
    y32[...] = dot_split(c2, q3)
    to_o = dot_split(split(y12[...]), c0)
    to_i = dot_split(split(y32[...]), c3)
    mass2 = plus_diagonal(y12[...] * m1 + y32[...] * m3, m2)
    work_a[0] = to_o + to_i + mass2

    def ends_i():
        y3i[...] = dot_split(c3, q3)

    def ends_o():
        y10[...] = dot_split(c0, q1)

    def from_i():
        work_b[0] = dot_split(split(y3i[...]), c2)

    def from_o():
        work_b[1] = dot_split(split(y10[...]), c1)

    inverse_in([work_a], [ends_i, ends_o, from_i, from_o])
    i2[...] = work_a[0]
    q2 = split(i2[...])
    sm = split(mass2)
    m0 = mass(0)
    left_on = jnp.where(right == 1, 0.0, 1.0)
    yi[...] = dot_split(split(work_b[0]), q2)
    si = split(yi[...])
    back = dot_split(si, split(to_o))
    gio[...] = back
    mi[...] = plus_diagonal(
        y3i[...] * m3 + dot_split(si, sm) + back * jnp.where(flags[LAST] == 1, 1.0, 0.0),
        m0 * (1.0 - left_on),
    )
    pack_half(flags, mi, mi_half)

    @pl.when(flags[LAST] == 0)
    def _():
        yo[...] = dot_split(split(work_b[1]), q2)
        so = split(yo[...])
        goi[...] = dot_split(so, split(to_i))
        mo[...] = plus_diagonal(y10[...] * m1 + dot_split(so, sm), m0 * left_on)

    @pl.when(flags[LAST] == 1)
    def _():
        yo[...] = jnp.zeros_like(yo)


def pack_half(flags, full, packed):
    half = packed.shape[1]
    middle = half + half // 2
    first = flags[COL] == 0
    packed[:half, :] = jnp.where(first, full[:half, :half], full[half:, half:])
    packed[half:, :] = jnp.where(first, full[half:middle, :half], full[middle:, :half])


def whole(flags, mine, other):
    half = mine.shape[1]
    first = flags[COL] == 0
    a, b = mine[...], other[...]
    low, high = jnp.where(first, a, b), jnp.where(first, b, a)
    corner = jnp.concatenate([low[half:], high[half:]], axis=0)
    return jnp.concatenate(
        [
            jnp.concatenate([low[:half], corner.T], axis=1),
            jnp.concatenate([corner, high[:half]], axis=1),
        ],
        axis=0,
    )


def chain_kernel(planes, flags, goi, gio, mo, mi, mine, other, new_half, si, y, work):
    @pl.when((flags[PLANE] == planes[0]) | (flags[PLANE] == planes[1]))
    def _():
        mass_o = mo[...] + whole(flags, mine, other)
        work[0] = goi[...] + mass_o
        inverse_in([work])
        si[...] = work[0]
        y[...] = dot3(gio[...], si[...])
        work[0] = mi[...] + dot3(y[...], mass_o)
        pack_half(flags, work.at[0], new_half)


def root_first_kernel(
    root, flags, goi, gio, mo, mi, o_mine, o_other, i_mine, i_other, inv_i, y, left, work
):
    @pl.when(flags[PLANE] == root)
    def _():
        mass_i = mi[...] + whole(flags, i_mine, i_other)
        work[0] = gio[...] + mass_i
        inverse_in([work])
        inv_i[...] = work[0]
        y[...] = dot3(goi[...], inv_i[...])
        mass_o = mo[...] + whole(flags, o_mine, o_other)
        left[...] = mass_o + dot3(y[...], mass_i)


def root_last_kernel(
    root, flags, inv_i, y, left, ro, ro_in, ri, ri_in, xo, xi, work, inner, outer
):
    @pl.when(flags[PLANE] == root)
    def _():
        work[0] = left[...]

        def columns():
            s = split(ri[...] + ri_in[...])
            inner[...] = dot_split(split(inv_i[...]), s)
            outer[...] = ro[...] + ro_in[...] + dot_split(split(y[...]), s)

        inverse_in([work], [columns])
        xo[...] = dot3(work[0], outer[...])
        xi[...] = inner[...] + dot_down(y[...], xo[...])


def columns_kernel(
    flags, own, by_x, by_y, by_xy, p_mine, p_other, i2, y10, y12, y32, y3i, yo, yi, w, ao, ai, ro, ri, rhs
):
    right = flags[RIGHT]
    member = flags[MEMBER]
    for rel, piece in enumerate((own, by_x, by_y, by_xy)):
        rhs[member ^ rel] = piece[...]
    r0 = rhs[0]
    r2 = rhs[2]
    r1 = rhs[jnp.where(right == 1, 3, 1)]
    r3 = rhs[jnp.where(right == 1, 1, 3)]
    s1, s3 = split(r1), split(r3)
    p1, p3 = sides(flags, p_mine, p_other)
    v1 = dot_split(split(p1), s1)
    v3 = dot_split(split(p3), s3)
    r2 = r2 + dot_split(split(y12[...]), s1) + dot_split(split(y32[...]), s3)
    s2 = split(r2)
    v2 = dot_split(split(i2[...]), s2)
    left_on = jnp.where(right == 1, 0.0, 1.0)
    yos, yis = split(yo[...]), split(yi[...])
    ro[...] = r0 * left_on + dot_split(split(y10[...]), s1) + dot_split(yos, s2)
    ri[...] = r0 * (1.0 - left_on) + dot_split(split(y3i[...]), s3) + dot_split(yis, s2)
    is_2 = member == 2
    is_1 = member == jnp.where(right == 1, 3, 1)
    z = jnp.where(is_1, y12[...], y32[...])
    zs = split(z)
    w[...] = jnp.where(is_2, v2, jnp.where(is_1, v1, v3) + dot_down(z, v2))
    ao[...] = jnp.where(is_2, yo[...], dot_split(yos, zs) + jnp.where(is_1, y10[...], 0.0))
    ai[...] = jnp.where(is_2, yi[...], dot_split(yis, zs) + jnp.where(is_1, 0.0, y3i[...]))


def chain_columns_kernel(y, si, ro, ro_in, ri, new_ri, vo):
    s = split(ro[...] + ro_in[...])
    new_ri[...] = ri[...] + dot_split(split(y[...]), s)
    vo[...] = dot_split(split(si[...]), s)


def chain_back_kernel(vo, y, xi, xo):
    xo[...] = vo[...] + dot_down(y[...], xi[...])


def final_kernel(flags, w, ao, ai, y, vo, last_y, last_vo, xo, xi, in_a, in_b, in_c, out):
    last = flags[LAST] == 1
    settled = flags[SETTLED] == 1
    came = in_a[...] + in_b[...] + in_c[...]
    end = jnp.where(last, last_vo[...], vo[...]) + dot_down(
        jnp.where(last, last_y[...], y[...]), came
    )
    end_o = jnp.where(settled, xo[...], jnp.where(last, 0.0, end))
    end_i = jnp.where(settled, xi[...], jnp.where(last, end, came))
    mine = w[...] + dot_down(ao[...], end_o) + dot_down(ai[...], end_i)
    here = jnp.where(flags[RIGHT] == 1, end_i, end_o)
    out[...] = jnp.where(flags[MEMBER] == 0, here, mine)


def call(kernel, args, outs, scratch=(), flops=0):
    def spec(a):
        space = pltpu.SMEM if a.dtype == jnp.int32 else pltpu.VMEM
        return pl.BlockSpec(memory_space=space)

    moved = sum(a.size * 4 for a in args) + sum(4 * math.prod(s) for s in outs)
    held = moved + sum(4 * math.prod(s) for s in scratch)
    return pl.pallas_call(
        kernel,
        out_shape=[jax.ShapeDtypeStruct(s, jnp.float32) for s in outs],
        in_specs=[spec(a) for a in args],
        out_specs=[pl.BlockSpec(memory_space=pltpu.VMEM) for _ in outs],
        scratch_shapes=[pltpu.VMEM(s, jnp.float32) for s in scratch],
        cost_estimate=pl.CostEstimate(flops=flops, bytes_accessed=moved, transcendentals=0),
        compiler_params=pltpu.CompilerParams(vmem_limit_bytes=held + SPARE_BYTES),
    )(*args)


def on_device(coupling, tile_pattern, orbital_mass, sources):
    width = coupling.shape[1]
    half = coupling.shape[2]
    modes = sources.shape[2]
    column = lax.axis_index("col")
    member = lax.axis_index("member")
    group = lax.axis_index("group")
    groups = lax.axis_size("group")
    middle = groups // 2

    def send(x, pairs):
        return lax.ppermute(x, "group", pairs)

    def swap(x, bits):
        return lax.ppermute(x, "member", [(m, m ^ bits) for m in range(MEMBERS)])

    def other_core(x):
        return lax.ppermute(x, "col", [(0, 1), (1, 0)])

    def after(x, *others):
        return lax.optimization_barrier((x, *others))[0]

    (own,) = call(
        panel_kernel,
        [tile_pattern[0].reshape(-1), coupling[0], orbital_mass],
        [(width + GROUP, half)],
    )
    by_x, by_y = swap(own, 1), swap(own, 2)
    top, bottom = swap(by_x[:half], 2), swap(by_y[half:], 1)
    mine = [own, by_x, by_y, top, bottom]
    pieces = mine + [other_core(piece) for piece in mine]
    settled = flags[SETTLED] == 1
    came = in_a[...] + in_b[...] + in_c[...]
    end = jnp.where(last, last_vo[...], vo[...]) + dot_down(
        jnp.where(last, last_y[...], y[...]), came
    )
    end_o = jnp.where(settled, xo[...], jnp.where(last, 0.0, end))
    end_i = jnp.where(settled, xi[...], jnp.where(last, end, came))
    mine = w[...] + dot_down(ao[...], end_o) + dot_down(ai[...], end_i)
    here = jnp.where(flags[RIGHT] == 1, end_i, end_o)
    out[...] = jnp.where(flags[MEMBER] == 0, here, mine)


def call(kernel, args, outs, scratch=(), flops=0):
    def spec(a):
        space = pltpu.SMEM if a.dtype == jnp.int32 else pltpu.VMEM
        return pl.BlockSpec(memory_space=space)

    moved = sum(a.size * 4 for a in args) + sum(4 * math.prod(s) for s in outs)
    held = moved + sum(4 * math.prod(s) for s in scratch)
    return pl.pallas_call(
        kernel,
        out_shape=[jax.ShapeDtypeStruct(s, jnp.float32) for s in outs],
        in_specs=[spec(a) for a in args],
        out_specs=[pl.BlockSpec(memory_space=pltpu.VMEM) for _ in outs],
        scratch_shapes=[pltpu.VMEM(s, jnp.float32) for s in scratch],
        cost_estimate=pl.CostEstimate(flops=flops, bytes_accessed=moved, transcendentals=0),
        compiler_params=pltpu.CompilerParams(vmem_limit_bytes=held + SPARE_BYTES),
    )(*args)


def on_device(coupling, tile_pattern, orbital_mass, sources):
    width = coupling.shape[1]
    half = coupling.shape[2]
    modes = sources.shape[2]
    column = lax.axis_index("col")
    member = lax.axis_index("member")
    group = lax.axis_index("group")
    groups = lax.axis_size("group")
    middle = groups // 2

    def send(x, pairs):
        return lax.ppermute(x, "group", pairs)

    def swap(x, bits):
        return lax.ppermute(x, "member", [(m, m ^ bits) for m in range(MEMBERS)])

    def other_core(x):
        return lax.ppermute(x, "col", [(0, 1), (1, 0)])

    def after(x, *others):
        return lax.optimization_barrier((x, *others))[0]

    (own,) = call(
        panel_kernel,
        [tile_pattern[0].reshape(-1), coupling[0], orbital_mass],
        [(width + GROUP, half)],
    )
    by_x, by_y = swap(own, 1), swap(own, 2)
    top, bottom = swap(by_x[:half], 2), swap(by_y[half:], 1)
    mine = [own, by_x, by_y, top, bottom]
    pieces = mine + [other_core(piece) for piece in mine]
    settled = (group != 0) & (group < groups - 2)
    flags = jnp.stack(
        [
            (group >= middle).astype(jnp.int32),
            (group == groups - 1).astype(jnp.int32),
            column.astype(jnp.int32),
            member.astype(jnp.int32),
            settled.astype(jnp.int32),
            group.astype(jnp.int32),
        ]
    )
    square = (width, width)
    block = (width, modes)
    packed = (half + half // 2, half)
    room = (2, width, width)
    unit_flops = 6 * width**3
    bonds, p_mine = call(
        first_kernel,
        [flags, *pieces],
        [(MEMBERS, width + GROUP, width), square],
        [(MEMBERS, width + GROUP, width), room],
        20 * unit_flops,
    )
    p_other = other_core(p_mine)
    i2, y10, y12, y32, y3i, yo, yi, goi, gio, mo, mi, mi_half = call(
        reduce_kernel,
        [flags, bonds, p_mine, p_other],
        [square] * 11 + [packed],
        [room, room],
        30 * unit_flops,
    )
    first = [(groups - 1, groups - 2)]
    into_o = send(mi_half, first)
    source = after(sources[0], mi_half)
    rhs = [source, swap(source, 1), swap(source, 2), swap(source, 3)]
    into_o, *rhs = lax.optimization_barrier((into_o, *rhs))
    steps = []
    for t in range(middle - 1):
        new_half, si, y = call(
            functools.partial(chain_kernel, (t, groups - 2 - t)),
            [flags, goi, gio, mo, mi, into_o, other_core(into_o)],
            [packed, square, square],
            [room],
            20 * unit_flops,
        )
        upward = [(t, t + 1)]
        downward = [(groups - 2 - t, groups - 3 - t)]
        from_left, from_right = send(new_half, upward), send(new_half, downward)
        if t == 0:
            w, ao, ai, ro, ri = call(
                columns_kernel,
                [
                    *[flags, after(rhs[0], new_half), *rhs[1:], p_mine, p_other],
                    *[i2, y10, y12, y32, y3i, yo, yi],
                ],
                [block, square, square, block, block],
                [(MEMBERS, width, modes)],
                flops=6 * unit_flops,
            )
            ro_in = send(ri, first)
        new_ri, vo = call(
            chain_columns_kernel, [y, si, ro, ro_in, ri], [block] * 2, flops=unit_flops
        )
        steps.append((y, vo))
        rhs_left, rhs_right = send(new_ri, upward), send(new_ri, downward)
        from_left, from_right = after(from_left, vo), after(from_right, vo)
        if groups - 3 - t >= middle:
            into_o = from_left + from_right
            ro_in = rhs_left + rhs_right
        else:
            into_o, into_i = from_left, from_right
            ro_in, ri_in = rhs_left, rhs_right
    inv_i, y, left = call(
        functools.partial(root_first_kernel, middle - 1),
        [flags, goi, gio, mo, mi, into_o, other_core(into_o), into_i, other_core(into_i)],
        [square] * 3,
        [room],
        20 * unit_flops,
    )
    last_y, last_vo = (send(after(part, inv_i), [(groups - 2, groups - 1)]) for part in steps[0])
    xo, xi = call(
        functools.partial(root_last_kernel, middle - 1),
        [flags, inv_i, y, left, ro, ro_in, ri, ri_in],
        [block] * 2,
        [room, block, block],
        20 * unit_flops,
    )
    for t in reversed(range(1, middle - 1)):
        y, vo = steps[t]
        from_right = send(xo, [(t + 1, t)])
        from_left = send(jnp.where(group == middle - 1, xi, xo), [(groups - 3 - t, groups - 2 - t)])
        on_left = group == t
        on_right = group == groups - 2 - t
        xi = jnp.where(on_left, from_right, jnp.where(on_right, from_left, xi))
        (outer,) = call(chain_back_kernel, [vo, y, xi], [block], flops=unit_flops)
        xo = jnp.where(on_left | on_right, outer, xo)
    outward = xi if middle - 1 == groups - 3 else xo
    in_a = send(xo, [(1, 0)])
    in_b = send(outward, [(groups - 3, groups - 2)])
    in_c = send(outward, [(groups - 3, groups - 1)])
    y, vo = steps[0]
    (out,) = call(
        final_kernel,
        [flags, w, ao, ai, y, vo, last_y, last_vo, xo, xi, in_a, in_b, in_c],
        [block],
        flops=2 * unit_flops,
    )
    return out[None]


def solution(mesh):
    groups = mesh.shape["slab"] // MEMBERS
    fine = Mesh(
        mesh.devices.reshape(groups, MEMBERS, mesh.shape["col"]), ("group", "member", "col")
    )
    slab = ("group", "member")
    placed = (
        P(slab, None, "col"),
        P(slab, None, "col"),
        P(slab, "col"),
        P(slab, None, "col"),
    )
    return jax.shard_map(
        on_device, mesh=fine, in_specs=placed, out_specs=P(slab, None, "col"), check_vma=False
    )
```

```python
import functools
import math

import jax
import jax.numpy as jnp
from jax import lax
from jax.experimental import pallas as pl
from jax.experimental.pallas import tpu as pltpu
from jax.sharding import Mesh
from jax.sharding import PartitionSpec as P

MEMBERS = 4
SPARE_BYTES = 16 * 1024 * 1024
LEAF = 128
PANEL = 32
GROUP = 8


def split(x):
    high = x.astype(jnp.bfloat16)
    low = (x - high.astype(jnp.float32)).astype(jnp.bfloat16)
    return high, low


def dot_split(a, b):
    (ah, al), (bh, bl) = a, b
    left = jnp.concatenate([ah, ah, al], axis=1)
    right = jnp.concatenate([bh, bl, bh], axis=0)
    return jnp.dot(left, right, preferred_element_type=jnp.float32)


def dot3(a, b):
    return dot_split(split(a), split(b))


def reciprocal(x):
    guess = pl.reciprocal(x, approx=True)
    return guess * (2.0 - x * guess)


def leaf_inverse(blocks, background=()):
    shape = (GROUP, LEAF)
    lane = lax.broadcasted_iota(jnp.int32, shape, 1)
    sub = lax.broadcasted_iota(jnp.int32, shape, 0)
    count = LEAF // GROUP
    sets = [[b[GROUP * i : GROUP * (i + 1), :] for i in range(count)] for b in blocks]
    background = list(background)

    def row_of(v, p):
        return jnp.broadcast_to(v[p : p + 1, :], shape)

    def col_of(v, c):
        return jnp.broadcast_to(v[:, c : c + 1], shape)

    def eliminate(k, order):
        base = GROUP * k
        vs = [rows[k] for rows in sets]
        cols = [[col_of(v, base + p) for p in range(GROUP)] for v in vs]
        inside = (lane >= base) & (lane < base + GROUP)
        unit = jnp.where(lane == sub + base, 1.0, 0.0)
        vs = [jnp.where(inside, unit, v) for v in vs]
        for p in range(GROUP):
            here = sub == p
            invs = [reciprocal(row_of(c[p], p)) for c in cols]
            for q in range(p + 1, GROUP):
                for c, inv in zip(cols, invs):
                    entry = row_of(c[q], p) * inv
                    c[q] = jnp.where(here, entry, c[q] - c[p] * entry)
            for at, (c, inv) in enumerate(zip(cols, invs)):
                scaled = row_of(vs[at], p) * inv
                vs[at] = jnp.where(here, scaled, vs[at] - c[p] * scaled)
        pivots = [[row_of(v, p) for p in range(GROUP)] for v in vs]
        for rows, v in zip(sets, vs):
            rows[k] = v
        for i in order:
            for rows, pivot in zip(sets, pivots):
                w = rows[i]
                terms = [col_of(w, base + p) * pivot[p] for p in range(GROUP)]
                while len(terms) > 1:
                    terms = [x + y for x, y in zip(terms[::2], terms[1::2])]
                rows[i] = jnp.where(inside, 0.0, w) - terms[0]

    per = PANEL // GROUP
    panels = count // per
    for j in range(panels):
        panel = list(range(per * j, per * (j + 1)))
        if j + 1 < panels:
            eager = list(range(per * (j + 1), per * (j + 2)))
        else:
            eager = list(range(per * j))
        others = [i for i in range(count) if i not in panel and i not in eager]
        for k in panel:
            eliminate(k, [i for i in panel if i > k] + [i for i in panel if i < k] + eager)
        inside = (lane >= PANEL * j) & (lane < PANEL * (j + 1))
        zeros = jnp.zeros(shape, jnp.float32)
        if others:
            for rows in sets:
                left = jnp.concatenate([jnp.where(inside, rows[i], 0.0) for i in others], axis=0)
                pivot = jnp.concatenate(
                    [rows[i] if i in panel else zeros for i in range(count)], axis=0
                )
                product = dot3(left, pivot)
                for at, i in enumerate(others):
                    kept = jnp.where(inside, 0.0, rows[i])
                    rows[i] = kept - product[GROUP * at : GROUP * (at + 1), :]
        share = -(-len(background) // (panels - j))
        for part in background[:share]:
            part()
        background = background[share:]
    return [jnp.concatenate(rows, axis=0) for rows in sets]


def inverse_in(work_refs, background=()):
    n = work_refs[0].shape[-1]
    steps = n // LEAF
    rest = n - LEAF

    def update(ref, src, dst, leaf):
        ls = split(leaf)
        cs = [split(ref[src, LEAF * r : LEAF * (r + 1), :LEAF]) for r in range(1, steps)]
        q = dot_split(ls, split(ref[src, :LEAF, LEAF : 2 * LEAF]))
        qs = [split(q)]
        pivot = ref[src, LEAF : 2 * LEAF, LEAF : 2 * LEAF] - dot_split(cs[0], qs[0])

        def prepare():
            wide = dot_split(ls, split(ref[src, :LEAF, 2 * LEAF :]))
            ref[dst, rest:, :LEAF] = q
            ref[dst, rest:, LEAF:rest] = wide
            ref[dst, rest:, rest:] = leaf
            ref[dst, :LEAF, :LEAF] = pivot
            whole_q = jnp.concatenate([q, wide], axis=1)
            qs[0] = split(whole_q)

        def strip(r):
            def run():
                rows = slice(LEAF * r, LEAF * (r + 1))
                out = slice(LEAF * (r - 1), LEAF * r)
                new = ref[src, rows, LEAF:] - dot_split(cs[r - 1], qs[0])
                if r == 1:
                    ref[dst, out, LEAF:rest] = new[:, LEAF:]
                else:
                    ref[dst, out, :rest] = new
                ref[dst, out, rest:] = -dot_split(cs[r - 1], ls)

            return run

        return pivot, [prepare] + [strip(r) for r in range(1, steps)]

    def body(step, leaves):
        src = lax.rem(step, 2)
        pivots, parts = [], []
        for ref, leaf in zip(work_refs, leaves):
            pivot, own = update(ref, src, 1 - src, leaf)
            pivots.append(pivot)
            parts.append(own)
        return tuple(leaf_inverse(pivots, [part for group in zip(*parts) for part in group]))

    leaves = tuple(leaf_inverse([ref[0, :LEAF, :LEAF] for ref in work_refs], background))
    leaves = lax.fori_loop(0, steps - 1, body, leaves)
    for ref, leaf in zip(work_refs, leaves):
        for part in update(ref, (steps - 1) % 2, steps % 2, leaf)[1]:
            part()


def plus_diagonal(matrix, row):
    shape = matrix.shape
    here = lax.broadcasted_iota(jnp.int32, shape, 0) == lax.broadcasted_iota(jnp.int32, shape, 1)
    return matrix + jnp.where(here, jnp.broadcast_to(row, shape), 0.0)


def dot_down(a, b):
    (ah, al), (bh, bl) = split(a), split(b)
    mul = functools.partial(
        lax.dot_general,
        dimension_numbers=(((0,), (0,)), ((), ())),
        preferred_element_type=jnp.float32,
    )
    return mul(ah, bh) + (mul(ah, bl) + mul(al, bh))


RIGHT, LAST, COL, MEMBER, SETTLED, PLANE = range(6)


def panel_kernel(pattern, coupling, mass, panel):
    half = coupling.shape[1]
    count = half // LEAF
    first = lax.axis_index("col") == 0
    rows = lax.broadcasted_iota(jnp.int32, (LEAF, LEAF), 0)
    columns = lax.broadcasted_iota(jnp.int32, (LEAF, LEAF), 1)
    unit = (rows == columns).astype(jnp.float32)

    def tile(r, c):
        on = pattern[count * r + c].astype(jnp.float32)
        return on * coupling[LEAF * r : LEAF * (r + 1), LEAF * c : LEAF * (c + 1)]

    for c in range(count):
        at = slice(LEAF * c, LEAF * (c + 1))
        for r in range(count):
            block = jnp.where(first, tile(r, c), tile(count + r, c))
            panel[LEAF * r : LEAF * (r + 1), at] = block + unit if r == c else block
        for r in range(count // 2):
            low = half + LEAF * r
            above = tile(c, count // 2 + r).T
            panel[low : low + LEAF, at] = jnp.where(first, tile(count + r, c), above)
    panel[half + half // 2 :, :] = jnp.broadcast_to(mass[...], (GROUP, half))


def place_bonds(flags, pieces, bonds):
    width = bonds.shape[-1]
    half = width // 2
    low = half // 2
    right = flags[RIGHT] == 1
    for source in range(2):
        core = flags[COL] if source == 0 else 1 - flags[COL]
        own, by_x, by_y, top, bottom = pieces[5 * source : 5 * source + 5]
        crossed = jnp.concatenate([top[...], bottom[...]], axis=0)
        same = pl.ds(pl.multiple_of(core * half, half), half)
        below = pl.ds(pl.multiple_of(half + core * low, low), low)
        for rel, piece in enumerate((own[...], by_x[...], by_y[...], crossed)):
            member = flags[MEMBER] ^ rel
            k = jnp.where(right, MEMBERS - 1 - member, member)
            corner = piece[half : half + low, :]
            bonds[k, same, same] = piece[:half, :]
            bonds[k, below, :half] = corner
            bonds[k, :half, below] = corner.T
            k = jnp.where(right & (member > 0), MEMBERS - member, member)
            bonds[k, width:, same] = piece[half + low :, :]


def first_kernel(flags, *refs):
    pieces = refs[:10]
    bonds, inverse, work = refs[10:]
    width = inverse.shape[0]
    place_bonds(flags, pieces, bonds)
    side = 2 * flags[COL]
    work[0] = plus_diagonal(
        bonds[side, :width, :] + bonds[side + 1, :width, :], bonds[side + 1, width : width + 1, :]
    )
    inverse_in([work])
    inverse[...] = work[0]


def sides(flags, mine, other):
    first = flags[COL] == 0
    a, b = mine[...], other[...]
    return jnp.where(first, a, b), jnp.where(first, b, a)


def reduce_kernel(
    flags, bonds, mine, other, i2, y10, y12, y32, y3i, yo, yi, goi, gio, mo, mi, mi_half, work_a, work_b
):
    width = i2.shape[0]

    def bond(k):
        return bonds[k, :width, :]

    def mass(k):
        return bonds[k, width : width + 1, :]

    right = flags[RIGHT]
    m1, m2, m3 = mass(1), mass(2), mass(3)
    c0, c1, c2, c3 = (split(bond(k)) for k in range(MEMBERS))
    p1, p3 = sides(flags, mine, other)
    q1, q3 = split(p1), split(p3)
    y12[...] = dot_split(c1, q1)
    y32[...] = dot_split(c2, q3)
    to_o = dot_split(split(y12[...]), c0)
    to_i = dot_split(split(y32[...]), c3)
    mass2 = plus_diagonal(y12[...] * m1 + y32[...] * m3, m2)
    work_a[0] = to_o + to_i + mass2

    def ends_i():
        y3i[...] = dot_split(c3, q3)

    def ends_o():
        y10[...] = dot_split(c0, q1)

    def from_i():
        work_b[0] = dot_split(split(y3i[...]), c2)

    def from_o():
        work_b[1] = dot_split(split(y10[...]), c1)

    inverse_in([work_a], [ends_i, ends_o, from_i, from_o])
    i2[...] = work_a[0]
    q2 = split(i2[...])
    sm = split(mass2)
    m0 = mass(0)
    left_on = jnp.where(right == 1, 0.0, 1.0)
    yi[...] = dot_split(split(work_b[0]), q2)
    si = split(yi[...])
    back = dot_split(si, split(to_o))
    gio[...] = back
    mi[...] = plus_diagonal(
        y3i[...] * m3 + dot_split(si, sm) + back * jnp.where(flags[LAST] == 1, 1.0, 0.0),
        m0 * (1.0 - left_on),
    )
    pack_half(flags, mi, mi_half)

    @pl.when(flags[LAST] == 0)
    def _():
        yo[...] = dot_split(split(work_b[1]), q2)
        so = split(yo[...])
        goi[...] = dot_split(so, split(to_i))
        mo[...] = plus_diagonal(y10[...] * m1 + dot_split(so, sm), m0 * left_on)

    @pl.when(flags[LAST] == 1)
    def _():
        yo[...] = jnp.zeros_like(yo)


def pack_half(flags, full, packed):
    half = packed.shape[1]
    middle = half + half // 2
    first = flags[COL] == 0
    packed[:half, :] = jnp.where(first, full[:half, :half], full[half:, half:])
    packed[half:, :] = jnp.where(first, full[half:middle, :half], full[middle:, :half])


def whole(flags, mine, other):
    half = mine.shape[1]
    first = flags[COL] == 0
    a, b = mine[...], other[...]
    low, high = jnp.where(first, a, b), jnp.where(first, b, a)
    corner = jnp.concatenate([low[half:], high[half:]], axis=0)
    return jnp.concatenate(
        [
            jnp.concatenate([low[:half], corner.T], axis=1),
            jnp.concatenate([corner, high[:half]], axis=1),
        ],
        axis=0,
    )


def chain_kernel(planes, flags, goi, gio, mo, mi, mine, other, new_half, si, y, work):
    @pl.when((flags[PLANE] == planes[0]) | (flags[PLANE] == planes[1]))
    def _():
        mass_o = mo[...] + whole(flags, mine, other)
        work[0] = goi[...] + mass_o
        inverse_in([work])
        si[...] = work[0]
        y[...] = dot3(gio[...], si[...])
        work[0] = mi[...] + dot3(y[...], mass_o)
        pack_half(flags, work.at[0], new_half)


def root_first_kernel(
    root, flags, goi, gio, mo, mi, o_mine, o_other, i_mine, i_other, inv_i, y, left, work
):
    @pl.when(flags[PLANE] == root)
    def _():
        mass_i = mi[...] + whole(flags, i_mine, i_other)
        work[0] = gio[...] + mass_i
        inverse_in([work])
        inv_i[...] = work[0]
        y[...] = dot3(goi[...], inv_i[...])
        mass_o = mo[...] + whole(flags, o_mine, o_other)
        left[...] = mass_o + dot3(y[...], mass_i)


def root_last_kernel(
    root, flags, inv_i, y, left, ro, ro_in, ri, ri_in, xo, xi, work, inner, outer
):
    @pl.when(flags[PLANE] == root)
    def _():
        work[0] = left[...]

        def columns():
            s = split(ri[...] + ri_in[...])
            inner[...] = dot_split(split(inv_i[...]), s)
            outer[...] = ro[...] + ro_in[...] + dot_split(split(y[...]), s)

        inverse_in([work], [columns])
        xo[...] = dot3(work[0], outer[...])
        xi[...] = inner[...] + dot_down(y[...], xo[...])


def columns_kernel(
    flags, own, by_x, by_y, by_xy, p_mine, p_other, i2, y10, y12, y32, y3i, yo, yi, w, ao, ai, ro, ri, rhs
):
    right = flags[RIGHT]
    member = flags[MEMBER]
    for rel, piece in enumerate((own, by_x, by_y, by_xy)):
        rhs[member ^ rel] = piece[...]
    r0 = rhs[0]
    r2 = rhs[2]
    r1 = rhs[jnp.where(right == 1, 3, 1)]
    r3 = rhs[jnp.where(right == 1, 1, 3)]
    s1, s3 = split(r1), split(r3)
    p1, p3 = sides(flags, p_mine, p_other)
    v1 = dot_split(split(p1), s1)
    v3 = dot_split(split(p3), s3)
    r2 = r2 + dot_split(split(y12[...]), s1) + dot_split(split(y32[...]), s3)
    s2 = split(r2)
    v2 = dot_split(split(i2[...]), s2)
    left_on = jnp.where(right == 1, 0.0, 1.0)
    yos, yis = split(yo[...]), split(yi[...])
    ro[...] = r0 * left_on + dot_split(split(y10[...]), s1) + dot_split(yos, s2)
    ri[...] = r0 * (1.0 - left_on) + dot_split(split(y3i[...]), s3) + dot_split(yis, s2)
    is_2 = member == 2
    is_1 = member == jnp.where(right == 1, 3, 1)
    z = jnp.where(is_1, y12[...], y32[...])
    zs = split(z)
    w[...] = jnp.where(is_2, v2, jnp.where(is_1, v1, v3) + dot_down(z, v2))
    ao[...] = jnp.where(is_2, yo[...], dot_split(yos, zs) + jnp.where(is_1, y10[...], 0.0))
    ai[...] = jnp.where(is_2, yi[...], dot_split(yis, zs) + jnp.where(is_1, 0.0, y3i[...]))


def chain_columns_kernel(y, si, ro, ro_in, ri, new_ri, vo):
    s = split(ro[...] + ro_in[...])
    new_ri[...] = ri[...] + dot_split(split(y[...]), s)
    vo[...] = dot_split(split(si[...]), s)


def chain_back_kernel(vo, y, xi, xo):
    xo[...] = vo[...] + dot_down(y[...], xi[...])


def final_kernel(flags, w, ao, ai, y, vo, last_y, last_vo, xo, xi, in_a, in_b, in_c, out):
    last = flags[LAST] == 1
    settled = flags[SETTLED] == 1
    came = in_a[...] + in_b[...] + in_c[...]
    end = jnp.where(last, last_vo[...], vo[...]) + dot_down(
        jnp.where(last, last_y[...], y[...]), came
    )
    end_o = jnp.where(settled, xo[...], jnp.where(last, 0.0, end))
    end_i = jnp.where(settled, xi[...], jnp.where(last, end, came))
    mine = w[...] + dot_down(ao[...], end_o) + dot_down(ai[...], end_i)
    here = jnp.where(flags[RIGHT] == 1, end_i, end_o)
    out[...] = jnp.where(flags[MEMBER] == 0, here, mine)


def call(kernel, args, outs, scratch=(), flops=0):
    def spec(a):
        space = pltpu.SMEM if a.dtype == jnp.int32 else pltpu.VMEM
        return pl.BlockSpec(memory_space=space)

    moved = sum(a.size * 4 for a in args) + sum(4 * math.prod(s) for s in outs)
    held = moved + sum(4 * math.prod(s) for s in scratch)
    return pl.pallas_call(
        kernel,
        out_shape=[jax.ShapeDtypeStruct(s, jnp.float32) for s in outs],
        in_specs=[spec(a) for a in args],
        out_specs=[pl.BlockSpec(memory_space=pltpu.VMEM) for _ in outs],
        scratch_shapes=[pltpu.VMEM(s, jnp.float32) for s in scratch],
        cost_estimate=pl.CostEstimate(flops=flops, bytes_accessed=moved, transcendentals=0),
        compiler_params=pltpu.CompilerParams(vmem_limit_bytes=held + SPARE_BYTES),
    )(*args)


def on_device(coupling, tile_pattern, orbital_mass, sources):
    width = coupling.shape[1]
    half = coupling.shape[2]
    modes = sources.shape[2]
    column = lax.axis_index("col")
    member = lax.axis_index("member")
    group = lax.axis_index("group")
    groups = lax.axis_size("group")
    middle = groups // 2

    def send(x, pairs):
        return lax.ppermute(x, "group", pairs)

    def swap(x, bits):
        return lax.ppermute(x, "member", [(m, m ^ bits) for m in range(MEMBERS)])

    def other_core(x):
        return lax.ppermute(x, "col", [(0, 1), (1, 0)])

    def after(x, *others):
        return lax.optimization_barrier((x, *others))[0]

    (own,) = call(
        panel_kernel,
        [tile_pattern[0].reshape(-1), coupling[0], orbital_mass],
        [(half + half // 2 + GROUP, half)],
    )
    by_x, by_y = swap(own, 1), swap(own, 2)
    cut = half - half // 4
    top, bottom = swap(by_x[:cut], 2), swap(by_y[cut:], 1)
    mine = [own, by_x, by_y, top, bottom]
    pieces = mine + [other_core(piece) for piece in mine]
    settled = flags[SETTLED] == 1
    came = in_a[...] + in_b[...] + in_c[...]
    end = jnp.where(last, last_vo[...], vo[...]) + dot_down(
        jnp.where(last, last_y[...], y[...]), came
    )
    end_o = jnp.where(settled, xo[...], jnp.where(last, 0.0, end))
    end_i = jnp.where(settled, xi[...], jnp.where(last, end, came))
    mine = w[...] + dot_down(ao[...], end_o) + dot_down(ai[...], end_i)
    here = jnp.where(flags[RIGHT] == 1, end_i, end_o)
    out[...] = jnp.where(flags[MEMBER] == 0, here, mine)


def call(kernel, args, outs, scratch=(), flops=0):
    def spec(a):
        space = pltpu.SMEM if a.dtype == jnp.int32 else pltpu.VMEM
        return pl.BlockSpec(memory_space=space)

    moved = sum(a.size * 4 for a in args) + sum(4 * math.prod(s) for s in outs)
    held = moved + sum(4 * math.prod(s) for s in scratch)
    return pl.pallas_call(
        kernel,
        out_shape=[jax.ShapeDtypeStruct(s, jnp.float32) for s in outs],
        in_specs=[spec(a) for a in args],
        out_specs=[pl.BlockSpec(memory_space=pltpu.VMEM) for _ in outs],
        scratch_shapes=[pltpu.VMEM(s, jnp.float32) for s in scratch],
        cost_estimate=pl.CostEstimate(flops=flops, bytes_accessed=moved, transcendentals=0),
        compiler_params=pltpu.CompilerParams(vmem_limit_bytes=held + SPARE_BYTES),
    )(*args)


def on_device(coupling, tile_pattern, orbital_mass, sources):
    width = coupling.shape[1]
    half = coupling.shape[2]
    modes = sources.shape[2]
    column = lax.axis_index("col")
    member = lax.axis_index("member")
    group = lax.axis_index("group")
    groups = lax.axis_size("group")
    middle = groups // 2

    def send(x, pairs):
        return lax.ppermute(x, "group", pairs)

    def swap(x, bits):
        return lax.ppermute(x, "member", [(m, m ^ bits) for m in range(MEMBERS)])

    def other_core(x):
        return lax.ppermute(x, "col", [(0, 1), (1, 0)])

    def after(x, *others):
        return lax.optimization_barrier((x, *others))[0]

    (own,) = call(
        panel_kernel,
        [tile_pattern[0].reshape(-1), coupling[0], orbital_mass],
        [(half + half // 2 + GROUP, half)],
    )
    by_x, by_y = swap(own, 1), swap(own, 2)
    cut = half - half // 4
    top, bottom = swap(by_x[:cut], 2), swap(by_y[cut:], 1)
    mine = [own, by_x, by_y, top, bottom]
    pieces = mine + [other_core(piece) for piece in mine]
    settled = (group != 0) & (group < groups - 2)
    flags = jnp.stack(
        [
            (group >= middle).astype(jnp.int32),
            (group == groups - 1).astype(jnp.int32),
            column.astype(jnp.int32),
            member.astype(jnp.int32),
            settled.astype(jnp.int32),
            group.astype(jnp.int32),
        ]
    )
    square = (width, width)
    block = (width, modes)
    packed = (half + half // 2, half)
    room = (2, width, width)
    unit_flops = 6 * width**3
    bonds, p_mine = call(
        first_kernel,
        [flags, *pieces],
        [(MEMBERS, width + GROUP, width), square],
        [room],
        20 * unit_flops,
    )
    p_other = other_core(p_mine)
    source = after(sources[0], p_mine)
    rhs = [source, swap(source, 1), swap(source, 2), swap(source, 3)]
    i2, y10, y12, y32, y3i, yo, yi, goi, gio, mo, mi, mi_half = call(
        reduce_kernel,
        [flags, bonds, p_mine, p_other],
        [square] * 11 + [packed],
        [room, room],
        30 * unit_flops,
    )
    first = [(groups - 1, groups - 2)]
    into_o = send(mi_half, first)
    steps = []
    for t in range(middle - 1):
        new_half, si, y = call(
            functools.partial(chain_kernel, (t, groups - 2 - t)),
            [flags, goi, gio, mo, mi, into_o, other_core(into_o)],
            [packed, square, square],
            [room],
            20 * unit_flops,
        )
        upward = [(t, t + 1)]
        downward = [(groups - 2 - t, groups - 3 - t)]
        from_left, from_right = send(new_half, upward), send(new_half, downward)
        if t == 0:
            w, ao, ai, ro, ri = call(
                columns_kernel,
                [
                    *[flags, after(rhs[0], new_half), *rhs[1:], p_mine, p_other],
                    *[i2, y10, y12, y32, y3i, yo, yi],
                ],
                [block, square, square, block, block],
                [(MEMBERS, width, modes)],
                flops=6 * unit_flops,
            )
            ro_in = send(ri, first)
        new_ri, vo = call(
            chain_columns_kernel, [y, si, ro, ro_in, ri], [block] * 2, flops=unit_flops
        )
        steps.append((y, vo))
        rhs_left, rhs_right = send(new_ri, upward), send(new_ri, downward)
        from_left, from_right = after(from_left, vo), after(from_right, vo)
        if groups - 3 - t >= middle:
            into_o = from_left + from_right
            ro_in = rhs_left + rhs_right
        else:
            into_o, into_i = from_left, from_right
            ro_in, ri_in = rhs_left, rhs_right
    inv_i, y, left = call(
        functools.partial(root_first_kernel, middle - 1),
        [flags, goi, gio, mo, mi, into_o, other_core(into_o), into_i, other_core(into_i)],
        [square] * 3,
        [room],
        20 * unit_flops,
    )
    last_y, last_vo = (send(after(part, inv_i), [(groups - 2, groups - 1)]) for part in steps[0])
    xo, xi = call(
        functools.partial(root_last_kernel, middle - 1),
        [flags, inv_i, y, left, ro, ro_in, ri, ri_in],
        [block] * 2,
        [room, block, block],
        20 * unit_flops,
    )
    for t in reversed(range(1, middle - 1)):
        y, vo = steps[t]
        from_right = send(xo, [(t + 1, t)])
        from_left = send(jnp.where(group == middle - 1, xi, xo), [(groups - 3 - t, groups - 2 - t)])
        on_left = group == t
        on_right = group == groups - 2 - t
        xi = jnp.where(on_left, from_right, jnp.where(on_right, from_left, xi))
        (outer,) = call(chain_back_kernel, [vo, y, xi], [block], flops=unit_flops)
        xo = jnp.where(on_left | on_right, outer, xo)
    outward = xi if middle - 1 == groups - 3 else xo
    in_a = send(xo, [(1, 0)])
    in_b = send(outward, [(groups - 3, groups - 2)])
    in_c = send(outward, [(groups - 3, groups - 1)])
    y, vo = steps[0]
    (out,) = call(
        final_kernel,
        [flags, w, ao, ai, y, vo, last_y, last_vo, xo, xi, in_a, in_b, in_c],
        [block],
        flops=2 * unit_flops,
    )
    return out[None]


def solution(mesh):
    groups = mesh.shape["slab"] // MEMBERS
    fine = Mesh(
        mesh.devices.reshape(groups, MEMBERS, mesh.shape["col"]), ("group", "member", "col")
    )
    slab = ("group", "member")
    placed = (
        P(slab, None, "col"),
        P(slab, None, "col"),
        P(slab, "col"),
        P(slab, None, "col"),
    )
    return jax.shard_map(
        on_device, mesh=fine, in_specs=placed, out_specs=P(slab, None, "col"), check_vma=False
    )
```

```python
import functools
import math

import jax
import jax.numpy as jnp
from jax import lax
from jax.experimental import pallas as pl
from jax.experimental.pallas import tpu as pltpu
from jax.sharding import Mesh
from jax.sharding import PartitionSpec as P

MEMBERS = 4
SPARE_BYTES = 16 * 1024 * 1024
LEAF = 128
PANEL = 32
GROUP = 8


def split(x):
    high = x.astype(jnp.bfloat16)
    low = (x - high.astype(jnp.float32)).astype(jnp.bfloat16)
    return high, low


def dot_split(a, b):
    (ah, al), (bh, bl) = a, b
    left = jnp.concatenate([ah, ah, al], axis=1)
    right = jnp.concatenate([bh, bl, bh], axis=0)
    return jnp.dot(left, right, preferred_element_type=jnp.float32)


def dot3(a, b):
    return dot_split(split(a), split(b))


def reciprocal(x):
    guess = pl.reciprocal(x, approx=True)
    return guess * (2.0 - x * guess)


def leaf_inverse(blocks, background=()):
    shape = (GROUP, LEAF)
    lane = lax.broadcasted_iota(jnp.int32, shape, 1)
    sub = lax.broadcasted_iota(jnp.int32, shape, 0)
    count = LEAF // GROUP
    sets = [[b[GROUP * i : GROUP * (i + 1), :] for i in range(count)] for b in blocks]
    background = list(background)

    def row_of(v, p):
        return jnp.broadcast_to(v[p : p + 1, :], shape)

    def col_of(v, c):
        return jnp.broadcast_to(v[:, c : c + 1], shape)

    def eliminate(k, order):
        base = GROUP * k
        vs = [rows[k] for rows in sets]
        cols = [[col_of(v, base + p) for p in range(GROUP)] for v in vs]
        inside = (lane >= base) & (lane < base + GROUP)
        unit = jnp.where(lane == sub + base, 1.0, 0.0)
        vs = [jnp.where(inside, unit, v) for v in vs]
        for p in range(GROUP):
            here = sub == p
            invs = [reciprocal(row_of(c[p], p)) for c in cols]
            for q in range(p + 1, GROUP):
                for c, inv in zip(cols, invs):
                    entry = row_of(c[q], p) * inv
                    c[q] = jnp.where(here, entry, c[q] - c[p] * entry)
            for at, (c, inv) in enumerate(zip(cols, invs)):
                scaled = row_of(vs[at], p) * inv
                vs[at] = jnp.where(here, scaled, vs[at] - c[p] * scaled)
        pivots = [[row_of(v, p) for p in range(GROUP)] for v in vs]
        for rows, v in zip(sets, vs):
            rows[k] = v
        for i in order:
            for rows, pivot in zip(sets, pivots):
                w = rows[i]
                terms = [col_of(w, base + p) * pivot[p] for p in range(GROUP)]
                while len(terms) > 1:
                    terms = [x + y for x, y in zip(terms[::2], terms[1::2])]
                rows[i] = jnp.where(inside, 0.0, w) - terms[0]

    per = PANEL // GROUP
    panels = count // per
    for j in range(panels):
        panel = list(range(per * j, per * (j + 1)))
        if j + 1 < panels:
            eager = list(range(per * (j + 1), per * (j + 2)))
        else:
            eager = list(range(per * j))
        others = [i for i in range(count) if i not in panel and i not in eager]
        for k in panel:
            eliminate(k, [i for i in panel if i > k] + [i for i in panel if i < k] + eager)
        inside = (lane >= PANEL * j) & (lane < PANEL * (j + 1))
        zeros = jnp.zeros(shape, jnp.float32)
        if others:
            for rows in sets:
                left = jnp.concatenate([jnp.where(inside, rows[i], 0.0) for i in others], axis=0)
                pivot = jnp.concatenate(
                    [rows[i] if i in panel else zeros for i in range(count)], axis=0
                )
                product = dot3(left, pivot)
                for at, i in enumerate(others):
                    kept = jnp.where(inside, 0.0, rows[i])
                    rows[i] = kept - product[GROUP * at : GROUP * (at + 1), :]
        share = -(-len(background) // (panels - j))
        for part in background[:share]:
            part()
        background = background[share:]
    return [jnp.concatenate(rows, axis=0) for rows in sets]


def inverse_in(work_refs, background=()):
    n = work_refs[0].shape[-1]
    steps = n // LEAF
    rest = n - LEAF

    def update(ref, src, dst, leaf):
        ls = split(leaf)
        cs = [split(ref[src, LEAF * r : LEAF * (r + 1), :LEAF]) for r in range(1, steps)]
        q = dot_split(ls, split(ref[src, :LEAF, LEAF : 2 * LEAF]))
        qs = [split(q)]
        pivot = ref[src, LEAF : 2 * LEAF, LEAF : 2 * LEAF] - dot_split(cs[0], qs[0])

        def prepare():
            wide = dot_split(ls, split(ref[src, :LEAF, 2 * LEAF :]))
            ref[dst, rest:, :LEAF] = q
            ref[dst, rest:, LEAF:rest] = wide
            ref[dst, rest:, rest:] = leaf
            ref[dst, :LEAF, :LEAF] = pivot
            whole_q = jnp.concatenate([q, wide], axis=1)
            qs[0] = split(whole_q)

        def strip(r):
            def run():
                rows = slice(LEAF * r, LEAF * (r + 1))
                out = slice(LEAF * (r - 1), LEAF * r)
                new = ref[src, rows, LEAF:] - dot_split(cs[r - 1], qs[0])
                if r == 1:
                    ref[dst, out, LEAF:rest] = new[:, LEAF:]
                else:
                    ref[dst, out, :rest] = new
                ref[dst, out, rest:] = -dot_split(cs[r - 1], ls)

            return run

        return pivot, [prepare] + [strip(r) for r in range(1, steps)]

    def body(step, leaves):
        src = lax.rem(step, 2)
        pivots, parts = [], []
        for ref, leaf in zip(work_refs, leaves):
            pivot, own = update(ref, src, 1 - src, leaf)
            pivots.append(pivot)
            parts.append(own)
        return tuple(leaf_inverse(pivots, [part for group in zip(*parts) for part in group]))

    leaves = tuple(leaf_inverse([ref[0, :LEAF, :LEAF] for ref in work_refs], background))
    leaves = lax.fori_loop(0, steps - 1, body, leaves)
    for ref, leaf in zip(work_refs, leaves):
        for part in update(ref, (steps - 1) % 2, steps % 2, leaf)[1]:
            part()


def plus_diagonal(matrix, row):
    shape = matrix.shape
    here = lax.broadcasted_iota(jnp.int32, shape, 0) == lax.broadcasted_iota(jnp.int32, shape, 1)
    return matrix + jnp.where(here, jnp.broadcast_to(row, shape), 0.0)


def dot_down(a, b):
    (ah, al), (bh, bl) = split(a), split(b)
    mul = functools.partial(
        lax.dot_general,
        dimension_numbers=(((0,), (0,)), ((), ())),
        preferred_element_type=jnp.float32,
    )
    return mul(ah, bh) + (mul(ah, bl) + mul(al, bh))


RIGHT, LAST, COL, MEMBER, SETTLED, PLANE = range(6)


def panel_kernel(pattern, coupling, mass, panel):
    half = coupling.shape[1]
    count = half // LEAF
    first = lax.axis_index("col") == 0
    rows = lax.broadcasted_iota(jnp.int32, (LEAF, LEAF), 0)
    columns = lax.broadcasted_iota(jnp.int32, (LEAF, LEAF), 1)
    unit = (rows == columns).astype(jnp.float32)

    def tile(r, c):
        on = pattern[count * r + c].astype(jnp.float32)
        return on * coupling[LEAF * r : LEAF * (r + 1), LEAF * c : LEAF * (c + 1)]

    for c in range(count):
        at = slice(LEAF * c, LEAF * (c + 1))
        for r in range(count):
            block = jnp.where(first, tile(r, c), tile(count + r, c))
            panel[LEAF * r : LEAF * (r + 1), at] = block + unit if r == c else block
        for r in range(count // 2):
            low = half + LEAF * r
            above = tile(c, count // 2 + r).T
            panel[low : low + LEAF, at] = jnp.where(first, tile(count + r, c), above)
    panel[half + half // 2 :, :] = jnp.broadcast_to(mass[...], (GROUP, half))


def place_bonds(flags, pieces, bonds):
    width = bonds.shape[-1]
    half = width // 2
    low = half // 2
    right = flags[RIGHT] == 1
    for source in range(2):
        core = flags[COL] if source == 0 else 1 - flags[COL]
        own, by_x, by_y, top, bottom = pieces[5 * source : 5 * source + 5]
        crossed = jnp.concatenate([top[...], bottom[...]], axis=0)
        same = pl.ds(pl.multiple_of(core * half, half), half)
        below = pl.ds(pl.multiple_of(half + core * low, low), low)
        for rel, piece in enumerate((own[...], by_x[...], by_y[...], crossed)):
            member = flags[MEMBER] ^ rel
            k = jnp.where(right, MEMBERS - 1 - member, member)
            corner = piece[half : half + low, :]
            bonds[k, same, same] = piece[:half, :]
            bonds[k, below, :half] = corner
            bonds[k, :half, below] = corner.T
            k = jnp.where(right & (member > 0), MEMBERS - member, member)
            bonds[k, width:, same] = piece[half + low :, :]


def first_kernel(flags, *refs):
    pieces = refs[:10]
    bonds, inverse, work = refs[10:]
    width = inverse.shape[0]
    place_bonds(flags, pieces, bonds)
    side = 2 * flags[COL]
    work[0] = plus_diagonal(
        bonds[side, :width, :] + bonds[side + 1, :width, :], bonds[side + 1, width : width + 1, :]
    )
    inverse_in([work])
    inverse[...] = work[0]


def sides(flags, mine, other):
    first = flags[COL] == 0
    a, b = mine[...], other[...]
    return jnp.where(first, a, b), jnp.where(first, b, a)


def reduce_kernel(
    flags, bonds, mine, other, i2, y10, y12, y32, y3i, yo, yi, goi, gio, mo, mi, mi_half, work_a, work_b
):
    width = i2.shape[0]

    def bond(k):
        return bonds[k, :width, :]

    def mass(k):
        return bonds[k, width : width + 1, :]

    right = flags[RIGHT]
    m1, m2, m3 = mass(1), mass(2), mass(3)
    c0, c1, c2, c3 = (split(bond(k)) for k in range(MEMBERS))
    p1, p3 = sides(flags, mine, other)
    q1, q3 = split(p1), split(p3)
    y12[...] = dot_split(c1, q1)
    y32[...] = dot_split(c2, q3)
    to_o = dot_split(split(y12[...]), c0)
    to_i = dot_split(split(y32[...]), c3)
    mass2 = plus_diagonal(y12[...] * m1 + y32[...] * m3, m2)
    work_a[0] = to_o + to_i + mass2

    def ends_i():
        y3i[...] = dot_split(c3, q3)

    def ends_o():
        y10[...] = dot_split(c0, q1)

    def from_i():
        work_b[0] = dot_split(split(y3i[...]), c2)

    def from_o():
        work_b[1] = dot_split(split(y10[...]), c1)

    inverse_in([work_a], [ends_i, ends_o, from_i, from_o])
    i2[...] = work_a[0]
    q2 = split(i2[...])
    sm = split(mass2)
    m0 = mass(0)
    left_on = jnp.where(right == 1, 0.0, 1.0)
    yi[...] = dot_split(split(work_b[0]), q2)
    si = split(yi[...])
    back = dot_split(si, split(to_o))
    gio[...] = back
    mi[...] = plus_diagonal(
        y3i[...] * m3 + dot_split(si, sm) + back * jnp.where(flags[LAST] == 1, 1.0, 0.0),
        m0 * (1.0 - left_on),
    )
    pack_half(flags, mi, mi_half)

    @pl.when(flags[LAST] == 0)
    def _():
        yo[...] = dot_split(split(work_b[1]), q2)
        so = split(yo[...])
        goi[...] = dot_split(so, split(to_i))
        mo[...] = plus_diagonal(y10[...] * m1 + dot_split(so, sm), m0 * left_on)

    @pl.when(flags[LAST] == 1)
    def _():
        yo[...] = jnp.zeros_like(yo)


def pack_half(flags, full, packed):
    half = packed.shape[1]
    middle = half + half // 2
    first = flags[COL] == 0
    packed[:half, :] = jnp.where(first, full[:half, :half], full[half:, half:])
    packed[half:, :] = jnp.where(first, full[half:middle, :half], full[middle:, :half])


def whole(flags, mine, other):
    half = mine.shape[1]
    first = flags[COL] == 0
    a, b = mine[...], other[...]
    low, high = jnp.where(first, a, b), jnp.where(first, b, a)
    corner = jnp.concatenate([low[half:], high[half:]], axis=0)
    return jnp.concatenate(
        [
            jnp.concatenate([low[:half], corner.T], axis=1),
            jnp.concatenate([corner, high[:half]], axis=1),
        ],
        axis=0,
    )


def chain_kernel(planes, flags, goi, gio, mo, mi, mine, other, new_half, si, y, work):
    @pl.when((flags[PLANE] == planes[0]) | (flags[PLANE] == planes[1]))
    def _():
        mass_o = mo[...] + whole(flags, mine, other)
        work[0] = goi[...] + mass_o
        inverse_in([work])
        si[...] = work[0]
        y[...] = dot3(gio[...], si[...])
        work[0] = mi[...] + dot3(y[...], mass_o)
        pack_half(flags, work.at[0], new_half)


def root_first_kernel(
    root, flags, goi, gio, mo, mi, o_mine, o_other, i_mine, i_other, inv_i, y, left, work
):
    @pl.when(flags[PLANE] == root)
    def _():
        mass_i = mi[...] + whole(flags, i_mine, i_other)
        work[0] = gio[...] + mass_i
        inverse_in([work])
        inv_i[...] = work[0]
        y[...] = dot3(goi[...], inv_i[...])
        mass_o = mo[...] + whole(flags, o_mine, o_other)
        left[...] = mass_o + dot3(y[...], mass_i)


def root_last_kernel(
    root, flags, inv_i, y, left, ro, ro_in, ri, ri_in, xo, xi, work, inner, outer
):
    @pl.when(flags[PLANE] == root)
    def _():
        work[0] = left[...]

        def columns():
            s = split(ri[...] + ri_in[...])
            inner[...] = dot_split(split(inv_i[...]), s)
            outer[...] = ro[...] + ro_in[...] + dot_split(split(y[...]), s)

        inverse_in([work], [columns])
        xo[...] = dot3(work[0], outer[...])
        xi[...] = inner[...] + dot_down(y[...], xo[...])


def columns_kernel(
    flags, own, by_x, by_y, by_xy, p_mine, p_other, i2, y10, y12, y32, y3i, yo, yi, w, ao, ai, ro, ri, rhs
):
    right = flags[RIGHT]
    member = flags[MEMBER]
    for rel, piece in enumerate((own, by_x, by_y, by_xy)):
        rhs[member ^ rel] = piece[...]
    r0 = rhs[0]
    r2 = rhs[2]
    r1 = rhs[jnp.where(right == 1, 3, 1)]
    r3 = rhs[jnp.where(right == 1, 1, 3)]
    s1, s3 = split(r1), split(r3)
    p1, p3 = sides(flags, p_mine, p_other)
    v1 = dot_split(split(p1), s1)
    v3 = dot_split(split(p3), s3)
    r2 = r2 + dot_split(split(y12[...]), s1) + dot_split(split(y32[...]), s3)
    s2 = split(r2)
    v2 = dot_split(split(i2[...]), s2)
    left_on = jnp.where(right == 1, 0.0, 1.0)
    yos, yis = split(yo[...]), split(yi[...])
    ro[...] = r0 * left_on + dot_split(split(y10[...]), s1) + dot_split(yos, s2)
    ri[...] = r0 * (1.0 - left_on) + dot_split(split(y3i[...]), s3) + dot_split(yis, s2)
    is_2 = member == 2
    is_1 = member == jnp.where(right == 1, 3, 1)
    z = jnp.where(is_1, y12[...], y32[...])
    zs = split(z)
    w[...] = jnp.where(is_2, v2, jnp.where(is_1, v1, v3) + dot_down(z, v2))
    ao[...] = jnp.where(is_2, yo[...], dot_split(yos, zs) + jnp.where(is_1, y10[...], 0.0))
    ai[...] = jnp.where(is_2, yi[...], dot_split(yis, zs) + jnp.where(is_1, 0.0, y3i[...]))


def chain_columns_kernel(y, si, ro, ro_in, ri, new_ri, vo):
    s = split(ro[...] + ro_in[...])
    new_ri[...] = ri[...] + dot_split(split(y[...]), s)
    vo[...] = dot_split(split(si[...]), s)


def chain_back_kernel(vo, y, xi, xo):
    xo[...] = vo[...] + dot_down(y[...], xi[...])


def final_kernel(flags, w, ao, ai, y, vo, last_y, last_vo, xo, xi, in_a, in_b, in_c, out):
    last = flags[LAST] == 1
    settled = flags[SETTLED] == 1
    came = in_a[...] + in_b[...] + in_c[...]
    end = jnp.where(last, last_vo[...], vo[...]) + dot_down(
        jnp.where(last, last_y[...], y[...]), came
    )
    end_o = jnp.where(settled, xo[...], jnp.where(last, 0.0, end))
    end_i = jnp.where(settled, xi[...], jnp.where(last, end, came))
    mine = w[...] + dot_down(ao[...], end_o) + dot_down(ai[...], end_i)
    here = jnp.where(flags[RIGHT] == 1, end_i, end_o)
    out[...] = jnp.where(flags[MEMBER] == 0, here, mine)


def call(kernel, args, outs, scratch=(), flops=0):
    def spec(a):
        space = pltpu.SMEM if a.dtype == jnp.int32 else pltpu.VMEM
        return pl.BlockSpec(memory_space=space)

    moved = sum(a.size * 4 for a in args) + sum(4 * math.prod(s) for s in outs)
    held = moved + sum(4 * math.prod(s) for s in scratch)
    return pl.pallas_call(
        kernel,
        out_shape=[jax.ShapeDtypeStruct(s, jnp.float32) for s in outs],
        in_specs=[spec(a) for a in args],
        out_specs=[pl.BlockSpec(memory_space=pltpu.VMEM) for _ in outs],
        scratch_shapes=[pltpu.VMEM(s, jnp.float32) for s in scratch],
        cost_estimate=pl.CostEstimate(flops=flops, bytes_accessed=moved, transcendentals=0),
        compiler_params=pltpu.CompilerParams(vmem_limit_bytes=held + SPARE_BYTES),
    )(*args)


def on_device(coupling, tile_pattern, orbital_mass, sources):
    width = coupling.shape[1]
    half = coupling.shape[2]
    modes = sources.shape[2]
    column = lax.axis_index("col")
    member = lax.axis_index("member")
    group = lax.axis_index("group")
    groups = lax.axis_size("group")
    middle = groups // 2

    def send(x, pairs):
        return lax.ppermute(x, "group", pairs)

    def swap(x, bits):
        return lax.ppermute(x, "member", [(m, m ^ bits) for m in range(MEMBERS)])

    def other_core(x):
        return lax.ppermute(x, "col", [(0, 1), (1, 0)])

    def after(x, *others):
        return lax.optimization_barrier((x, *others))[0]

    (own,) = call(
        panel_kernel,
        [tile_pattern[0].reshape(-1), coupling[0], orbital_mass],
        [(half + half // 2 + GROUP, half)],
    )
    by_x, by_y = swap(own, 1), swap(own, 2)
    cut = half - half // 4
    top, bottom = swap(by_x[:cut], 2), swap(by_y[cut:], 1)
    mine = [own, by_x, by_y, top, bottom]
    pieces = mine + [other_core(piece) for piece in mine]
    settled = flags[SETTLED] == 1
    came = in_a[...] + in_b[...] + in_c[...]
    end = jnp.where(last, last_vo[...], vo[...]) + dot_down(
        jnp.where(last, last_y[...], y[...]), came
    )
    end_o = jnp.where(settled, xo[...], jnp.where(last, 0.0, end))
    end_i = jnp.where(settled, xi[...], jnp.where(last, end, came))
    mine = w[...] + dot_down(ao[...], end_o) + dot_down(ai[...], end_i)
    here = jnp.where(flags[RIGHT] == 1, end_i, end_o)
    out[...] = jnp.where(flags[MEMBER] == 0, here, mine)


def call(kernel, args, outs, scratch=(), flops=0):
    def spec(a):
        space = pltpu.SMEM if a.dtype == jnp.int32 else pltpu.VMEM
        return pl.BlockSpec(memory_space=space)

    moved = sum(a.size * 4 for a in args) + sum(4 * math.prod(s) for s in outs)
    held = moved + sum(4 * math.prod(s) for s in scratch)
    return pl.pallas_call(
        kernel,
        out_shape=[jax.ShapeDtypeStruct(s, jnp.float32) for s in outs],
        in_specs=[spec(a) for a in args],
        out_specs=[pl.BlockSpec(memory_space=pltpu.VMEM) for _ in outs],
        scratch_shapes=[pltpu.VMEM(s, jnp.float32) for s in scratch],
        cost_estimate=pl.CostEstimate(flops=flops, bytes_accessed=moved, transcendentals=0),
        compiler_params=pltpu.CompilerParams(vmem_limit_bytes=held + SPARE_BYTES),
    )(*args)


def on_device(coupling, tile_pattern, orbital_mass, sources):
    width = coupling.shape[1]
    half = coupling.shape[2]
    modes = sources.shape[2]
    column = lax.axis_index("col")
    member = lax.axis_index("member")
    group = lax.axis_index("group")
    groups = lax.axis_size("group")
    middle = groups // 2

    def send(x, pairs):
        return lax.ppermute(x, "group", pairs)

    def swap(x, bits):
        return lax.ppermute(x, "member", [(m, m ^ bits) for m in range(MEMBERS)])

    def other_core(x):
        return lax.ppermute(x, "col", [(0, 1), (1, 0)])

    def after(x, *others):
        return lax.optimization_barrier((x, *others))[0]

    (own,) = call(
        panel_kernel,
        [tile_pattern[0].reshape(-1), coupling[0], orbital_mass],
        [(half + half // 2 + GROUP, half)],
    )
    by_x, by_y = swap(own, 1), swap(own, 2)
    cut = half - half // 4
    top, bottom = swap(by_x[:cut], 2), swap(by_y[cut:], 1)
    mine = [own, by_x, by_y, top, bottom]
    pieces = mine + [other_core(piece) for piece in mine]
    settled = (group != 0) & (group < groups - 2)
    flags = jnp.stack(
        [
            (group >= middle).astype(jnp.int32),
            (group == groups - 1).astype(jnp.int32),
            column.astype(jnp.int32),
            member.astype(jnp.int32),
            settled.astype(jnp.int32),
            group.astype(jnp.int32),
        ]
    )
    square = (width, width)
    block = (width, modes)
    packed = (half + half // 2, half)
    room = (2, width, width)
    unit_flops = 6 * width**3
    bonds, p_mine = call(
        first_kernel,
        [flags, *pieces],
        [(MEMBERS, width + GROUP, width), square],
        [room],
        20 * unit_flops,
    )
    p_other = other_core(p_mine)
    source = after(sources[0], p_mine)
    rhs = [source, swap(source, 1), swap(source, 2), swap(source, 3)]
    i2, y10, y12, y32, y3i, yo, yi, goi, gio, mo, mi, mi_half = call(
        reduce_kernel,
        [flags, bonds, p_mine, p_other],
        [square] * 11 + [packed],
        [room, room],
        30 * unit_flops,
    )
    first = [(groups - 1, groups - 2)]
    mi_half, *rhs = lax.optimization_barrier((mi_half, *rhs))
    into_o = send(mi_half, first)
    steps = []
    for t in range(middle - 1):
        new_half, si, y = call(
            functools.partial(chain_kernel, (t, groups - 2 - t)),
            [flags, goi, gio, mo, mi, into_o, other_core(into_o)],
            [packed, square, square],
            [room],
            20 * unit_flops,
        )
        upward = [(t, t + 1)]
        downward = [(groups - 2 - t, groups - 3 - t)]
        from_left, from_right = send(new_half, upward), send(new_half, downward)
        if t == 0:
            w, ao, ai, ro, ri = call(
                columns_kernel,
                [
                    *[flags, after(rhs[0], new_half), *rhs[1:], p_mine, p_other],
                    *[i2, y10, y12, y32, y3i, yo, yi],
                ],
                [block, square, square, block, block],
                [(MEMBERS, width, modes)],
                flops=6 * unit_flops,
            )
            ro_in = send(ri, first)
        new_ri, vo = call(
            chain_columns_kernel, [y, si, ro, ro_in, ri], [block] * 2, flops=unit_flops
        )
        steps.append((y, vo))
        rhs_left, rhs_right = send(new_ri, upward), send(new_ri, downward)
        from_left, from_right = after(from_left, vo), after(from_right, vo)
        if groups - 3 - t >= middle:
            into_o = from_left + from_right
            ro_in = rhs_left + rhs_right
        else:
            into_o, into_i = from_left, from_right
            ro_in, ri_in = rhs_left, rhs_right
    inv_i, y, left = call(
        functools.partial(root_first_kernel, middle - 1),
        [flags, goi, gio, mo, mi, into_o, other_core(into_o), into_i, other_core(into_i)],
        [square] * 3,
        [room],
        20 * unit_flops,
    )
    last_y, last_vo = (send(after(part, inv_i), [(groups - 2, groups - 1)]) for part in steps[0])
    xo, xi = call(
        functools.partial(root_last_kernel, middle - 1),
        [flags, inv_i, y, left, ro, ro_in, ri, ri_in],
        [block] * 2,
        [room, block, block],
        20 * unit_flops,
    )
    for t in reversed(range(1, middle - 1)):
        y, vo = steps[t]
        from_right = send(xo, [(t + 1, t)])
        from_left = send(jnp.where(group == middle - 1, xi, xo), [(groups - 3 - t, groups - 2 - t)])
        on_left = group == t
        on_right = group == groups - 2 - t
        xi = jnp.where(on_left, from_right, jnp.where(on_right, from_left, xi))
        (outer,) = call(chain_back_kernel, [vo, y, xi], [block], flops=unit_flops)
        xo = jnp.where(on_left | on_right, outer, xo)
    outward = xi if middle - 1 == groups - 3 else xo
    in_a = send(xo, [(1, 0)])
    in_b = send(outward, [(groups - 3, groups - 2)])
    in_c = send(outward, [(groups - 3, groups - 1)])
    y, vo = steps[0]
    (out,) = call(
        final_kernel,
        [flags, w, ao, ai, y, vo, last_y, last_vo, xo, xi, in_a, in_b, in_c],
        [block],
        flops=2 * unit_flops,
    )
    return out[None]


def solution(mesh):
    groups = mesh.shape["slab"] // MEMBERS
    fine = Mesh(
        mesh.devices.reshape(groups, MEMBERS, mesh.shape["col"]), ("group", "member", "col")
    )
    slab = ("group", "member")
    placed = (
        P(slab, None, "col"),
        P(slab, None, "col"),
        P(slab, "col"),
        P(slab, None, "col"),
    )
    return jax.shard_map(
        on_device, mesh=fine, in_specs=placed, out_specs=P(slab, None, "col"), check_vma=False
    )
```
